128 devices in a mesh: dom: 64 (over z_lo, x, y, core), head: 2 (over z_hi).
Axes of the slice: x: 4, y: 4, z: 4 (z_hi: 2, z_lo: 2; z = z_hi * 2 + z_lo), core: 2. Of those that a mesh axis runs over, the one named last changes fastest.
Arguments:
- node_feats: bfloat16 [131072, 512], P(('dom', 'head')), may hold values from -16 to 16
- w_qkv: bfloat16 [512, 1536], replicated, may hold values from -1 to 1
- w_out: bfloat16 [512, 512], replicated, may hold values from -2 to 2
- neighbours: int32 [1024, 4], P('dom'), may hold values from 0 to 15
- tiles: int32 [1024, 4, 128, 128], P('dom'), may hold values 0 or 1
- partner: int32 [1024], P('dom'), may hold values from 0 to 1023, as said below
- layer_cot: bfloat16 [131072, 512], P(('dom', 'head')), may hold values from -6 to 6
Outputs:
- layer_out: bfloat16 [131072, 512], P(('dom', 'head'))
- feat_grad: bfloat16 [131072, 512], P(('dom', 'head'))
- dw_qkv: float32 [512, 1536], P('dom', 'head')
- dw_out: float32 [512, 512], P('head', 'dom')
The draws below stay inside these ranges and needn't reach their ends.
Inputs may be any that keep to these rules, and one draw needn't show every extreme that they name: partner is a perfect matching of the 1024 node blocks: partner[partner[b]] = b, and the partner of a block lies in another part (part = block // 16). For every two parts, at most 1 block of one are matched to blocks of the other, and some two parts have exactly 1 such pairs.
All inputs are finite; a program needn't handle non-finite values. No bound on the sum of `tiles` on one device may be relied on, other than what follows from the above.
Results may differ from the reference program's by a relative error of at most 0.019.
The reference program's roundings to bfloat16 on the way count: a program that leaves them out, or rounds other values in their place, can miss the bound.
Values may be sent and summed in bfloat16 or wider, within the bound.
No kernel may reach another device: no remote copies, remote signals or barrier semaphores. Data moves between devices by JAX's collectives and lax.ppermute only.
A program may use at most 192 MiB of HBM per device.

```python
import jax
import jax.numpy as jnp
from jax import lax

D = 512
H = 8
BS = 128
NBR = 4
GB = 4
BLK = 16
HG = 4
NB = 1024
NODES = 131072
N_DOM = 64
N_HEAD = 2


def draw_partner(key, part):
    count = N_DOM
    key_labels, key_rounds, key_slots = jax.random.split(jax.random.fold_in(key, 7), 3)
    labels = jax.random.permutation(key_labels, count).astype(jnp.int32)
    inverse = jnp.zeros((count,), jnp.int32).at[labels].set(jnp.arange(count, dtype=jnp.int32))
    rounds = jax.random.permutation(key_rounds, count - 1).astype(jnp.int32)
    chosen = rounds[jnp.arange(BLK, dtype=jnp.int32) % (count - 1)]
    label_col = labels[:, None]
    round_row = chosen[None, :]
    other = jnp.where(label_col == count - 1, round_row, jnp.where(label_col == round_row, count - 1, (2 * round_row - label_col) % (count - 1)))
    partner_part = inverse[other]
    slot_keys = jax.random.split(key_slots, count)
    slot_table = jax.vmap(lambda single: jax.random.permutation(single, BLK))(slot_keys).astype(jnp.int32)
    columns = jnp.broadcast_to(jnp.arange(BLK, dtype=jnp.int32)[None, :], (count, BLK))
    partner_slot = slot_table[partner_part, columns]
    matched = partner_part * BLK + partner_slot
    row_ids = jnp.broadcast_to(jnp.arange(count, dtype=jnp.int32)[:, None], (count, BLK))
    result = jnp.zeros((count, BLK), jnp.int32).at[row_ids, slot_table].set(matched)
    return result.reshape(count * BLK)


def draw_node_feats(key, part):
    base = jax.random.fold_in(key, 11)
    key_noise = jax.random.fold_in(base, 0)
    result = jnp.clip(jax.random.normal(key_noise, (NODES, D), jnp.float32), -6.0, 6.0)
    return result.astype(jnp.bfloat16)


def draw_w_qkv(key, part):
    base = jax.random.fold_in(key, 13)
    raw = jnp.clip(jax.random.normal(base, (D, N_HEAD, 3, D // N_HEAD), jnp.float32), -4.0, 4.0) * D ** (-0.5)
    return raw.reshape(D, 3 * D).astype(jnp.bfloat16)


def set_ends(drawn, rng, smallest, high):
    place = [jax.random.randint(jax.random.fold_in(rng, axis), (), 0, length) for axis, length in enumerate(drawn.shape)]
    widest = drawn.shape.index(max(drawn.shape))
    neighbour = place[:widest] + [(place[widest] + 1) % drawn.shape[widest]] + place[widest + 1:]
    return drawn.at[tuple(place)].set(smallest).at[tuple(neighbour)].set(high)


def block_levels(stream_key, extent, pieces, low, high):
    factor_of, own = 1.0, jax.random.fold_in(stream_key, 6)
    for dim, shards_of in pieces:
        heights = jnp.exp(jax.random.uniform(jax.random.fold_in(own, dim), (shards_of,), jnp.float32, low / len(pieces), high / len(pieces)))
        factor_of = factor_of * jnp.repeat(heights, extent[dim] // shards_of).reshape([-1 if axis == dim else 1 for axis in range(len(extent))])
    return factor_of


def normal_values(rng, shape, spread, most, cuts=(), held_as=jnp.bfloat16):
    drawn = jax.random.normal(rng, shape, jnp.float32) * spread
    if len(cuts) > 0:
        drawn = block_levels(rng, shape, cuts, -0.22, 0.18) * drawn
    return jnp.clip(drawn, min=-most, max=most).astype(held_as)


def setup_inputs(seed: int = 0) -> dict:
    arg_keys = jax.random.split(jax.random.key(seed), 8)
    return {
        "node_feats": draw_node_feats(jax.random.fold_in(arg_keys[7], 71), 0),
        "w_qkv": draw_w_qkv(jax.random.fold_in(arg_keys[7], 71), 0),
        "w_out": normal_values(arg_keys[2], (D, D), (max(D // 64, 1)) ** -0.5, 2.0),
        "neighbours": set_ends(jax.random.randint(arg_keys[3], (NB, NBR), 0, BLK), jax.random.fold_in(arg_keys[3], 1), 0, BLK - 1).astype(jnp.int32),
        "tiles": set_ends((jax.random.randint(arg_keys[4], (NB, NBR, BS, BS), 0, 2) < 1).astype(jnp.int32), jax.random.fold_in(arg_keys[4], 1), 0, 1),
        "partner": draw_partner(jax.random.fold_in(arg_keys[7], 71), 0),
        "layer_cot": normal_values(arg_keys[6], (NODES, D), 1.0, 6.0, ((0, 128),)),
    }


def reference(node_feats, w_qkv, w_out, neighbours, tiles, partner, layer_cot):
    head_dim = D // H
    scale = head_dim ** -0.5
    qkv = jnp.dot(node_feats, w_qkv, preferred_element_type=jnp.float32).astype(jnp.bfloat16)
    split = qkv.reshape(NB, BS, N_HEAD, 3, HG * head_dim)
    queries = split[:, :, :, 0].reshape(NB, BS, H, head_dim)
    keys = split[:, :, :, 1].reshape(NB, BS, H, head_dim)
    values = split[:, :, :, 2].reshape(NB, BS, H, head_dim)
    cot_attn = jnp.dot(layer_cot, w_out.T, preferred_element_type=jnp.float32).astype(jnp.bfloat16)
    cot_attn = cot_attn.reshape(NB, BS, H, head_dim)
    block_base = (jnp.arange(NB, dtype=jnp.int32) // BLK) * BLK
    key_ids = jnp.concatenate([block_base[:, None] + neighbours, partner[:, None]], axis=1).astype(jnp.int32)

    def attend(carry, start):
        key_grads, value_grads = carry
        ids = lax.dynamic_slice_in_dim(key_ids, start, GB, 0)
        query_block = lax.dynamic_slice_in_dim(queries, start, GB, 0).astype(jnp.float32)
        key_block = keys[ids].reshape(GB, (NBR + 1) * BS, H, head_dim).astype(jnp.float32)
        value_block = values[ids].reshape(GB, (NBR + 1) * BS, H, head_dim).astype(jnp.float32)
        tile_block = lax.dynamic_slice_in_dim(tiles, start, GB, 0)
        visible = jnp.concatenate([tile_block.transpose(0, 2, 1, 3).reshape(GB, BS, NBR * BS) != 0,
                                   jnp.ones((GB, BS, BS), dtype=jnp.bool_)], axis=2)
        scores = jnp.einsum('bqhd,bkhd->bhqk', query_block, key_block) * scale
        scores = jnp.where(visible[:, None], scores, -1e30)
        peak = jnp.max(scores, axis=-1, keepdims=True)
        total = jnp.sum(jnp.exp(scores - peak), axis=-1, keepdims=True)
        probs = jnp.exp(scores - peak) / total
        probs_low = probs.astype(jnp.bfloat16).astype(jnp.float32)
        attended = jnp.einsum('bhqk,bkhd->bqhd', probs_low, value_block).astype(jnp.bfloat16)
        grad_block = lax.dynamic_slice_in_dim(cot_attn, start, GB, 0).astype(jnp.float32)
        delta = jnp.sum(grad_block * attended.astype(jnp.float32), axis=-1).transpose(0, 2, 1)
        grad_values = jnp.einsum('bhqk,bqhd->bkhd', probs_low, grad_block)
        grad_probs = jnp.einsum('bqhd,bkhd->bhqk', grad_block, value_block)
        grad_scores = (probs * (grad_probs - delta[..., None]) * scale).astype(jnp.bfloat16).astype(jnp.float32)
        grad_query = jnp.einsum('bhqk,bkhd->bqhd', grad_scores, key_block)
        grad_keys = jnp.einsum('bhqk,bqhd->bkhd', grad_scores, query_block)
        near_ids = ids[:, :NBR].reshape(-1)
        near_keys = grad_keys[:, :NBR * BS].reshape(GB * NBR, BS, D)
        near_values = grad_values[:, :NBR * BS].reshape(GB * NBR, BS, D)
        key_grads = key_grads.at[near_ids].add(near_keys)
        value_grads = value_grads.at[near_ids].add(near_values)
        far_term = jnp.concatenate([grad_keys[:, NBR * BS:].reshape(GB, BS, D),
                                    grad_values[:, NBR * BS:].reshape(GB, BS, D)], axis=-1).astype(jnp.bfloat16)
        return (key_grads, value_grads), (attended.reshape(GB, BS, D), grad_query.reshape(GB, BS, D), far_term)

    starts = jnp.arange(0, NB, GB, dtype=jnp.int32)
    zero_grads = jnp.zeros((NB, BS, D), jnp.float32)
    (key_grads, value_grads), (attended, grad_query, far_term) = lax.scan(attend, (zero_grads, zero_grads), starts)
    far_term = lax.optimization_barrier(far_term.reshape(NB, BS, 2 * D))
    partner_term = far_term[partner].astype(jnp.float32)
    key_grads = key_grads + partner_term[..., :D]
    value_grads = value_grads + partner_term[..., D:]
    attended = attended.reshape(NODES, D)
    layer_out = jnp.dot(attended, w_out, preferred_element_type=jnp.float32).astype(jnp.bfloat16)
    stacked = jnp.stack([grad_query.reshape(NB, BS, N_HEAD, HG * head_dim),
                         key_grads.reshape(NB, BS, N_HEAD, HG * head_dim),
                         value_grads.reshape(NB, BS, N_HEAD, HG * head_dim)], axis=3)
    dqkv = stacked.reshape(NODES, 3 * D).astype(jnp.bfloat16)
    feat_grad = jnp.dot(dqkv, w_qkv.T, preferred_element_type=jnp.float32).astype(jnp.bfloat16)
    dw_qkv = jnp.dot(node_feats.T, dqkv, preferred_element_type=jnp.float32)
    dw_out = jnp.dot(attended.T, layer_cot, preferred_element_type=jnp.float32)
    return (layer_out, feat_grad, dw_qkv, dw_out)
```

```python
import jax
import jax.numpy as jnp
from jax import lax
from jax.experimental import pallas as pl
from jax.experimental.pallas import tpu as pltpu
from jax.sharding import PartitionSpec as P

H = 8
NBR = 4
DEVICES = ("dom", "head")
F32, BF16 = jnp.float32, jnp.bfloat16
NEG = -1e30
LANES = 128
STATS = 3 * H
VMEM_LIMIT = 58 * 1024 * 1024


def nn(a, b):
    return jnp.dot(a, b, preferred_element_type=F32)


def nt(a, b):
    return lax.dot_general(a, b, (((1,), (1,)), ((), ())), preferred_element_type=F32)


def two_heads(pair):
    lane = lax.broadcasted_iota(jnp.int32, pair.shape, 1)
    zero = jnp.zeros_like(pair)
    return jnp.concatenate(
        [jnp.where(lane < LANES // 2, pair, zero), jnp.where(lane >= LANES // 2, pair, zero)], axis=0
    )


def own_heads(both):
    half, rows = both.shape[0] // 2, both.shape[1] // 2
    return jnp.concatenate([both[:half, :rows], both[half:, rows:]], axis=0)


def bias_of(tile):
    bias = jnp.where(tile != 0, 0.0, NEG).astype(F32).T
    return jnp.concatenate([bias, bias], axis=1)


def split_stat(row):
    return row[:, : row.shape[1] // 2], row[:, row.shape[1] // 2 :]


def query_kernel(near_ids, meta, q_ref, cot_ref, tile_ref, k_ref, v_ref, kt_ref, vt_ref, fk_ref,
                 fv_ref, fkt_ref, fvt_ref, att_ref, dq_ref, acc_ref, stats_ref, slot_ref, p_scr, ds_scr,
                 qz_scr, cz_scr, bias_scr):
    i = pl.program_id(0)
    pairs = q_ref.shape[1] // LANES
    bs = q_ref.shape[0]
    width = q_ref.shape[1]
    own = acc_ref.shape[0]

    @pl.when(i == 0)
    def _():
        acc_ref[...] = jnp.zeros_like(acc_ref)

    for j in range(NBR):
        bias_scr[j] = bias_of(tile_ref[0, j])
    ids = [near_ids[i, j] for j in range(NBR)]
    for c in range(pairs):
        cols = slice(c * LANES, (c + 1) * LANES)
        cot = cot_ref[:, cols]
        qz = two_heads(q_ref[:, cols])
        cz = two_heads(cot)
        qz_scr[c] = qz
        cz_scr[c] = cz
        scores = [nt(k_ref[ids[j], :, cols], qz) + bias_scr[j] for j in range(NBR)]
        scores.append(nt(fk_ref[0, :, cols], qz))
        scores = jnp.concatenate(scores, axis=0)
        peak = jnp.max(scores, axis=0, keepdims=True)
        probs = jnp.exp(scores - peak)
        inv = 1.0 / jnp.sum(probs, axis=0, keepdims=True)
        probs = probs * inv
        low = probs.astype(BF16)
        vt = jnp.concatenate([vt_ref[ids[j], cols, :] for j in range(NBR)] + [fvt_ref[0, cols, :]], axis=1)
        att = own_heads(nn(vt, low)).astype(BF16).astype(F32)
        att_ref[:, cols] = att.T.astype(BF16)
        prod = cot.astype(F32).T * att
        delta = jnp.concatenate(
            [jnp.sum(prod[: LANES // 2], axis=0, keepdims=True), jnp.sum(prod[LANES // 2 :], axis=0, keepdims=True)],
            axis=1,
        )
        grad_probs = jnp.concatenate(
            [nt(v_ref[ids[j], :, cols], cz) for j in range(NBR)] + [nt(fv_ref[0, :, cols], cz)], axis=0
        )
        ds = (probs * (grad_probs - delta)).astype(BF16)
        kt = jnp.concatenate([kt_ref[ids[j], cols, :] for j in range(NBR)] + [fkt_ref[0, cols, :]], axis=1)
        dq = own_heads(nn(kt, ds)) * 0.125
        dq_ref[:, cols] = dq.T.astype(BF16)
        p_scr[c] = low[: NBR * bs]
        ds_scr[c] = ds[: NBR * bs]
        for s, row in enumerate((peak, inv, delta)):
            first, second = split_stat(row)
            for e, part in enumerate((first, second)):
                at = s * H + 2 * c + e
                stats_ref[0, at : at + 1, :] = part
                slot_ref[0, at : at + 1, :] = part

    for j in range(NBR):

        @pl.when(ids[j] < own)
        def _(j=j):
            n = ids[j]
            for c in range(pairs):
                cols = slice(c * LANES, (c + 1) * LANES)
                vcols = slice(width + c * LANES, width + (c + 1) * LANES)
                rows = slice(j * bs, (j + 1) * bs)
                acc_ref[n, :, cols] += nn(ds_scr[c, rows, :], qz_scr[c])
                acc_ref[n, :, vcols] += nn(p_scr[c, rows, :], cz_scr[c])


def load_stats(ref, c):
    return [
        jnp.concatenate(
            [ref[0, s * H + 2 * c : s * H + 2 * c + 1, :], ref[0, s * H + 2 * c + 1 : s * H + 2 * c + 2, :]], axis=1
        )
        for s in range(3)
    ]


def key_terms(k, v, qz, cz, bias, stats):
    peak, inv, delta = stats
    scores = nt(k, qz)
    if bias is not None:
        scores = scores + bias
    probs = jnp.exp(scores - peak) * inv
    ds = (probs * (nt(v, cz) - delta)).astype(BF16)
    return nn(ds, qz), nn(probs.astype(BF16), cz)


def peer_kernel(near_ids, meta, q_ref, cot_ref, stats_ref, tile_ref, k_ref, v_ref, acc_in, acc_ref, qz_scr, cz_scr):
    i = pl.program_id(0)
    pairs = q_ref.shape[1] // LANES
    width = q_ref.shape[1]
    own = acc_ref.shape[0]

    @pl.when(i == 0)
    def _():
        acc_ref[...] = acc_in[...]

    for c in range(pairs):
        cols = slice(c * LANES, (c + 1) * LANES)
        qz_scr[c] = two_heads(q_ref[:, cols])
        cz_scr[c] = two_heads(cot_ref[:, cols])
    for j in range(NBR):
        n = near_ids[own + i, j]

        @pl.when(n < own)
        def _(j=j, n=n):
            bias = bias_of(tile_ref[0, j])
            for c in range(pairs):
                cols = slice(c * LANES, (c + 1) * LANES)
                vcols = slice(width + c * LANES, width + (c + 1) * LANES)
                dk, dv = key_terms(
                    k_ref[n, :, cols], v_ref[n, :, cols], qz_scr[c], cz_scr[c], bias, load_stats(stats_ref, c)
                )
                acc_ref[n, :, cols] += dk
                acc_ref[n, :, vcols] += dv


def far_kernel(meta, q_ref, cot_ref, stats_ref, k_ref, v_ref, acc_ref, dkv_ref):
    pairs = q_ref.shape[1] // LANES
    width = q_ref.shape[1]
    for c in range(pairs):
        cols = slice(c * LANES, (c + 1) * LANES)
        vcols = slice(width + c * LANES, width + (c + 1) * LANES)
        dk, dv = key_terms(
            k_ref[0, :, cols], v_ref[0, :, cols], two_heads(q_ref[:, cols]), two_heads(cot_ref[:, cols]), None,
            load_stats(stats_ref, c),
        )
        dkv_ref[:, cols] = (acc_ref[0, :, cols] + dk.astype(BF16).astype(F32)).astype(BF16)
        dkv_ref[:, vcols] = (acc_ref[0, :, vcols] + dv.astype(BF16).astype(F32)).astype(BF16)


def call(kernel, scalars, steps, in_specs, out_specs, out_shape, scratch, flops, touched, name):
    return pl.pallas_call(
        kernel,
        grid_spec=pltpu.PrefetchScalarGridSpec(
            num_scalar_prefetch=scalars, grid=(steps,), in_specs=in_specs, out_specs=out_specs, scratch_shapes=scratch
        ),
        out_shape=out_shape,
        compiler_params=pltpu.CompilerParams(dimension_semantics=("arbitrary",), vmem_limit_bytes=VMEM_LIMIT),
        cost_estimate=pl.CostEstimate(flops=flops, bytes_accessed=touched, transcendentals=0),
        name=name,
    )


def once(shape, at=0):
    return pl.BlockSpec(shape, lambda i, *s: (at,) + (0,) * (len(shape) - 1), pipeline_mode=pl.Buffered(1))


def body(node_feats, w_qkv, w_out, neighbours, tiles, partner, layer_cot):
    rows, width = node_feats.shape
    doms, groups = lax.axis_size("dom"), lax.axis_size("head")
    devices = doms * groups
    blocks = partner.shape[0]
    own = blocks // groups
    bs = tiles.shape[2]
    span = width // groups
    half = lax.axis_index("head")
    base = half * own

    near_ids = jnp.roll((neighbours - base) % blocks, -base, axis=0)
    mine = lax.dynamic_slice_in_dim(partner, base, own, 0)
    meta = jnp.concatenate([base[None].astype(jnp.int32), mine // own])
    table = lax.all_gather(partner, "dom", axis=0, tiled=True)
    one_hot = (table[:, None] == jnp.arange(table.shape[0], dtype=jnp.int32)[None, :]).astype(BF16)

    w_by = w_qkv.reshape(width, groups, 3, span).transpose(2, 0, 1, 3).reshape(3, width, width)
    w_all = jnp.concatenate([w_by[0] * jnp.asarray(0.125, BF16), w_by[1], w_by[2]], axis=1)

    def swap(x):
        return lax.ppermute(x, "head", [(0, 1), (1, 0)])

    def exchange(x):
        return lax.all_to_all(x, DEVICES, split_axis=0, concat_axis=0, tiled=True)

    def far(x):
        spread = exchange(x.reshape(own, bs, width).transpose(1, 0, 2))
        picked = jnp.dot(one_hot, spread.reshape(-1, width), preferred_element_type=F32).astype(BF16)
        back = exchange(picked.reshape(devices, own, width))
        return back.transpose(1, 0, 2).reshape(rows, width)

    cot = jnp.dot(layer_cot, w_out.T, preferred_element_type=F32).astype(BF16)
    far_feats = far(node_feats)
    peer_feats = swap(node_feats)
    far_cot = far(cot)
    peer_cot = swap(cot)

    part_feats = jnp.concatenate([node_feats, peer_feats], axis=0)
    part_qkv = jnp.dot(part_feats, w_all, preferred_element_type=F32).astype(BF16)
    far_qkv = jnp.dot(far_feats, w_all, preferred_element_type=F32).astype(BF16)

    def turned(feats):
        flat = jnp.einsum("dc,brd->bcr", w_all[:, width:], feats.reshape(-1, bs, width), preferred_element_type=F32)
        return flat.astype(BF16)

    part_t, far_t = turned(part_feats), turned(far_feats)
    part_blk = part_qkv.reshape(blocks, bs, 3 * width)
    far_blk = far_qkv.reshape(own, bs, 3 * width)

    step = lambda i, *s: (i, 0)
    pair_flops = 2 * bs * bs * width * 2
    att, dq, acc, stats, slots = call(
        query_kernel, 2, own,
        [
            pl.BlockSpec((bs, width), step),
            pl.BlockSpec((bs, width), step),
            pl.BlockSpec((1, NBR, bs, bs), lambda i, ids, meta: (meta[0] + i, 0, 0, 0)),
            pl.BlockSpec((blocks, bs, width), lambda i, *s: (0, 0, 1), pipeline_mode=pl.Buffered(1)),
            pl.BlockSpec((blocks, bs, width), lambda i, *s: (0, 0, 2), pipeline_mode=pl.Buffered(1)),
            pl.BlockSpec((blocks, width, bs), lambda i, *s: (0, 0, 0), pipeline_mode=pl.Buffered(1)),
            pl.BlockSpec((blocks, width, bs), lambda i, *s: (0, 1, 0), pipeline_mode=pl.Buffered(1)),
            pl.BlockSpec((1, bs, width), lambda i, *s: (i, 0, 1)),
            pl.BlockSpec((1, bs, width), lambda i, *s: (i, 0, 2)),
            pl.BlockSpec((1, width, bs), lambda i, *s: (i, 0, 0)),
            pl.BlockSpec((1, width, bs), lambda i, *s: (i, 1, 0)),
        ],
        [
            pl.BlockSpec((bs, width), step),
            pl.BlockSpec((bs, width), step),
            pl.BlockSpec((own, bs, 2 * width), lambda i, *s: (0, 0, 0)),
            pl.BlockSpec((1, STATS, bs), lambda i, *s: (i, 0, 0)),
            pl.BlockSpec((1, STATS, bs), lambda i, ids, meta: (meta[1 + i], 0, 0)),
        ],
        [
            jax.ShapeDtypeStruct((rows, width), BF16),
            jax.ShapeDtypeStruct((rows, width), BF16),
            jax.ShapeDtypeStruct((own, bs, 2 * width), F32),
            jax.ShapeDtypeStruct((own, STATS, bs), F32),
            jax.ShapeDtypeStruct((devices, STATS, bs), F32),
        ],
        [
            pltpu.VMEM((width // LANES, NBR * bs, 2 * bs), BF16),
            pltpu.VMEM((width // LANES, NBR * bs, 2 * bs), BF16),
            pltpu.VMEM((width // LANES, 2 * bs, LANES), BF16),
            pltpu.VMEM((width // LANES, 2 * bs, LANES), BF16),
            pltpu.VMEM((NBR, bs, 2 * bs), F32),
        ],
        own * 40 * pair_flops, 30 << 20, "own_queries",
    )(near_ids, meta, part_qkv, cot, tiles, part_blk, part_blk, part_t, part_t, far_blk, far_blk, far_t, far_t)

    peer_stats = swap(stats)
    far_slots = exchange(slots)

    layer_out = jnp.dot(att, w_out, preferred_element_type=F32).astype(BF16)
    dwo_t = jnp.einsum("rc,ra->ca", layer_cot, att, preferred_element_type=F32).astype(BF16)
    dwq = jnp.einsum("rd,rc->dc", node_feats, dq, preferred_element_type=F32).astype(BF16)

    def pieces(w):
        return w.reshape(doms, width // doms, groups, span).transpose(0, 2, 1, 3).reshape(devices, width // doms, span)

    def summed(ws):
        moved = exchange(jnp.concatenate([pieces(w) for w in ws], axis=2))
        return jnp.sum(moved.astype(F32), axis=0)

    early = summed([dwo_t, dwq])

    (acc,) = call(
        peer_kernel, 2, own,
        [
            pl.BlockSpec((bs, width), lambda i, *s: (own + i, 0)),
            pl.BlockSpec((bs, width), step),
            pl.BlockSpec((1, STATS, bs), lambda i, *s: (i, 0, 0)),
            pl.BlockSpec((1, NBR, bs, bs), lambda i, ids, meta: (own - meta[0] + i, 0, 0, 0)),
            pl.BlockSpec((own, bs, width), lambda i, *s: (0, 0, 1), pipeline_mode=pl.Buffered(1)),
            pl.BlockSpec((own, bs, width), lambda i, *s: (0, 0, 2), pipeline_mode=pl.Buffered(1)),
            once((own, bs, 2 * width)),
        ],
        [pl.BlockSpec((own, bs, 2 * width), lambda i, *s: (0, 0, 0))],
        [jax.ShapeDtypeStruct((own, bs, 2 * width), F32)],
        [
            pltpu.VMEM((width // LANES, 2 * bs, LANES), BF16),
            pltpu.VMEM((width // LANES, 2 * bs, LANES), BF16),
        ],
        own * 16 * pair_flops, 20 << 20, "peer_queries",
    )(near_ids, meta, part_qkv, peer_cot, peer_stats, tiles, part_blk, part_blk, acc)

    (dkv,) = call(
        far_kernel, 1, own,
        [
            pl.BlockSpec((bs, width), step),
            pl.BlockSpec((bs, width), step),
            pl.BlockSpec((1, STATS, bs), lambda i, meta: (meta[1 + i], 0, 0)),
            pl.BlockSpec((1, bs, width), lambda i, *s: (i, 0, 1)),
            pl.BlockSpec((1, bs, width), lambda i, *s: (i, 0, 2)),
            pl.BlockSpec((1, bs, 2 * width), lambda i, *s: (i, 0, 0)),
        ],
        [pl.BlockSpec((bs, 2 * width), step)],
        [jax.ShapeDtypeStruct((rows, 2 * width), BF16)],
        [], own * 8 * pair_flops, 10 << 20, "far_queries",
    )(meta, far_qkv, far_cot, far_slots, part_blk, part_blk, acc)

    dwkv = jnp.einsum("rd,rc->dc", node_feats, dkv, preferred_element_type=F32).astype(BF16)
    late = summed([dwkv[:, :width], dwkv[:, width:]])
    w_plain = w_by.transpose(1, 0, 2).reshape(width, 3 * width)
    feat_grad = (
        lax.dot_general(dq, w_plain[:, :width], (((1,), (1,)), ((), ())), preferred_element_type=F32)
        + lax.dot_general(dkv, w_plain[:, width:], (((1,), (1,)), ((), ())), preferred_element_type=F32)
    ).astype(BF16)
    dw_out = early[:, :span].T
    dw_qkv = jnp.concatenate([early[:, span:], late], axis=1)
    return (layer_out, feat_grad, dw_qkv, dw_out)


def solution(mesh):
    placed = (
        P(DEVICES, None),
        P(),
        P(),
        P("dom", None),
        P("dom", None, None, None),
        P("dom"),
        P(DEVICES, None),
    )
    return jax.shard_map(
        body,
        mesh=mesh,
        in_specs=placed,
        out_specs=(P(DEVICES, None), P(DEVICES, None), P("dom", "head"), P("head", "dom")),
        check_vma=False,
    )
```

```python
import functools

import jax
import jax.numpy as jnp
from jax import lax
from jax.experimental import pallas as pl
from jax.experimental.pallas import tpu as pltpu
from jax.sharding import PartitionSpec as P

H = 8
NBR = 4
DEVICES = ("dom", "head")
F32, BF16 = jnp.float32, jnp.bfloat16
NEG = -1e30
LANES = 128
STATS = 3 * H
DIGIT = 32
VMEM_LIMIT = 58 * 1024 * 1024


def nn(a, b):
    return jnp.dot(a, b, preferred_element_type=F32)


def nt(a, b):
    return lax.dot_general(a, b, (((1,), (1,)), ((), ())), preferred_element_type=F32)


def two_heads(pair):
    lane = lax.broadcasted_iota(jnp.int32, pair.shape, 1)
    zero = jnp.zeros_like(pair)
    return jnp.concatenate(
        [jnp.where(lane < LANES // 2, pair, zero), jnp.where(lane >= LANES // 2, pair, zero)], axis=0
    )


def own_heads(both):
    half, rows = both.shape[0] // 2, both.shape[1] // 2
    return jnp.concatenate([both[:half, :rows], both[half:, rows:]], axis=0)


def bias_of(tile):
    bias = jnp.where(tile != 0, 0.0, NEG).astype(F32).T
    return jnp.concatenate([bias, bias], axis=1)


def split_stat(row):
    return row[:, : row.shape[1] // 2], row[:, row.shape[1] // 2 :]


def query_kernel(first, near_ids, meta, q_ref, cot_ref, tile_ref, k_ref, v_ref, kt_ref, vt_ref, fk_ref,
                 fv_ref, fkt_ref, fvt_ref, *rest):
    if first:
        acc_in = None
    else:
        acc_in, rest = rest[0], rest[5:]
    att_ref, dq_ref, acc_ref, stats_ref, slot_ref, p_scr, ds_scr, qz_scr, cz_scr, bias_scr = rest
    i = pl.program_id(0)
    block = i if first else i + pl.num_programs(0)
    pairs = q_ref.shape[1] // LANES
    bs = q_ref.shape[0]
    width = q_ref.shape[1]
    own = acc_ref.shape[0]

    @pl.when(i == 0)
    def _():
        acc_ref[...] = jnp.zeros_like(acc_ref) if first else acc_in[...]

    for j in range(NBR):
        bias_scr[j] = bias_of(tile_ref[0, j])
    ids = [near_ids[block, j] for j in range(NBR)]
    for c in range(pairs):
        cols = slice(c * LANES, (c + 1) * LANES)
        cot = cot_ref[:, cols]
        qz = two_heads(q_ref[:, cols])
        cz = two_heads(cot)
        qz_scr[c] = qz
        cz_scr[c] = cz
        scores = [nt(k_ref[ids[j], :, cols], qz) + bias_scr[j] for j in range(NBR)]
        scores.append(nt(fk_ref[0, :, cols], qz))
        scores = jnp.concatenate(scores, axis=0)
        peak = jnp.max(scores, axis=0, keepdims=True)
        probs = jnp.exp(scores - peak)
        inv = 1.0 / jnp.sum(probs, axis=0, keepdims=True)
        probs = probs * inv
        low = probs.astype(BF16)
        vt = jnp.concatenate([vt_ref[ids[j], cols, :] for j in range(NBR)] + [fvt_ref[0, cols, :]], axis=1)
        att = own_heads(nn(vt, low)).astype(BF16).astype(F32)
        att_ref[:, cols] = att.T.astype(BF16)
        prod = cot.astype(F32).T * att
        delta = jnp.concatenate(
            [jnp.sum(prod[: LANES // 2], axis=0, keepdims=True), jnp.sum(prod[LANES // 2 :], axis=0, keepdims=True)],
            axis=1,
        )
        grad_probs = jnp.concatenate(
            [nt(v_ref[ids[j], :, cols], cz) for j in range(NBR)] + [nt(fv_ref[0, :, cols], cz)], axis=0
        )
        ds = (probs * (grad_probs - delta)).astype(BF16)
        kt = jnp.concatenate([kt_ref[ids[j], cols, :] for j in range(NBR)] + [fkt_ref[0, cols, :]], axis=1)
        dq = own_heads(nn(kt, ds)) * 0.125
        dq_ref[:, cols] = dq.T.astype(BF16)
        p_scr[c] = low[: NBR * bs]
        ds_scr[c] = ds[: NBR * bs]
        for s, row in enumerate((peak, inv, delta)):
            first, second = split_stat(row)
            for e, part in enumerate((first, second)):
                at = s * H + 2 * c + e
                stats_ref[0, at : at + 1, :] = part
                slot_ref[0, at : at + 1, :] = part

    for j in range(NBR):

        @pl.when(ids[j] < own)
        def _(j=j):
            n = ids[j]
            for c in range(pairs):
                cols = slice(c * LANES, (c + 1) * LANES)
                vcols = slice(width + c * LANES, width + (c + 1) * LANES)
                rows = slice(j * bs, (j + 1) * bs)
                acc_ref[n, :, cols] += nn(ds_scr[c, rows, :], qz_scr[c])
                acc_ref[n, :, vcols] += nn(p_scr[c, rows, :], cz_scr[c])


def load_stats(ref, c):
    return [
        jnp.concatenate(
            [ref[0, s * H + 2 * c : s * H + 2 * c + 1, :], ref[0, s * H + 2 * c + 1 : s * H + 2 * c + 2, :]], axis=1
        )
        for s in range(3)
    ]


def key_terms(k, v, qz, cz, bias, stats):
    peak, inv, delta = stats
    scores = nt(k, qz)
    if bias is not None:
        scores = scores + bias
    probs = jnp.exp(scores - peak) * inv
    ds = (probs * (nt(v, cz) - delta)).astype(BF16)
    return nn(ds, qz), nn(probs.astype(BF16), cz)


def peer_kernel(near_ids, meta, q_ref, cot_ref, stats_ref, tile_ref, k_ref, v_ref, acc_in, acc_ref, qz_scr, cz_scr):
    i = pl.program_id(0)
    pairs = q_ref.shape[1] // LANES
    width = q_ref.shape[1]
    own = acc_ref.shape[0]

    @pl.when(i == 0)
    def _():
        acc_ref[...] = acc_in[...]

    for c in range(pairs):
        cols = slice(c * LANES, (c + 1) * LANES)
        qz_scr[c] = two_heads(q_ref[:, cols])
        cz_scr[c] = two_heads(cot_ref[:, cols])
    for j in range(NBR):
        n = near_ids[own + i, j]

        @pl.when(n < own)
        def _(j=j, n=n):
            bias = bias_of(tile_ref[0, j])
            for c in range(pairs):
                cols = slice(c * LANES, (c + 1) * LANES)
                vcols = slice(width + c * LANES, width + (c + 1) * LANES)
                dk, dv = key_terms(
                    k_ref[n, :, cols], v_ref[n, :, cols], qz_scr[c], cz_scr[c], bias, load_stats(stats_ref, c)
                )
                acc_ref[n, :, cols] += dk
                acc_ref[n, :, vcols] += dv


def far_kernel(meta, q_ref, cot_ref, stats_ref, k_ref, v_ref, acc_ref, dkv_ref):
    pairs = q_ref.shape[1] // LANES
    width = q_ref.shape[1]
    for c in range(pairs):
        cols = slice(c * LANES, (c + 1) * LANES)
        vcols = slice(width + c * LANES, width + (c + 1) * LANES)
        dk, dv = key_terms(
            k_ref[0, :, cols], v_ref[0, :, cols], two_heads(q_ref[:, cols]), two_heads(cot_ref[:, cols]), None,
            load_stats(stats_ref, c),
        )
        dkv_ref[:, cols] = (acc_ref[0, :, cols] + dk.astype(BF16).astype(F32)).astype(BF16)
        dkv_ref[:, vcols] = (acc_ref[0, :, vcols] + dv.astype(BF16).astype(F32)).astype(BF16)


def call(kernel, scalars, steps, in_specs, out_specs, out_shape, scratch, flops, touched, name, aliases={}):
    return pl.pallas_call(
        kernel,
        grid_spec=pltpu.PrefetchScalarGridSpec(
            num_scalar_prefetch=scalars, grid=(steps,), in_specs=in_specs, out_specs=out_specs, scratch_shapes=scratch
        ),
        out_shape=out_shape,
        input_output_aliases=aliases,
        compiler_params=pltpu.CompilerParams(dimension_semantics=("arbitrary",), vmem_limit_bytes=VMEM_LIMIT),
        cost_estimate=pl.CostEstimate(flops=flops, bytes_accessed=touched, transcendentals=0),
        name=name,
    )


def once(shape, at=0):
    return pl.BlockSpec(shape, lambda i, *s: (at,) + (0,) * (len(shape) - 1), pipeline_mode=pl.Buffered(1))


def body(node_feats, w_qkv, w_out, neighbours, tiles, partner, layer_cot):
    rows, width = node_feats.shape
    doms, groups = lax.axis_size("dom"), lax.axis_size("head")
    devices = doms * groups
    blocks = partner.shape[0]
    own = blocks // groups
    bs = tiles.shape[2]
    span = width // groups
    half = lax.axis_index("head")
    base = half * own

    near_ids = jnp.roll((neighbours - base) % blocks, -base, axis=0)
    mine = lax.dynamic_slice_in_dim(partner, base, own, 0)
    meta = jnp.concatenate([base[None].astype(jnp.int32), mine // own])

    w_by = w_qkv.reshape(width, groups, 3, span).transpose(2, 0, 1, 3).reshape(3, width, width)
    w_all = jnp.concatenate([w_by[0] * jnp.asarray(0.125, BF16), w_by[1], w_by[2]], axis=1)

    def swap(x):
        return lax.ppermute(x, "head", [(0, 1), (1, 0)])

    def exchange(x):
        return lax.all_to_all(x, DEVICES, split_axis=0, concat_axis=0, tiled=True)

    def spread(x):
        return x.reshape(own, bs, width).transpose(1, 0, 2)

    def gathered(x):
        return jnp.dot(one_hot, x.reshape(-1, width), preferred_element_type=F32).astype(BF16).reshape(
            devices, own, width
        )

    digits = jnp.stack([mine // DIGIT, mine % DIGIT], axis=1).astype(BF16)
    digits = jnp.pad(digits, ((0, 0), (0, LANES - 2)))
    digits = jnp.broadcast_to(digits[None], (devices, own, LANES))
    rows_in = exchange(jnp.concatenate([spread(node_feats), digits], axis=2))
    peer_feats = swap(node_feats)
    cot = jnp.dot(layer_cot, w_out.T, preferred_element_type=F32).astype(BF16)
    ids = rows_in[:, :, width].astype(F32) * DIGIT + rows_in[:, :, width + 1].astype(F32)
    ids = ids.astype(jnp.int32).reshape(-1)
    one_hot = (ids[:, None] == jnp.arange(ids.shape[0], dtype=jnp.int32)[None, :]).astype(BF16)
    far_rows = exchange(gathered(rows_in[:, :, :width]))

    part_feats = jnp.concatenate([node_feats, peer_feats], axis=0)
    part_qkv = jnp.dot(part_feats, w_all, preferred_element_type=F32).astype(BF16)

    def turned(feats):
        flat = jnp.einsum("dc,brd->bcr", w_all[:, width:], feats.reshape(-1, bs, width), preferred_element_type=F32)
        return flat.astype(BF16)

    part_t = turned(part_feats)
    far_rows, part_qkv, part_t, cot = lax.optimization_barrier((far_rows, part_qkv, part_t, cot))
    far_feats = far_rows.transpose(1, 0, 2).reshape(rows, width)
    cot_in = exchange(spread(cot))
    peer_cot = swap(cot)
    far_qkv = jnp.dot(far_feats, w_all, preferred_element_type=F32).astype(BF16)
    far_t = turned(far_feats)
    part_blk = part_qkv.reshape(blocks, bs, 3 * width)
    far_blk = far_qkv.reshape(own, bs, 3 * width)

    step = lambda i, *s: (i, 0)
    pair_flops = 2 * bs * bs * width * 2
    hold = pl.BlockSpec(memory_space=pl.ANY)

    def own_queries(first, carried=()):
        steps = own // 2
        off = 0 if first else steps
        at = lambda i, *s: (off + i, 0)
        return call(
            functools.partial(query_kernel, first), 2, steps,
            [
                pl.BlockSpec((bs, width), at),
                pl.BlockSpec((bs, width), at),
                pl.BlockSpec((1, NBR, bs, bs), lambda i, ids, meta: (meta[0] + off + i, 0, 0, 0)),
                pl.BlockSpec((blocks, bs, width), lambda i, *s: (0, 0, 1), pipeline_mode=pl.Buffered(1)),
                pl.BlockSpec((blocks, bs, width), lambda i, *s: (0, 0, 2), pipeline_mode=pl.Buffered(1)),
                pl.BlockSpec((blocks, width, bs), lambda i, *s: (0, 0, 0), pipeline_mode=pl.Buffered(1)),
                pl.BlockSpec((blocks, width, bs), lambda i, *s: (0, 1, 0), pipeline_mode=pl.Buffered(1)),
                pl.BlockSpec((1, bs, width), lambda i, *s: (off + i, 0, 1)),
                pl.BlockSpec((1, bs, width), lambda i, *s: (off + i, 0, 2)),
                pl.BlockSpec((1, width, bs), lambda i, *s: (off + i, 0, 0)),
                pl.BlockSpec((1, width, bs), lambda i, *s: (off + i, 1, 0)),
            ]
            + ([] if first else [once((own, bs, 2 * width)), hold, hold, hold, hold]),
            [
                pl.BlockSpec((bs, width), at),
                pl.BlockSpec((bs, width), at),
                pl.BlockSpec((own, bs, 2 * width), lambda i, *s: (0, 0, 0)),
                pl.BlockSpec((1, STATS, bs), lambda i, *s: (off + i, 0, 0)),
                pl.BlockSpec((1, STATS, bs), lambda i, ids, meta: (meta[1 + off + i], 0, 0)),
            ],
            [
                jax.ShapeDtypeStruct((rows, width), BF16),
                jax.ShapeDtypeStruct((rows, width), BF16),
                jax.ShapeDtypeStruct((own, bs, 2 * width), F32),
                jax.ShapeDtypeStruct((own, STATS, bs), F32),
                jax.ShapeDtypeStruct((devices, STATS, bs), F32),
            ],
            [
                pltpu.VMEM((width // LANES, NBR * bs, 2 * bs), BF16),
                pltpu.VMEM((width // LANES, NBR * bs, 2 * bs), BF16),
                pltpu.VMEM((width // LANES, 2 * bs, LANES), BF16),
                pltpu.VMEM((width // LANES, 2 * bs, LANES), BF16),
                pltpu.VMEM((NBR, bs, 2 * bs), F32),
            ],
            steps * 40 * pair_flops, 30 << 20, "own_first" if first else "own_second",
            aliases={} if first else {13: 2, 14: 0, 15: 1, 16: 3, 17: 4},
        )(near_ids, meta, part_qkv, cot, tiles, part_blk, part_blk, part_t, part_t, far_blk, far_blk, far_t, far_t,
          *carried)

    att, dq, acc, stats, slots = own_queries(True)
    acc, cot_in = lax.optimization_barrier((acc, cot_in))
    picked, acc = lax.optimization_barrier((gathered(cot_in), acc))
    far_cot = exchange(picked)
    att, dq, acc, stats, slots = own_queries(False, (acc, att, dq, stats, slots))
    far_cot, slots = lax.optimization_barrier((far_cot, slots))
    far_cot = far_cot.transpose(1, 0, 2).reshape(rows, width)

    peer_stats = swap(stats)
    far_slots = exchange(slots)

    layer_out = jnp.dot(att, w_out, preferred_element_type=F32).astype(BF16)
    dwo_t = jnp.einsum("rc,ra->ca", layer_cot, att, preferred_element_type=F32).astype(BF16)
    dwq = jnp.einsum("rd,rc->dc", node_feats, dq, preferred_element_type=F32).astype(BF16)

    (acc,) = call(
        peer_kernel, 2, own,
        [
            pl.BlockSpec((bs, width), lambda i, *s: (own + i, 0)),
            pl.BlockSpec((bs, width), step),
            pl.BlockSpec((1, STATS, bs), lambda i, *s: (i, 0, 0)),
            pl.BlockSpec((1, NBR, bs, bs), lambda i, ids, meta: (own - meta[0] + i, 0, 0, 0)),
            pl.BlockSpec((own, bs, width), lambda i, *s: (0, 0, 1), pipeline_mode=pl.Buffered(1)),
            pl.BlockSpec((own, bs, width), lambda i, *s: (0, 0, 2), pipeline_mode=pl.Buffered(1)),
            once((own, bs, 2 * width)),
        ],
        [pl.BlockSpec((own, bs, 2 * width), lambda i, *s: (0, 0, 0))],
        [jax.ShapeDtypeStruct((own, bs, 2 * width), F32)],
        [
            pltpu.VMEM((width // LANES, 2 * bs, LANES), BF16),
            pltpu.VMEM((width // LANES, 2 * bs, LANES), BF16),
        ],
        own * 16 * pair_flops, 20 << 20, "peer_queries",
    )(near_ids, meta, part_qkv, peer_cot, peer_stats, tiles, part_blk, part_blk, acc)

    (dkv,) = call(
        far_kernel, 1, own,
        [
            pl.BlockSpec((bs, width), step),
            pl.BlockSpec((bs, width), step),
            pl.BlockSpec((1, STATS, bs), lambda i, meta: (meta[1 + i], 0, 0)),
            pl.BlockSpec((1, bs, width), lambda i, *s: (i, 0, 1)),
            pl.BlockSpec((1, bs, width), lambda i, *s: (i, 0, 2)),
            pl.BlockSpec((1, bs, 2 * width), lambda i, *s: (i, 0, 0)),
        ],
        [pl.BlockSpec((bs, 2 * width), step)],
        [jax.ShapeDtypeStruct((rows, 2 * width), BF16)],
        [], own * 8 * pair_flops, 10 << 20, "far_queries",
    )(meta, far_qkv, far_cot, far_slots, part_blk, part_blk, acc)

    dwkv = jnp.einsum("rd,rc->dc", node_feats, dkv, preferred_element_type=F32).astype(BF16)
    parts = [w.reshape(doms, width // doms, width) for w in (dwo_t, dwq, dwkv[:, :width], dwkv[:, width:])]
    split = jnp.stack(
        [jnp.concatenate([w[:, :, g * span : (g + 1) * span] for w in parts], axis=2) for g in range(groups)], axis=1
    )
    moved = exchange(split.reshape(devices, width // doms, 4 * span))
    summed = jnp.sum(moved.astype(F32), axis=0)
    w_plain = w_by.transpose(1, 0, 2).reshape(width, 3 * width)
    feat_grad = (
        lax.dot_general(dq, w_plain[:, :width], (((1,), (1,)), ((), ())), preferred_element_type=F32)
        + lax.dot_general(dkv, w_plain[:, width:], (((1,), (1,)), ((), ())), preferred_element_type=F32)
    ).astype(BF16)
    dw_out = summed[:, :span].T
    dw_qkv = summed[:, span:]
    return (layer_out, feat_grad, dw_qkv, dw_out)


def solution(mesh):
    placed = (
        P(DEVICES, None),
        P(),
        P(),
        P("dom", None),
        P("dom", None, None, None),
        P("dom"),
        P(DEVICES, None),
    )
    return jax.shard_map(
        body,
        mesh=mesh,
        in_specs=placed,
        out_specs=(P(DEVICES, None), P(DEVICES, None), P("dom", "head"), P("head", "dom")),
        check_vma=False,
    )
```

```python
import jax
import jax.numpy as jnp
from jax import lax
from jax.experimental import pallas as pl
from jax.experimental.pallas import tpu as pltpu
from jax.sharding import PartitionSpec as P

H = 8
NBR = 4
DEVICES = ("dom", "head")
F32, BF16 = jnp.float32, jnp.bfloat16
NEG = -1e30
LANES = 128
STATS = 3 * H
DIGIT = 32
VMEM_LIMIT = 58 * 1024 * 1024


def nn(a, b):
    return jnp.dot(a, b, preferred_element_type=F32)


def nt(a, b):
    return lax.dot_general(a, b, (((1,), (1,)), ((), ())), preferred_element_type=F32)


def two_heads(pair):
    lane = lax.broadcasted_iota(jnp.int32, pair.shape, 1)
    zero = jnp.zeros_like(pair)
    return jnp.concatenate(
        [jnp.where(lane < LANES // 2, pair, zero), jnp.where(lane >= LANES // 2, pair, zero)], axis=0
    )


def own_heads(both):
    half, rows = both.shape[0] // 2, both.shape[1] // 2
    return jnp.concatenate([both[:half, :rows], both[half:, rows:]], axis=0)


def bias_of(tile):
    bias = jnp.where(tile != 0, 0.0, NEG).astype(F32).T
    return jnp.concatenate([bias, bias], axis=1)


def split_stat(row):
    return row[:, : row.shape[1] // 2], row[:, row.shape[1] // 2 :]


def query_kernel(near_ids, meta, q_ref, cot_ref, tile_ref, k_ref, v_ref, kt_ref, vt_ref, fk_ref,
                 fv_ref, fkt_ref, fvt_ref, att_ref, dq_ref, acc_ref, stats_ref, slot_ref, p_scr, ds_scr,
                 qz_scr, cz_scr, bias_scr):
    i = pl.program_id(0)
    pairs = q_ref.shape[1] // LANES
    bs = q_ref.shape[0]
    width = q_ref.shape[1]
    own = acc_ref.shape[0]

    @pl.when(i == 0)
    def _():
        acc_ref[...] = jnp.zeros_like(acc_ref)

    for j in range(NBR):
        bias_scr[j] = bias_of(tile_ref[0, j])
    ids = [near_ids[i, j] for j in range(NBR)]
    for c in range(pairs):
        cols = slice(c * LANES, (c + 1) * LANES)
        cot = cot_ref[:, cols]
        qz = two_heads(q_ref[:, cols])
        cz = two_heads(cot)
        qz_scr[c] = qz
        cz_scr[c] = cz
        scores = [nt(k_ref[ids[j], :, cols], qz) + bias_scr[j] for j in range(NBR)]
        scores.append(nt(fk_ref[0, :, cols], qz))
        scores = jnp.concatenate(scores, axis=0)
        peak = jnp.max(scores, axis=0, keepdims=True)
        probs = jnp.exp(scores - peak)
        inv = 1.0 / jnp.sum(probs, axis=0, keepdims=True)
        probs = probs * inv
        low = probs.astype(BF16)
        vt = jnp.concatenate([vt_ref[ids[j], cols, :] for j in range(NBR)] + [fvt_ref[0, cols, :]], axis=1)
        att = own_heads(nn(vt, low)).astype(BF16).astype(F32)
        att_ref[:, cols] = att.T.astype(BF16)
        prod = cot.astype(F32).T * att
        delta = jnp.concatenate(
            [jnp.sum(prod[: LANES // 2], axis=0, keepdims=True), jnp.sum(prod[LANES // 2 :], axis=0, keepdims=True)],
            axis=1,
        )
        grad_probs = jnp.concatenate(
            [nt(v_ref[ids[j], :, cols], cz) for j in range(NBR)] + [nt(fv_ref[0, :, cols], cz)], axis=0
        )
        ds = (probs * (grad_probs - delta)).astype(BF16)
        kt = jnp.concatenate([kt_ref[ids[j], cols, :] for j in range(NBR)] + [fkt_ref[0, cols, :]], axis=1)
        dq = own_heads(nn(kt, ds)) * 0.125
        dq_ref[:, cols] = dq.T.astype(BF16)
        p_scr[c] = low[: NBR * bs]
        ds_scr[c] = ds[: NBR * bs]
        for s, row in enumerate((peak, inv, delta)):
            first, second = split_stat(row)
            for e, part in enumerate((first, second)):
                at = s * H + 2 * c + e
                stats_ref[0, at : at + 1, :] = part
                slot_ref[0, at : at + 1, :] = part

    for j in range(NBR):

        @pl.when(ids[j] < own)
        def _(j=j):
            n = ids[j]
            for c in range(pairs):
                cols = slice(c * LANES, (c + 1) * LANES)
                vcols = slice(width + c * LANES, width + (c + 1) * LANES)
                rows = slice(j * bs, (j + 1) * bs)
                acc_ref[n, :, cols] += nn(ds_scr[c, rows, :], qz_scr[c])
                acc_ref[n, :, vcols] += nn(p_scr[c, rows, :], cz_scr[c])


def load_stats(ref, c):
    return [
        jnp.concatenate(
            [ref[0, s * H + 2 * c : s * H + 2 * c + 1, :], ref[0, s * H + 2 * c + 1 : s * H + 2 * c + 2, :]], axis=1
        )
        for s in range(3)
    ]


def key_terms(k, v, qz, cz, bias, stats):
    peak, inv, delta = stats
    scores = nt(k, qz)
    if bias is not None:
        scores = scores + bias
    probs = jnp.exp(scores - peak) * inv
    ds = (probs * (nt(v, cz) - delta)).astype(BF16)
    return nn(ds, qz), nn(probs.astype(BF16), cz)


def peer_kernel(near_ids, meta, q_ref, cot_ref, stats_ref, tile_ref, k_ref, v_ref, acc_in, acc_ref, qz_scr, cz_scr):
    i = pl.program_id(0)
    pairs = q_ref.shape[1] // LANES
    width = q_ref.shape[1]
    own = acc_ref.shape[0]

    @pl.when(i == 0)
    def _():
        acc_ref[...] = acc_in[...]

    for c in range(pairs):
        cols = slice(c * LANES, (c + 1) * LANES)
        qz_scr[c] = two_heads(q_ref[:, cols])
        cz_scr[c] = two_heads(cot_ref[:, cols])
    for j in range(NBR):
        n = near_ids[own + i, j]

        @pl.when(n < own)
        def _(j=j, n=n):
            bias = bias_of(tile_ref[0, j])
            for c in range(pairs):
                cols = slice(c * LANES, (c + 1) * LANES)
                vcols = slice(width + c * LANES, width + (c + 1) * LANES)
                dk, dv = key_terms(
                    k_ref[n, :, cols], v_ref[n, :, cols], qz_scr[c], cz_scr[c], bias, load_stats(stats_ref, c)
                )
                acc_ref[n, :, cols] += dk
                acc_ref[n, :, vcols] += dv


def far_kernel(meta, q_ref, cot_ref, stats_ref, k_ref, v_ref, acc_ref, dkv_ref):
    pairs = q_ref.shape[1] // LANES
    width = q_ref.shape[1]
    for c in range(pairs):
        cols = slice(c * LANES, (c + 1) * LANES)
        vcols = slice(width + c * LANES, width + (c + 1) * LANES)
        dk, dv = key_terms(
            k_ref[0, :, cols], v_ref[0, :, cols], two_heads(q_ref[:, cols]), two_heads(cot_ref[:, cols]), None,
            load_stats(stats_ref, c),
        )
        dkv_ref[:, cols] = (acc_ref[0, :, cols] + dk.astype(BF16).astype(F32)).astype(BF16)
        dkv_ref[:, vcols] = (acc_ref[0, :, vcols] + dv.astype(BF16).astype(F32)).astype(BF16)


def project_kernel(x_ref, w_ref, wt_ref, *rest):
    qkv_ref, t_ref = rest[-2:]
    bs = t_ref.shape[2]
    qkv_ref[...] = nn(x_ref[...], w_ref[...]).astype(BF16)
    for b in range(t_ref.shape[0]):
        t_ref[b] = nt(wt_ref[...], x_ref[b * bs : (b + 1) * bs, :]).astype(BF16)


def call(kernel, scalars, steps, in_specs, out_specs, out_shape, scratch, flops, touched, name, aliases={}):
    return pl.pallas_call(
        kernel,
        grid_spec=pltpu.PrefetchScalarGridSpec(
            num_scalar_prefetch=scalars, grid=(steps,), in_specs=in_specs, out_specs=out_specs, scratch_shapes=scratch
        ),
        out_shape=out_shape,
        input_output_aliases=aliases,
        compiler_params=pltpu.CompilerParams(dimension_semantics=("arbitrary",), vmem_limit_bytes=VMEM_LIMIT),
        cost_estimate=pl.CostEstimate(flops=flops, bytes_accessed=touched, transcendentals=0),
        name=name,
    )


def once(shape, at=0):
    return pl.BlockSpec(shape, lambda i, *s: (at,) + (0,) * (len(shape) - 1), pipeline_mode=pl.Buffered(1))


def body(node_feats, w_qkv, w_out, neighbours, tiles, partner, layer_cot):
    rows, width = node_feats.shape
    doms, groups = lax.axis_size("dom"), lax.axis_size("head")
    devices = doms * groups
    blocks = partner.shape[0]
    own = blocks // groups
    bs = tiles.shape[2]
    span = width // groups
    half = lax.axis_index("head")
    base = half * own

    near_ids = jnp.roll((neighbours - base) % blocks, -base, axis=0)
    mine = lax.dynamic_slice_in_dim(partner, base, own, 0)
    meta = jnp.concatenate([base[None].astype(jnp.int32), mine // own])

    w_by = w_qkv.reshape(width, groups, 3, span).transpose(2, 0, 1, 3).reshape(3, width, width)
    w_all = jnp.concatenate([w_by[0] * jnp.asarray(0.125, BF16), w_by[1], w_by[2]], axis=1)

    def swap(x):
        return lax.ppermute(x, "head", [(0, 1), (1, 0)])

    def exchange(x):
        return lax.all_to_all(x, DEVICES, split_axis=0, concat_axis=0, tiled=True)

    def spread(x):
        return x.reshape(own, bs, width).transpose(1, 0, 2)

    def gathered(x):
        return jnp.dot(one_hot, x.reshape(-1, width), preferred_element_type=F32).astype(BF16).reshape(
            devices, own, width
        )

    digits = jnp.stack([mine // DIGIT, mine % DIGIT], axis=1).astype(BF16)
    digits = jnp.pad(digits, ((0, 0), (0, LANES - 2)))
    digits = jnp.broadcast_to(digits[None], (devices, own, LANES))
    first_hop = jnp.concatenate([spread(node_feats), digits], axis=2)
    first_hop, feats_out = lax.optimization_barrier((first_hop, node_feats))
    rows_in = exchange(first_hop)
    peer_feats = swap(feats_out)
    cot = jnp.dot(layer_cot, w_out.T, preferred_element_type=F32).astype(BF16)
    cot_rows = spread(cot)

    w_turned = w_all[:, width:].T
    hold = pl.BlockSpec(memory_space=pl.ANY)

    def project(feats, total, at, carried, name):
        per = 2
        return call(
            project_kernel, 0, own // per,
            [
                pl.BlockSpec((per * bs, width), lambda i: (i, 0)),
                once((width, 3 * width)),
                once((2 * width, width)),
            ]
            + [hold] * len(carried),
            [
                pl.BlockSpec((per * bs, 3 * width), lambda i: (at // per + i, 0)),
                pl.BlockSpec((per, 2 * width, bs), lambda i: (at // per + i, 0, 0)),
            ],
            [
                jax.ShapeDtypeStruct((total * bs, 3 * width), BF16),
                jax.ShapeDtypeStruct((total, 2 * width, bs), BF16),
            ],
            [], 2 * rows * width * 5 * width, 8 << 20, name, aliases={3: 0, 4: 1} if carried else {},
        )(feats, w_all, w_turned, *carried)

    own_part = project(node_feats, blocks, 0, (), "project_own")
    rows_in, cot_rows, own_part, peer_feats = lax.optimization_barrier((rows_in, cot_rows, own_part, peer_feats))

    ids = rows_in[:, :, width].astype(F32) * DIGIT + rows_in[:, :, width + 1].astype(F32)
    ids = ids.astype(jnp.int32).reshape(-1)
    one_hot = (ids[:, None] == jnp.arange(ids.shape[0], dtype=jnp.int32)[None, :]).astype(BF16)
    second = jnp.concatenate([gathered(rows_in[:, :, :width]), cot_rows], axis=2)
    second, cot_out = lax.optimization_barrier((second, cot))
    second = exchange(second)
    peer_cot = swap(cot_out)
    part_qkv, part_t = project(peer_feats, blocks, own, own_part, "project_peer")
    second, peer_cot, part_qkv, part_t = lax.optimization_barrier((second, peer_cot, part_qkv, part_t))

    picked = gathered(second[:, :, width:])
    far_feats = second[:, :, :width].transpose(1, 0, 2).reshape(rows, width)
    picked, far_feats = lax.optimization_barrier((picked, far_feats))
    far_cot = exchange(picked)
    far_qkv, far_t = project(far_feats, own, 0, (), "project_far")
    part_blk = part_qkv.reshape(blocks, bs, 3 * width)
    far_blk = far_qkv.reshape(own, bs, 3 * width)

    step = lambda i, *s: (i, 0)
    pair_flops = 2 * bs * bs * width * 2
    def own_queries():
        at = lambda i, *s: (i, 0)
        return call(
            query_kernel, 2, own,
            [
                pl.BlockSpec((bs, width), at),
                pl.BlockSpec((bs, width), at),
                pl.BlockSpec((1, NBR, bs, bs), lambda i, ids, meta: (meta[0] + i, 0, 0, 0)),
                pl.BlockSpec((blocks, bs, width), lambda i, *s: (0, 0, 1), pipeline_mode=pl.Buffered(1)),
                pl.BlockSpec((blocks, bs, width), lambda i, *s: (0, 0, 2), pipeline_mode=pl.Buffered(1)),
                pl.BlockSpec((blocks, width, bs), lambda i, *s: (0, 0, 0), pipeline_mode=pl.Buffered(1)),
                pl.BlockSpec((blocks, width, bs), lambda i, *s: (0, 1, 0), pipeline_mode=pl.Buffered(1)),
                pl.BlockSpec((1, bs, width), lambda i, *s: (i, 0, 1)),
                pl.BlockSpec((1, bs, width), lambda i, *s: (i, 0, 2)),
                pl.BlockSpec((1, width, bs), lambda i, *s: (i, 0, 0)),
                pl.BlockSpec((1, width, bs), lambda i, *s: (i, 1, 0)),
            ],
            [
                pl.BlockSpec((bs, width), at),
                pl.BlockSpec((bs, width), at),
                pl.BlockSpec((own, bs, 2 * width), lambda i, *s: (0, 0, 0)),
                pl.BlockSpec((1, STATS, bs), lambda i, *s: (i, 0, 0)),
                pl.BlockSpec((1, STATS, bs), lambda i, ids, meta: (meta[1 + i], 0, 0)),
            ],
            [
                jax.ShapeDtypeStruct((rows, width), BF16),
                jax.ShapeDtypeStruct((rows, width), BF16),
                jax.ShapeDtypeStruct((own, bs, 2 * width), F32),
                jax.ShapeDtypeStruct((own, STATS, bs), F32),
                jax.ShapeDtypeStruct((devices, STATS, bs), F32),
            ],
            [
                pltpu.VMEM((width // LANES, NBR * bs, 2 * bs), BF16),
                pltpu.VMEM((width // LANES, NBR * bs, 2 * bs), BF16),
                pltpu.VMEM((width // LANES, 2 * bs, LANES), BF16),
                pltpu.VMEM((width // LANES, 2 * bs, LANES), BF16),
                pltpu.VMEM((NBR, bs, 2 * bs), F32),
            ],
            own * 40 * pair_flops, 30 << 20, "own_queries",
        )(near_ids, meta, part_qkv, cot, tiles, part_blk, part_blk, part_t, part_t, far_blk, far_blk, far_t, far_t)

    att, dq, acc, stats, slots = own_queries()
    far_cot, slots = lax.optimization_barrier((far_cot, slots))
    far_cot = far_cot.transpose(1, 0, 2).reshape(rows, width)

    peer_stats = swap(stats)
    far_slots = exchange(slots)

    layer_out = jnp.dot(att, w_out, preferred_element_type=F32).astype(BF16)
    dwo_t = jnp.einsum("rc,ra->ca", layer_cot, att, preferred_element_type=F32).astype(BF16)
    dwq = jnp.einsum("rd,rc->dc", node_feats, dq, preferred_element_type=F32).astype(BF16)

    (acc,) = call(
        peer_kernel, 2, own,
        [
            pl.BlockSpec((bs, width), lambda i, *s: (own + i, 0)),
            pl.BlockSpec((bs, width), step),
            pl.BlockSpec((1, STATS, bs), lambda i, *s: (i, 0, 0)),
            pl.BlockSpec((1, NBR, bs, bs), lambda i, ids, meta: (own - meta[0] + i, 0, 0, 0)),
            pl.BlockSpec((own, bs, width), lambda i, *s: (0, 0, 1), pipeline_mode=pl.Buffered(1)),
            pl.BlockSpec((own, bs, width), lambda i, *s: (0, 0, 2), pipeline_mode=pl.Buffered(1)),
            once((own, bs, 2 * width)),
        ],
        [pl.BlockSpec((own, bs, 2 * width), lambda i, *s: (0, 0, 0))],
        [jax.ShapeDtypeStruct((own, bs, 2 * width), F32)],
        [
            pltpu.VMEM((width // LANES, 2 * bs, LANES), BF16),
            pltpu.VMEM((width // LANES, 2 * bs, LANES), BF16),
        ],
        own * 16 * pair_flops, 20 << 20, "peer_queries",
    )(near_ids, meta, part_qkv, peer_cot, peer_stats, tiles, part_blk, part_blk, acc)

    (dkv,) = call(
        far_kernel, 1, own,
        [
            pl.BlockSpec((bs, width), step),
            pl.BlockSpec((bs, width), step),
            pl.BlockSpec((1, STATS, bs), lambda i, meta: (meta[1 + i], 0, 0)),
            pl.BlockSpec((1, bs, width), lambda i, *s: (i, 0, 1)),
            pl.BlockSpec((1, bs, width), lambda i, *s: (i, 0, 2)),
            pl.BlockSpec((1, bs, 2 * width), lambda i, *s: (i, 0, 0)),
        ],
        [pl.BlockSpec((bs, 2 * width), step)],
        [jax.ShapeDtypeStruct((rows, 2 * width), BF16)],
        [], own * 8 * pair_flops, 10 << 20, "far_queries",
    )(meta, far_qkv, far_cot, far_slots, part_blk, part_blk, acc)

    dwkv = jnp.einsum("rd,rc->dc", node_feats, dkv, preferred_element_type=F32).astype(BF16)
    parts = [w.reshape(doms, width // doms, width) for w in (dwo_t, dwq, dwkv[:, :width], dwkv[:, width:])]
    split = jnp.stack(
        [jnp.concatenate([w[:, :, g * span : (g + 1) * span] for w in parts], axis=2) for g in range(groups)], axis=1
    )
    moved = exchange(split.reshape(devices, width // doms, 4 * span))
    summed = jnp.sum(moved.astype(F32), axis=0)
    w_plain = w_by.transpose(1, 0, 2).reshape(width, 3 * width)
    feat_grad = (
        lax.dot_general(dq, w_plain[:, :width], (((1,), (1,)), ((), ())), preferred_element_type=F32)
        + lax.dot_general(dkv, w_plain[:, width:], (((1,), (1,)), ((), ())), preferred_element_type=F32)
    ).astype(BF16)
    dw_out = summed[:, :span].T
    dw_qkv = summed[:, span:]
    return (layer_out, feat_grad, dw_qkv, dw_out)


def solution(mesh):
    placed = (
        P(DEVICES, None),
        P(),
        P(),
        P("dom", None),
        P("dom", None, None, None),
        P("dom"),
        P(DEVICES, None),
    )
    return jax.shard_map(
        body,
        mesh=mesh,
        in_specs=placed,
        out_specs=(P(DEVICES, None), P(DEVICES, None), P("dom", "head"), P("head", "dom")),
        check_vma=False,
    )
```

```python
import jax
import jax.numpy as jnp
from jax import lax
from jax.experimental import pallas as pl
from jax.experimental.pallas import tpu as pltpu
from jax.sharding import PartitionSpec as P

H = 8
NBR = 4
DEVICES = ("dom", "head")
F32, BF16 = jnp.float32, jnp.bfloat16
NEG = -1e30
LANES = 128
STATS = 3 * H
DIGIT = 32
VMEM_LIMIT = 58 * 1024 * 1024


def nn(a, b):
    return jnp.dot(a, b, preferred_element_type=F32)


def nt(a, b):
    return lax.dot_general(a, b, (((1,), (1,)), ((), ())), preferred_element_type=F32)


def two_heads(pair):
    lane = lax.broadcasted_iota(jnp.int32, pair.shape, 1)
    zero = jnp.zeros_like(pair)
    return jnp.concatenate(
        [jnp.where(lane < LANES // 2, pair, zero), jnp.where(lane >= LANES // 2, pair, zero)], axis=0
    )


def own_heads(both):
    half, rows = both.shape[0] // 2, both.shape[1] // 2
    return jnp.concatenate([both[:half, :rows], both[half:, rows:]], axis=0)


def bias_of(tile):
    bias = jnp.where(tile != 0, 0.0, NEG).astype(F32).T
    return jnp.concatenate([bias, bias], axis=1)


def split_stat(row):
    return row[:, : row.shape[1] // 2], row[:, row.shape[1] // 2 :]


def near_kernel(near_ids, meta, q_ref, tile_ref, k_ref, vt_ref, out_ref, sums_ref, bias_scr):
    i = pl.program_id(0)
    for j in range(NBR):
        bias_scr[j] = bias_of(tile_ref[0, j])
    ids = [near_ids[i, j] for j in range(NBR)]
    for c in range(q_ref.shape[1] // LANES):
        cols = slice(c * LANES, (c + 1) * LANES)
        qz = two_heads(q_ref[:, cols])
        scores = jnp.concatenate([nt(k_ref[ids[j], :, cols], qz) + bias_scr[j] for j in range(NBR)], axis=0)
        peak = jnp.max(scores, axis=0, keepdims=True)
        terms = jnp.exp(scores - peak)
        total = jnp.sum(terms, axis=0, keepdims=True)
        vt = jnp.concatenate([vt_ref[ids[j], cols, :] for j in range(NBR)], axis=1)
        out_ref[0, cols, :] = own_heads(nn(vt, terms.astype(BF16)))
        store_rows(sums_ref, c, (peak, total))


def store_rows(ref, c, rows):
    for s, row in enumerate(rows):
        for e, part in enumerate(split_stat(row)):
            at = s * H + 2 * c + e
            ref[0, at : at + 1, :] = part


def merge_kernel(meta, q_ref, cot_ref, fk_ref, fvt_ref, out_ref, sums_ref, att_ref, stats_ref, slot_ref):
    mid = LANES // 2
    for c in range(q_ref.shape[1] // LANES):
        cols = slice(c * LANES, (c + 1) * LANES)
        near_peak, near_total = load_rows(sums_ref, c, 2)
        scores = nt(fk_ref[0, :, cols], two_heads(q_ref[:, cols]))
        peak = jnp.maximum(near_peak, jnp.max(scores, axis=0, keepdims=True))
        terms = jnp.exp(scores - peak)
        kept = jnp.exp(near_peak - peak)
        inv = 1.0 / (near_total * kept + jnp.sum(terms, axis=0, keepdims=True))
        far_out = own_heads(nn(fvt_ref[0, cols, :], (terms * inv).astype(BF16)))
        first, second = split_stat(kept * inv)
        near_out = out_ref[0, cols, :]
        near_out = jnp.concatenate([near_out[:mid] * first, near_out[mid:] * second], axis=0)
        att = (far_out + near_out).astype(BF16).astype(F32)
        att_ref[:, cols] = att.T.astype(BF16)
        prod = cot_ref[:, cols].astype(F32).T * att
        delta = jnp.concatenate(
            [jnp.sum(prod[:mid], axis=0, keepdims=True), jnp.sum(prod[mid:], axis=0, keepdims=True)], axis=1
        )
        store_rows(stats_ref, c, (peak, inv, delta))
        store_rows(slot_ref, c, (peak, inv, delta))


def own_kernel(near_ids, meta, q_ref, cot_ref, tile_ref, stats_ref, k_ref, v_ref, kt_ref, fk_ref, fv_ref, fkt_ref,
               dq_ref, acc_ref, p_scr, ds_scr, qz_scr, cz_scr, bias_scr):
    i = pl.program_id(0)
    bs, width = q_ref.shape
    pairs = width // LANES
    own = acc_ref.shape[0]

    @pl.when(i == 0)
    def _():
        acc_ref[...] = jnp.zeros_like(acc_ref)

    for j in range(NBR):
        bias_scr[j] = bias_of(tile_ref[0, j])
    ids = [near_ids[i, j] for j in range(NBR)]
    for c in range(pairs):
        cols = slice(c * LANES, (c + 1) * LANES)
        qz = two_heads(q_ref[:, cols])
        cz = two_heads(cot_ref[:, cols])
        qz_scr[c] = qz
        cz_scr[c] = cz
        peak, inv, delta = load_rows(stats_ref, c, 3)
        parts = []
        for j in range(NBR + 1):
            if j < NBR:
                scores = nt(k_ref[ids[j], :, cols], qz) + bias_scr[j]
                grad_probs = nt(v_ref[ids[j], :, cols], cz)
            else:
                scores = nt(fk_ref[0, :, cols], qz)
                grad_probs = nt(fv_ref[0, :, cols], cz)
            probs = jnp.exp(scores - peak) * inv
            parts.append((probs * (grad_probs - delta)).astype(BF16))
            if j < NBR:
                rows = slice(j * bs, (j + 1) * bs)
                p_scr[c, rows, :] = probs.astype(BF16)
                ds_scr[c, rows, :] = parts[j]
        kt = jnp.concatenate([kt_ref[ids[j], cols, :] for j in range(NBR)] + [fkt_ref[0, cols, :]], axis=1)
        dq = own_heads(nn(kt, jnp.concatenate(parts, axis=0))) * 0.125
        dq_ref[:, cols] = dq.T.astype(BF16)

    for j in range(NBR):

        @pl.when(ids[j] < own)
        def _(j=j):
            n = ids[j]
            for c in range(pairs):
                cols = slice(c * LANES, (c + 1) * LANES)
                vcols = slice(width + c * LANES, width + (c + 1) * LANES)
                rows = slice(j * bs, (j + 1) * bs)
                acc_ref[n, :, cols] += nn(ds_scr[c, rows, :], qz_scr[c])
                acc_ref[n, :, vcols] += nn(p_scr[c, rows, :], cz_scr[c])


def load_rows(ref, c, count):
    return [
        jnp.concatenate(
            [ref[0, s * H + 2 * c : s * H + 2 * c + 1, :], ref[0, s * H + 2 * c + 1 : s * H + 2 * c + 2, :]], axis=1
        )
        for s in range(count)
    ]


def key_terms(k, v, qz, cz, bias, stats):
    peak, inv, delta = stats
    scores = nt(k, qz)
    if bias is not None:
        scores = scores + bias
    probs = jnp.exp(scores - peak) * inv
    ds = (probs * (nt(v, cz) - delta)).astype(BF16)
    return nn(ds, qz), nn(probs.astype(BF16), cz)


def peer_kernel(near_ids, meta, q_ref, cot_ref, stats_ref, tile_ref, k_ref, v_ref, acc_in, acc_ref, qz_scr, cz_scr):
    i = pl.program_id(0)
    pairs = q_ref.shape[1] // LANES
    width = q_ref.shape[1]
    own = acc_ref.shape[0]

    @pl.when(i == 0)
    def _():
        acc_ref[...] = acc_in[...]

    for c in range(pairs):
        cols = slice(c * LANES, (c + 1) * LANES)
        qz_scr[c] = two_heads(q_ref[:, cols])
        cz_scr[c] = two_heads(cot_ref[:, cols])
    for j in range(NBR):
        n = near_ids[own + i, j]

        @pl.when(n < own)
        def _(j=j, n=n):
            bias = bias_of(tile_ref[0, j])
            for c in range(pairs):
                cols = slice(c * LANES, (c + 1) * LANES)
                vcols = slice(width + c * LANES, width + (c + 1) * LANES)
                dk, dv = key_terms(
                    k_ref[n, :, cols], v_ref[n, :, cols], qz_scr[c], cz_scr[c], bias, load_rows(stats_ref, c, 3)
                )
                acc_ref[n, :, cols] += dk
                acc_ref[n, :, vcols] += dv


def far_kernel(meta, q_ref, cot_ref, stats_ref, k_ref, v_ref, acc_ref, dkv_ref):
    pairs = q_ref.shape[1] // LANES
    width = q_ref.shape[1]
    for c in range(pairs):
        cols = slice(c * LANES, (c + 1) * LANES)
        vcols = slice(width + c * LANES, width + (c + 1) * LANES)
        dk, dv = key_terms(
            k_ref[0, :, cols], v_ref[0, :, cols], two_heads(q_ref[:, cols]), two_heads(cot_ref[:, cols]), None,
            load_rows(stats_ref, c, 3),
        )
        dkv_ref[:, cols] = (acc_ref[0, :, cols] + dk.astype(BF16).astype(F32)).astype(BF16)
        dkv_ref[:, vcols] = (acc_ref[0, :, vcols] + dv.astype(BF16).astype(F32)).astype(BF16)


def project_kernel(x_ref, w_ref, wt_ref, *rest):
    qkv_ref, t_ref = rest[-2:]
    bs = t_ref.shape[2]
    qkv_ref[...] = nn(x_ref[...], w_ref[...]).astype(BF16)
    for b in range(t_ref.shape[0]):
        t_ref[b] = nt(wt_ref[...], x_ref[b * bs : (b + 1) * bs, :]).astype(BF16)


def call(kernel, scalars, steps, in_specs, out_specs, out_shape, scratch, flops, touched, name, aliases={}):
    return pl.pallas_call(
        kernel,
        grid_spec=pltpu.PrefetchScalarGridSpec(
            num_scalar_prefetch=scalars, grid=(steps,), in_specs=in_specs, out_specs=out_specs, scratch_shapes=scratch
        ),
        out_shape=out_shape,
        input_output_aliases=aliases,
        compiler_params=pltpu.CompilerParams(dimension_semantics=("arbitrary",), vmem_limit_bytes=VMEM_LIMIT),
        cost_estimate=pl.CostEstimate(flops=flops, bytes_accessed=touched, transcendentals=0),
        name=name,
    )


def once(shape, at=0):
    return pl.BlockSpec(shape, lambda i, *s: (at,) + (0,) * (len(shape) - 1), pipeline_mode=pl.Buffered(1))


def body(node_feats, w_qkv, w_out, neighbours, tiles, partner, layer_cot):
    rows, width = node_feats.shape
    doms, groups = lax.axis_size("dom"), lax.axis_size("head")
    devices = doms * groups
    blocks = partner.shape[0]
    own = blocks // groups
    bs = tiles.shape[2]
    span = width // groups
    half = lax.axis_index("head")
    base = half * own

    near_ids = jnp.roll((neighbours - base) % blocks, -base, axis=0)
    mine = lax.dynamic_slice_in_dim(partner, base, own, 0)
    meta = jnp.concatenate([base[None].astype(jnp.int32), mine // own])

    w_by = w_qkv.reshape(width, groups, 3, span).transpose(2, 0, 1, 3).reshape(3, width, width)
    w_all = jnp.concatenate([w_by[0] * jnp.asarray(0.125, BF16), w_by[1], w_by[2]], axis=1)

    def swap(x):
        return lax.ppermute(x, "head", [(0, 1), (1, 0)])

    def exchange(x):
        return lax.all_to_all(x, DEVICES, split_axis=0, concat_axis=0, tiled=True)

    def spread(x):
        return x.reshape(own, bs, width).transpose(1, 0, 2)

    def gathered(x):
        return jnp.dot(one_hot, x.reshape(-1, width), preferred_element_type=F32).astype(BF16).reshape(
            devices, own, width
        )

    digits = jnp.stack([mine // DIGIT, mine % DIGIT], axis=1).astype(BF16)
    digits = jnp.pad(digits, ((0, 0), (0, LANES - 2)))
    digits = jnp.broadcast_to(digits[None], (devices, own, LANES))
    first_hop = jnp.concatenate([spread(node_feats), digits], axis=2)
    first_hop, feats_out = lax.optimization_barrier((first_hop, node_feats))
    rows_in = exchange(first_hop)
    peer_feats = swap(feats_out)
    cot = jnp.dot(layer_cot, w_out.T, preferred_element_type=F32).astype(BF16)
    cot_rows = spread(cot)

    w_turned = w_all[:, width:].T
    hold = pl.BlockSpec(memory_space=pl.ANY)

    def project(feats, total, at, carried, name):
        per = 2
        return call(
            project_kernel, 0, own // per,
            [
                pl.BlockSpec((per * bs, width), lambda i: (i, 0)),
                once((width, 3 * width)),
                once((2 * width, width)),
            ]
            + [hold] * len(carried),
            [
                pl.BlockSpec((per * bs, 3 * width), lambda i: (at // per + i, 0)),
                pl.BlockSpec((per, 2 * width, bs), lambda i: (at // per + i, 0, 0)),
            ],
            [
                jax.ShapeDtypeStruct((total * bs, 3 * width), BF16),
                jax.ShapeDtypeStruct((total, 2 * width, bs), BF16),
            ],
            [], 2 * rows * width * 5 * width, 8 << 20, name, aliases={3: 0, 4: 1} if carried else {},
        )(feats, w_all, w_turned, *carried)

    own_part = project(node_feats, blocks, 0, (), "project_own")
    rows_in, cot_rows, own_part, peer_feats = lax.optimization_barrier((rows_in, cot_rows, own_part, peer_feats))

    weigh = jnp.pad(jnp.asarray([DIGIT, 1], F32), (0, LANES - 2))
    ids = jnp.sum(rows_in.reshape(-1, width + LANES)[:, width:].astype(F32) * weigh[None], axis=1, keepdims=True)
    one_hot = (ids == jnp.arange(ids.shape[0], dtype=jnp.int32)[None, :].astype(F32)).astype(BF16)
    second = jnp.concatenate([gathered(rows_in[:, :, :width]), cot_rows], axis=2)
    second = exchange(second)
    part_qkv, part_t = project(peer_feats, blocks, own, own_part, "project_peer")
    part_blk = part_qkv.reshape(blocks, bs, 3 * width)
    pair_flops = 2 * bs * bs * width * 2
    step = lambda i, *s: (i, 0)
    row_step = lambda i, *s: (i, 0, 0)
    rows_spec = pl.BlockSpec((bs, width), step)
    tile_spec = pl.BlockSpec((1, NBR, bs, bs), lambda i, ids, meta: (meta[0] + i, 0, 0, 0))
    k_spec = pl.BlockSpec((blocks, bs, width), lambda i, *s: (0, 0, 1), pipeline_mode=pl.Buffered(1))
    v_spec = pl.BlockSpec((blocks, bs, width), lambda i, *s: (0, 0, 2), pipeline_mode=pl.Buffered(1))
    kt_spec = pl.BlockSpec((blocks, width, bs), lambda i, *s: (0, 0, 0), pipeline_mode=pl.Buffered(1))
    vt_spec = pl.BlockSpec((blocks, width, bs), lambda i, *s: (0, 1, 0), pipeline_mode=pl.Buffered(1))
    stats_spec = pl.BlockSpec((1, STATS, bs), row_step)
    near_out, sums = call(
        near_kernel, 2, own,
        [rows_spec, tile_spec, k_spec, vt_spec],
        [pl.BlockSpec((1, width, bs), row_step), pl.BlockSpec((1, 2 * H, bs), row_step)],
        [jax.ShapeDtypeStruct((own, width, bs), F32), jax.ShapeDtypeStruct((own, 2 * H, bs), F32)],
        [pltpu.VMEM((NBR, bs, 2 * bs), F32)],
        own * 16 * pair_flops, 10 << 20, "near_forward",
    )(near_ids, meta, part_qkv, tiles, part_blk, part_t)
    second, near_out, sums, cot_out = lax.optimization_barrier((second, near_out, sums, cot))

    picked = gathered(second[:, :, width:])
    far_feats = second[:, :, :width].transpose(1, 0, 2).reshape(rows, width)
    picked, far_feats = lax.optimization_barrier((picked, far_feats))
    far_cot = exchange(picked)
    far_qkv, far_t = project(far_feats, own, 0, (), "project_far")
    far_blk = far_qkv.reshape(own, bs, 3 * width)
    peer_cot = swap(cot_out)

    far_k_spec = pl.BlockSpec((1, bs, width), lambda i, *s: (i, 0, 1))
    far_v_spec = pl.BlockSpec((1, bs, width), lambda i, *s: (i, 0, 2))
    far_kt_spec = pl.BlockSpec((1, width, bs), row_step)
    far_vt_spec = pl.BlockSpec((1, width, bs), lambda i, *s: (i, 1, 0))
    att, stats, slots = call(
        merge_kernel, 1, own,
        [rows_spec, rows_spec, far_k_spec, far_vt_spec, pl.BlockSpec((1, width, bs), row_step),
         pl.BlockSpec((1, 2 * H, bs), row_step)],
        [rows_spec, stats_spec, pl.BlockSpec((1, STATS, bs), lambda i, meta: (meta[1 + i], 0, 0))],
        [
            jax.ShapeDtypeStruct((rows, width), BF16),
            jax.ShapeDtypeStruct((own, STATS, bs), F32),
            jax.ShapeDtypeStruct((devices, STATS, bs), F32),
        ],
        [], own * 4 * pair_flops, 6 << 20, "far_forward",
    )(meta, part_qkv, cot, far_blk, far_t, near_out, sums)
    far_cot, slots, stats = lax.optimization_barrier((far_cot, slots, stats))
    peer_stats = swap(stats)
    far_slots = exchange(slots)
    pairs = width // LANES
    dq, acc = call(
        own_kernel, 2, own,
        [rows_spec, rows_spec, tile_spec, stats_spec, k_spec, v_spec, kt_spec, far_k_spec, far_v_spec, far_kt_spec],
        [rows_spec, pl.BlockSpec((own, bs, 2 * width), lambda i, *s: (0, 0, 0))],
        [jax.ShapeDtypeStruct((rows, width), BF16), jax.ShapeDtypeStruct((own, bs, 2 * width), F32)],
        [
            pltpu.VMEM((pairs, NBR * bs, 2 * bs), BF16),
            pltpu.VMEM((pairs, NBR * bs, 2 * bs), BF16),
            pltpu.VMEM((pairs, 2 * bs, LANES), BF16),
            pltpu.VMEM((pairs, 2 * bs, LANES), BF16),
            pltpu.VMEM((NBR, bs, 2 * bs), F32),
        ],
        own * 24 * pair_flops, 30 << 20, "own_backward",
    )(near_ids, meta, part_qkv, cot, tiles, stats, part_blk, part_blk, part_t, far_blk, far_blk, far_t)
    acc, peer_stats, peer_cot = lax.optimization_barrier((acc, peer_stats, peer_cot))
    far_cot = far_cot.transpose(1, 0, 2).reshape(rows, width)

    layer_out = jnp.dot(att, w_out, preferred_element_type=F32).astype(BF16)
    dwo_t = jnp.einsum("rc,ra->ca", layer_cot, att, preferred_element_type=F32).astype(BF16)
    dwq = jnp.einsum("rd,rc->dc", node_feats, dq, preferred_element_type=F32).astype(BF16)

    (acc,) = call(
        peer_kernel, 2, own,
        [
            pl.BlockSpec((bs, width), lambda i, *s: (own + i, 0)),
            pl.BlockSpec((bs, width), step),
            pl.BlockSpec((1, STATS, bs), lambda i, *s: (i, 0, 0)),
            pl.BlockSpec((1, NBR, bs, bs), lambda i, ids, meta: (own - meta[0] + i, 0, 0, 0)),
            pl.BlockSpec((own, bs, width), lambda i, *s: (0, 0, 1), pipeline_mode=pl.Buffered(1)),
            pl.BlockSpec((own, bs, width), lambda i, *s: (0, 0, 2), pipeline_mode=pl.Buffered(1)),
            once((own, bs, 2 * width)),
        ],
        [pl.BlockSpec((own, bs, 2 * width), lambda i, *s: (0, 0, 0))],
        [jax.ShapeDtypeStruct((own, bs, 2 * width), F32)],
        [
            pltpu.VMEM((width // LANES, 2 * bs, LANES), BF16),
            pltpu.VMEM((width // LANES, 2 * bs, LANES), BF16),
        ],
        own * 16 * pair_flops, 20 << 20, "peer_queries",
    )(near_ids, meta, part_qkv, peer_cot, peer_stats, tiles, part_blk, part_blk, acc)

    (dkv,) = call(
        far_kernel, 1, own,
        [
            pl.BlockSpec((bs, width), step),
            pl.BlockSpec((bs, width), step),
            pl.BlockSpec((1, STATS, bs), lambda i, meta: (meta[1 + i], 0, 0)),
            pl.BlockSpec((1, bs, width), lambda i, *s: (i, 0, 1)),
            pl.BlockSpec((1, bs, width), lambda i, *s: (i, 0, 2)),
            pl.BlockSpec((1, bs, 2 * width), lambda i, *s: (i, 0, 0)),
        ],
        [pl.BlockSpec((bs, 2 * width), step)],
        [jax.ShapeDtypeStruct((rows, 2 * width), BF16)],
        [], own * 8 * pair_flops, 10 << 20, "far_queries",
    )(meta, far_qkv, far_cot, far_slots, part_blk, part_blk, acc)

    dwkv = jnp.einsum("rd,rc->dc", node_feats, dkv, preferred_element_type=F32).astype(BF16)
    parts = [w.reshape(doms, width // doms, width) for w in (dwo_t, dwq, dwkv[:, :width], dwkv[:, width:])]
    split = jnp.stack(
        [jnp.concatenate([w[:, :, g * span : (g + 1) * span] for w in parts], axis=2) for g in range(groups)], axis=1
    )
    moved = exchange(split.reshape(devices, width // doms, 4 * span))
    summed = jnp.sum(moved.astype(F32), axis=0)
    w_plain = w_by.transpose(1, 0, 2).reshape(width, 3 * width)
    feat_grad = (
        lax.dot_general(dq, w_plain[:, :width], (((1,), (1,)), ((), ())), preferred_element_type=F32)
        + lax.dot_general(dkv, w_plain[:, width:], (((1,), (1,)), ((), ())), preferred_element_type=F32)
    ).astype(BF16)
    dw_out = summed[:, :span].T
    dw_qkv = summed[:, span:]
    return (layer_out, feat_grad, dw_qkv, dw_out)


def solution(mesh):
    placed = (
        P(DEVICES, None),
        P(),
        P(),
        P("dom", None),
        P("dom", None, None, None),
        P("dom"),
        P(DEVICES, None),
    )
    return jax.shard_map(
        body,
        mesh=mesh,
        in_specs=placed,
        out_specs=(P(DEVICES, None), P(DEVICES, None), P("dom", "head"), P("head", "dom")),
        check_vma=False,
    )
```

```python
import jax
import jax.numpy as jnp
from jax import lax
from jax.experimental import pallas as pl
from jax.experimental.pallas import tpu as pltpu
from jax.sharding import PartitionSpec as P

H = 8
NBR = 4
DEVICES = ("dom", "head")
F32, BF16 = jnp.float32, jnp.bfloat16
NEG = -1e30
LANES = 128
STATS = 3 * H
DIGIT = 32
VMEM_LIMIT = 58 * 1024 * 1024


def nn(a, b):
    return jnp.dot(a, b, preferred_element_type=F32)


def nt(a, b):
    return lax.dot_general(a, b, (((1,), (1,)), ((), ())), preferred_element_type=F32)


def two_heads(pair):
    lane = lax.broadcasted_iota(jnp.int32, pair.shape, 1)
    zero = jnp.zeros_like(pair)
    return jnp.concatenate(
        [jnp.where(lane < LANES // 2, pair, zero), jnp.where(lane >= LANES // 2, pair, zero)], axis=0
    )


def own_heads(both):
    half, rows = both.shape[0] // 2, both.shape[1] // 2
    return jnp.concatenate([both[:half, :rows], both[half:, rows:]], axis=0)


def bias_of(tile):
    bias = jnp.where(tile != 0, 0.0, NEG).astype(F32).T
    return jnp.concatenate([bias, bias], axis=1)


def split_stat(row):
    return row[:, : row.shape[1] // 2], row[:, row.shape[1] // 2 :]


def near_kernel(near_ids, meta, q_ref, tile_ref, k_ref, vt_ref, out_ref, sums_ref, bias_scr):
    i = pl.program_id(0)
    for j in range(NBR):
        bias_scr[j] = bias_of(tile_ref[0, j])
    ids = [near_ids[i, j] for j in range(NBR)]
    pairs = q_ref.shape[1] // LANES

    def scores_of(c):
        cols = slice(c * LANES, (c + 1) * LANES)
        qz = two_heads(q_ref[:, cols])
        return jnp.concatenate([nt(k_ref[ids[j], :, cols], qz) + bias_scr[j] for j in range(NBR)], axis=0)

    ready = scores_of(0)
    for c in range(pairs):
        cols = slice(c * LANES, (c + 1) * LANES)
        scores, ready = ready, scores_of(c + 1) if c + 1 < pairs else None
        peak = jnp.max(scores, axis=0, keepdims=True)
        terms = jnp.exp(scores - peak)
        total = jnp.sum(terms, axis=0, keepdims=True)
        vt = jnp.concatenate([vt_ref[ids[j], cols, :] for j in range(NBR)], axis=1)
        out_ref[0, cols, :] = own_heads(nn(vt, terms.astype(BF16)))
        store_rows(sums_ref, c, (peak, total))


def store_rows(ref, c, rows):
    for s, row in enumerate(rows):
        for e, part in enumerate(split_stat(row)):
            at = s * H + 2 * c + e
            ref[0, at : at + 1, :] = part


def merge_kernel(meta, q_ref, cot_ref, fk_ref, fvt_ref, out_ref, sums_ref, att_ref, stats_ref, slot_ref):
    mid = LANES // 2
    pairs = q_ref.shape[1] // LANES
    cols = [slice(c * LANES, (c + 1) * LANES) for c in range(pairs)]
    scores = [nt(fk_ref[0, :, cols[c]], two_heads(q_ref[:, cols[c]])) for c in range(pairs)]
    turned_cot = [cot_ref[:, cols[c]].astype(F32).T for c in range(pairs)]
    peaks, kepts, invs, lows = [], [], [], []
    for c in range(pairs):
        near_peak, near_total = load_rows(sums_ref, c, 2)
        peak = jnp.maximum(near_peak, jnp.max(scores[c], axis=0, keepdims=True))
        terms = jnp.exp(scores[c] - peak)
        kept = jnp.exp(near_peak - peak)
        inv = 1.0 / (near_total * kept + jnp.sum(terms, axis=0, keepdims=True))
        lows.append((terms * inv).astype(BF16))
        peaks.append(peak)
        kepts.append(kept)
        invs.append(inv)
    far_outs = [own_heads(nn(fvt_ref[0, cols[c], :], lows[c])) for c in range(pairs)]
    atts = []
    for c in range(pairs):
        first, second = split_stat(kepts[c] * invs[c])
        near_out = out_ref[0, cols[c], :]
        near_out = jnp.concatenate([near_out[:mid] * first, near_out[mid:] * second], axis=0)
        atts.append((far_outs[c] + near_out).astype(BF16).astype(F32))
    for c in range(pairs):
        att_ref[:, cols[c]] = atts[c].T.astype(BF16)
        prod = turned_cot[c] * atts[c]
        delta = jnp.concatenate(
            [jnp.sum(prod[:mid], axis=0, keepdims=True), jnp.sum(prod[mid:], axis=0, keepdims=True)], axis=1
        )
        store_rows(stats_ref, c, (peaks[c], invs[c], delta))
        store_rows(slot_ref, c, (peaks[c], invs[c], delta))


def own_kernel(near_ids, meta, q_ref, cot_ref, tile_ref, stats_ref, k_ref, v_ref, kt_ref, fk_ref, fv_ref, fkt_ref,
               dq_ref, acc_ref, p_scr, ds_scr, qz_scr, cz_scr, bias_scr):
    i = pl.program_id(0)
    bs, width = q_ref.shape
    pairs = width // LANES
    own = acc_ref.shape[0]

    @pl.when(i == 0)
    def _():
        acc_ref[...] = jnp.zeros_like(acc_ref)

    for j in range(NBR):
        bias_scr[j] = bias_of(tile_ref[0, j])
    ids = [near_ids[i, j] for j in range(NBR)]
    for c in range(pairs):
        cols = slice(c * LANES, (c + 1) * LANES)
        qz = two_heads(q_ref[:, cols])
        cz = two_heads(cot_ref[:, cols])
        qz_scr[c] = qz
        cz_scr[c] = cz
        peak, inv, delta = load_rows(stats_ref, c, 3)
        parts = []
        for j in range(NBR + 1):
            if j < NBR:
                scores = nt(k_ref[ids[j], :, cols], qz) + bias_scr[j]
                grad_probs = nt(v_ref[ids[j], :, cols], cz)
            else:
                scores = nt(fk_ref[0, :, cols], qz)
                grad_probs = nt(fv_ref[0, :, cols], cz)
            probs = jnp.exp(scores - peak) * inv
            parts.append((probs * (grad_probs - delta)).astype(BF16))
            if j < NBR:
                rows = slice(j * bs, (j + 1) * bs)
                p_scr[c, rows, :] = probs.astype(BF16)
                ds_scr[c, rows, :] = parts[j]
        kt = jnp.concatenate([kt_ref[ids[j], cols, :] for j in range(NBR)] + [fkt_ref[0, cols, :]], axis=1)
        dq = own_heads(nn(kt, jnp.concatenate(parts, axis=0))) * 0.125
        dq_ref[:, cols] = dq.T.astype(BF16)

    for j in range(NBR):

        @pl.when(ids[j] < own)
        def _(j=j):
            n = ids[j]
            for c in range(pairs):
                cols = slice(c * LANES, (c + 1) * LANES)
                vcols = slice(width + c * LANES, width + (c + 1) * LANES)
                rows = slice(j * bs, (j + 1) * bs)
                acc_ref[n, :, cols] += nn(ds_scr[c, rows, :], qz_scr[c])
                acc_ref[n, :, vcols] += nn(p_scr[c, rows, :], cz_scr[c])


def load_rows(ref, c, count):
    return [
        jnp.concatenate(
            [ref[0, s * H + 2 * c : s * H + 2 * c + 1, :], ref[0, s * H + 2 * c + 1 : s * H + 2 * c + 2, :]], axis=1
        )
        for s in range(count)
    ]


def key_terms(ks, vs, qzs, czs, bias, stats):
    scores = [nt(k, qz) for k, qz in zip(ks, qzs)]
    grads = [nt(v, cz) for v, cz in zip(vs, czs)]
    probs = [
        jnp.exp((s if bias is None else s + bias) - peak) * inv for s, (peak, inv, _) in zip(scores, stats)
    ]
    ds = [(p * (g - delta)).astype(BF16) for p, g, (_, _, delta) in zip(probs, grads, stats)]
    return [nn(d, qz) for d, qz in zip(ds, qzs)], [nn(p.astype(BF16), cz) for p, cz in zip(probs, czs)]


def peer_kernel(near_ids, meta, q_ref, cot_ref, stats_ref, tile_ref, k_ref, v_ref, acc_in, acc_ref, qz_scr, cz_scr):
    i = pl.program_id(0)
    pairs = q_ref.shape[1] // LANES
    width = q_ref.shape[1]
    own = acc_ref.shape[0]

    @pl.when(i == 0)
    def _():
        acc_ref[...] = acc_in[...]

    for c in range(pairs):
        cols = slice(c * LANES, (c + 1) * LANES)
        qz_scr[c] = two_heads(q_ref[:, cols])
        cz_scr[c] = two_heads(cot_ref[:, cols])
    for j in range(NBR):
        n = near_ids[own + i, j]

        @pl.when(n < own)
        def _(j=j, n=n):
            every = range(pairs)
            cols = [slice(c * LANES, (c + 1) * LANES) for c in every]
            dks, dvs = key_terms(
                [k_ref[n, :, cols[c]] for c in every], [v_ref[n, :, cols[c]] for c in every],
                [qz_scr[c] for c in every], [cz_scr[c] for c in every], bias_of(tile_ref[0, j]),
                [load_rows(stats_ref, c, 3) for c in every],
            )
            for c in every:
                acc_ref[n, :, cols[c]] += dks[c]
                acc_ref[n, :, width + c * LANES : width + (c + 1) * LANES] += dvs[c]


def far_kernel(meta, q_ref, cot_ref, stats_ref, k_ref, v_ref, acc_ref, dkv_ref):
    width = q_ref.shape[1]
    every = range(width // LANES)
    cols = [slice(c * LANES, (c + 1) * LANES) for c in every]
    dks, dvs = key_terms(
        [k_ref[0, :, cols[c]] for c in every], [v_ref[0, :, cols[c]] for c in every],
        [two_heads(q_ref[:, cols[c]]) for c in every], [two_heads(cot_ref[:, cols[c]]) for c in every], None,
        [load_rows(stats_ref, c, 3) for c in every],
    )
    for c in every:
        vcols = slice(width + c * LANES, width + (c + 1) * LANES)
        dkv_ref[:, cols[c]] = (acc_ref[0, :, cols[c]] + dks[c].astype(BF16).astype(F32)).astype(BF16)
        dkv_ref[:, vcols] = (acc_ref[0, :, vcols] + dvs[c].astype(BF16).astype(F32)).astype(BF16)


def project_kernel(x_ref, w_ref, wt_ref, *rest):
    qkv_ref, t_ref = rest[-2:]
    bs = t_ref.shape[2]
    qkv_ref[...] = nn(x_ref[...], w_ref[...]).astype(BF16)
    turned = nt(wt_ref[...], x_ref[...]).astype(BF16)
    for b in range(t_ref.shape[0]):
        t_ref[b] = turned[:, b * bs : (b + 1) * bs]


def call(kernel, scalars, steps, in_specs, out_specs, out_shape, scratch, flops, touched, name, aliases={}):
    return pl.pallas_call(
        kernel,
        grid_spec=pltpu.PrefetchScalarGridSpec(
            num_scalar_prefetch=scalars, grid=(steps,), in_specs=in_specs, out_specs=out_specs, scratch_shapes=scratch
        ),
        out_shape=out_shape,
        input_output_aliases=aliases,
        compiler_params=pltpu.CompilerParams(dimension_semantics=("arbitrary",), vmem_limit_bytes=VMEM_LIMIT),
        cost_estimate=pl.CostEstimate(flops=flops, bytes_accessed=touched, transcendentals=0),
        name=name,
    )


def once(shape, at=0):
    return pl.BlockSpec(shape, lambda i, *s: (at,) + (0,) * (len(shape) - 1), pipeline_mode=pl.Buffered(1))


def body(node_feats, w_qkv, w_out, neighbours, tiles, partner, layer_cot):
    rows, width = node_feats.shape
    doms, groups = lax.axis_size("dom"), lax.axis_size("head")
    devices = doms * groups
    blocks = partner.shape[0]
    own = blocks // groups
    bs = tiles.shape[2]
    span = width // groups
    half = lax.axis_index("head")
    base = half * own

    near_ids = jnp.roll((neighbours - base) % blocks, -base, axis=0)
    mine = lax.dynamic_slice_in_dim(partner, base, own, 0)
    meta = jnp.concatenate([base[None].astype(jnp.int32), mine // own])

    w_by = w_qkv.reshape(width, groups, 3, span).transpose(2, 0, 1, 3).reshape(3, width, width)
    w_all = jnp.concatenate([w_by[0] * jnp.asarray(0.125, BF16), w_by[1], w_by[2]], axis=1)

    def swap(x):
        return lax.ppermute(x, "head", [(0, 1), (1, 0)])

    def exchange(x):
        return lax.all_to_all(x, DEVICES, split_axis=0, concat_axis=0, tiled=True)

    def spread(x):
        return x.reshape(own, bs, width).transpose(1, 0, 2)

    def gathered(x):
        return jnp.dot(one_hot, x.reshape(-1, width), preferred_element_type=F32).astype(BF16).reshape(
            devices, own, width
        )

    digits = jnp.stack([mine // DIGIT, mine % DIGIT], axis=1).astype(BF16)
    digits = jnp.pad(digits, ((0, 0), (0, LANES - 2)))
    digits = jnp.broadcast_to(digits[None], (devices, own, LANES))
    first_hop = jnp.concatenate([spread(node_feats), digits], axis=2)
    rows_in = exchange(first_hop)
    peer_feats = swap(node_feats)
    cot = jnp.dot(layer_cot, w_out.T, preferred_element_type=F32).astype(BF16)
    cot_rows = spread(cot)

    w_turned = w_all[:, width:].T
    hold = pl.BlockSpec(memory_space=pl.ANY)

    def project(feats, total, at, carried, name):
        per = 2
        return call(
            project_kernel, 0, own // per,
            [
                pl.BlockSpec((per * bs, width), lambda i: (i, 0)),
                once((width, 3 * width)),
                once((2 * width, width)),
            ]
            + [hold] * len(carried),
            [
                pl.BlockSpec((per * bs, 3 * width), lambda i: (at // per + i, 0)),
                pl.BlockSpec((per, 2 * width, bs), lambda i: (at // per + i, 0, 0)),
            ],
            [
                jax.ShapeDtypeStruct((total * bs, 3 * width), BF16),
                jax.ShapeDtypeStruct((total, 2 * width, bs), BF16),
            ],
            [], 2 * rows * width * 5 * width, 8 << 20, name, aliases={3: 0, 4: 1} if carried else {},
        )(feats, w_all, w_turned, *carried)

    own_part = project(node_feats, blocks, 0, (), "project_own")
    rows_in, cot_rows, own_part, peer_feats = lax.optimization_barrier((rows_in, cot_rows, own_part, peer_feats))

    weigh = jnp.pad(jnp.asarray([DIGIT, 1], F32), (0, LANES - 2))
    ids = jnp.sum(rows_in.reshape(-1, width + LANES)[:, width:].astype(F32) * weigh[None], axis=1, keepdims=True)
    one_hot = (ids == jnp.arange(ids.shape[0], dtype=jnp.int32)[None, :].astype(F32)).astype(BF16)
    second = jnp.concatenate([gathered(rows_in[:, :, :width]), cot_rows], axis=2)
    second = exchange(second)
    part_qkv, part_t = project(peer_feats, blocks, own, own_part, "project_peer")
    part_blk = part_qkv.reshape(blocks, bs, 3 * width)
    pair_flops = 2 * bs * bs * width * 2
    step = lambda i, *s: (i, 0)
    row_step = lambda i, *s: (i, 0, 0)
    rows_spec = pl.BlockSpec((bs, width), step)
    tile_spec = pl.BlockSpec((1, NBR, bs, bs), lambda i, ids, meta: (meta[0] + i, 0, 0, 0))
    k_spec = pl.BlockSpec((blocks, bs, width), lambda i, *s: (0, 0, 1), pipeline_mode=pl.Buffered(1))
    v_spec = pl.BlockSpec((blocks, bs, width), lambda i, *s: (0, 0, 2), pipeline_mode=pl.Buffered(1))
    kt_spec = pl.BlockSpec((blocks, width, bs), lambda i, *s: (0, 0, 0), pipeline_mode=pl.Buffered(1))
    vt_spec = pl.BlockSpec((blocks, width, bs), lambda i, *s: (0, 1, 0), pipeline_mode=pl.Buffered(1))
    stats_spec = pl.BlockSpec((1, STATS, bs), row_step)
    near_out, sums = call(
        near_kernel, 2, own,
        [rows_spec, tile_spec, k_spec, vt_spec],
        [pl.BlockSpec((1, width, bs), row_step), pl.BlockSpec((1, 2 * H, bs), row_step)],
        [jax.ShapeDtypeStruct((own, width, bs), F32), jax.ShapeDtypeStruct((own, 2 * H, bs), F32)],
        [pltpu.VMEM((NBR, bs, 2 * bs), F32)],
        own * 16 * pair_flops, 10 << 20, "near_forward",
    )(near_ids, meta, part_qkv, tiles, part_blk, part_t)
    second, near_out, sums, cot_out = lax.optimization_barrier((second, near_out, sums, cot))

    picked = gathered(second[:, :, width:])
    far_feats = second[:, :, :width].transpose(1, 0, 2).reshape(rows, width)
    picked, far_feats = lax.optimization_barrier((picked, far_feats))
    far_cot = exchange(picked)
    far_qkv, far_t = project(far_feats, own, 0, (), "project_far")
    far_blk = far_qkv.reshape(own, bs, 3 * width)
    peer_cot = swap(cot_out)

    far_k_spec = pl.BlockSpec((1, bs, width), lambda i, *s: (i, 0, 1))
    far_v_spec = pl.BlockSpec((1, bs, width), lambda i, *s: (i, 0, 2))
    far_kt_spec = pl.BlockSpec((1, width, bs), row_step)
    far_vt_spec = pl.BlockSpec((1, width, bs), lambda i, *s: (i, 1, 0))
    att, stats, slots = call(
        merge_kernel, 1, own,
        [rows_spec, rows_spec, far_k_spec, far_vt_spec, pl.BlockSpec((1, width, bs), row_step),
         pl.BlockSpec((1, 2 * H, bs), row_step)],
        [rows_spec, stats_spec, pl.BlockSpec((1, STATS, bs), lambda i, meta: (meta[1 + i], 0, 0))],
        [
            jax.ShapeDtypeStruct((rows, width), BF16),
            jax.ShapeDtypeStruct((own, STATS, bs), F32),
            jax.ShapeDtypeStruct((devices, STATS, bs), F32),
        ],
        [], own * 4 * pair_flops, 6 << 20, "far_forward",
    )(meta, part_qkv, cot, far_blk, far_t, near_out, sums)
    peer_stats = swap(stats)
    pairs = width // LANES
    dq, acc = call(
        own_kernel, 2, own,
        [rows_spec, rows_spec, tile_spec, stats_spec, k_spec, v_spec, kt_spec, far_k_spec, far_v_spec, far_kt_spec],
        [rows_spec, pl.BlockSpec((own, bs, 2 * width), lambda i, *s: (0, 0, 0))],
        [jax.ShapeDtypeStruct((rows, width), BF16), jax.ShapeDtypeStruct((own, bs, 2 * width), F32)],
        [
            pltpu.VMEM((pairs, NBR * bs, 2 * bs), BF16),
            pltpu.VMEM((pairs, NBR * bs, 2 * bs), BF16),
            pltpu.VMEM((pairs, 2 * bs, LANES), BF16),
            pltpu.VMEM((pairs, 2 * bs, LANES), BF16),
            pltpu.VMEM((NBR, bs, 2 * bs), F32),
        ],
        own * 24 * pair_flops, 30 << 20, "own_backward",
    )(near_ids, meta, part_qkv, cot, tiles, stats, part_blk, part_blk, part_t, far_blk, far_blk, far_t)
    acc, peer_stats, peer_cot, far_cot, slots = lax.optimization_barrier((acc, peer_stats, peer_cot, far_cot, slots))
    far_slots = exchange(slots)
    far_cot = far_cot.transpose(1, 0, 2).reshape(rows, width)

    layer_out = jnp.dot(att, w_out, preferred_element_type=F32).astype(BF16)
    dwo_t = jnp.einsum("rc,ra->ca", layer_cot, att, preferred_element_type=F32).astype(BF16)
    dwq = jnp.einsum("rd,rc->dc", node_feats, dq, preferred_element_type=F32).astype(BF16)

    (acc,) = call(
        peer_kernel, 2, own,
        [
            pl.BlockSpec((bs, width), lambda i, *s: (own + i, 0)),
            pl.BlockSpec((bs, width), step),
            pl.BlockSpec((1, STATS, bs), lambda i, *s: (i, 0, 0)),
            pl.BlockSpec((1, NBR, bs, bs), lambda i, ids, meta: (own - meta[0] + i, 0, 0, 0)),
            pl.BlockSpec((own, bs, width), lambda i, *s: (0, 0, 1), pipeline_mode=pl.Buffered(1)),
            pl.BlockSpec((own, bs, width), lambda i, *s: (0, 0, 2), pipeline_mode=pl.Buffered(1)),
            once((own, bs, 2 * width)),
        ],
        [pl.BlockSpec((own, bs, 2 * width), lambda i, *s: (0, 0, 0))],
        [jax.ShapeDtypeStruct((own, bs, 2 * width), F32)],
        [
            pltpu.VMEM((width // LANES, 2 * bs, LANES), BF16),
            pltpu.VMEM((width // LANES, 2 * bs, LANES), BF16),
        ],
        own * 16 * pair_flops, 20 << 20, "peer_queries",
    )(near_ids, meta, part_qkv, peer_cot, peer_stats, tiles, part_blk, part_blk, acc)

    (dkv,) = call(
        far_kernel, 1, own,
        [
            pl.BlockSpec((bs, width), step),
            pl.BlockSpec((bs, width), step),
            pl.BlockSpec((1, STATS, bs), lambda i, meta: (meta[1 + i], 0, 0)),
            pl.BlockSpec((1, bs, width), lambda i, *s: (i, 0, 1)),
            pl.BlockSpec((1, bs, width), lambda i, *s: (i, 0, 2)),
            pl.BlockSpec((1, bs, 2 * width), lambda i, *s: (i, 0, 0)),
        ],
        [pl.BlockSpec((bs, 2 * width), step)],
        [jax.ShapeDtypeStruct((rows, 2 * width), BF16)],
        [], own * 8 * pair_flops, 10 << 20, "far_queries",
    )(meta, far_qkv, far_cot, far_slots, part_blk, part_blk, acc)

    dwkv = jnp.einsum("rd,rc->dc", node_feats, dkv, preferred_element_type=F32).astype(BF16)
    parts = [w.reshape(doms, width // doms, width) for w in (dwo_t, dwq, dwkv[:, :width], dwkv[:, width:])]
    split = jnp.stack(
        [jnp.concatenate([w[:, :, g * span : (g + 1) * span] for w in parts], axis=2) for g in range(groups)], axis=1
    )
    moved = exchange(split.reshape(devices, width // doms, 4 * span))
    summed = jnp.sum(moved.astype(F32), axis=0)
    w_plain = w_by.transpose(1, 0, 2).reshape(width, 3 * width)
    feat_grad = (
        lax.dot_general(dq, w_plain[:, :width], (((1,), (1,)), ((), ())), preferred_element_type=F32)
        + lax.dot_general(dkv, w_plain[:, width:], (((1,), (1,)), ((), ())), preferred_element_type=F32)
    ).astype(BF16)
    dw_out = summed[:, :span].T
    dw_qkv = summed[:, span:]
    return (layer_out, feat_grad, dw_qkv, dw_out)


def solution(mesh):
    placed = (
        P(DEVICES, None),
        P(),
        P(),
        P("dom", None),
        P("dom", None, None, None),
        P("dom"),
        P(DEVICES, None),
    )
    return jax.shard_map(
        body,
        mesh=mesh,
        in_specs=placed,
        out_specs=(P(DEVICES, None), P(DEVICES, None), P("dom", "head"), P("head", "dom")),
        check_vma=False,
    )
```

```python
import jax
import jax.numpy as jnp
from jax import lax
from jax.experimental import pallas as pl
from jax.experimental.pallas import tpu as pltpu
from jax.sharding import PartitionSpec as P

H = 8
NBR = 4
DEVICES = ("dom", "head")
F32, BF16 = jnp.float32, jnp.bfloat16
NEG = -1e30
LANES = 128
STATS = 3 * H
DIGIT = 32
VMEM_LIMIT = 58 * 1024 * 1024


def nn(a, b):
    return jnp.dot(a, b, preferred_element_type=F32)


def nt(a, b):
    return lax.dot_general(a, b, (((1,), (1,)), ((), ())), preferred_element_type=F32)


def two_heads(pair):
    lane = lax.broadcasted_iota(jnp.int32, pair.shape, 1)
    zero = jnp.zeros_like(pair)
    return jnp.concatenate(
        [jnp.where(lane < LANES // 2, pair, zero), jnp.where(lane >= LANES // 2, pair, zero)], axis=0
    )


def own_heads(both):
    half, rows = both.shape[0] // 2, both.shape[1] // 2
    return jnp.concatenate([both[:half, :rows], both[half:, rows:]], axis=0)


def bias_of(tile):
    bias = jnp.where(tile != 0, 0.0, NEG).astype(F32).T
    return jnp.concatenate([bias, bias], axis=1)


def split_stat(row):
    return row[:, : row.shape[1] // 2], row[:, row.shape[1] // 2 :]


def near_kernel(near_ids, meta, q_ref, tile_ref, k_ref, vt_ref, out_ref, sums_ref, bias_scr):
    i = pl.program_id(0)
    for j in range(NBR):
        bias_scr[j] = bias_of(tile_ref[0, j])
    ids = [near_ids[i, j] for j in range(NBR)]
    pairs = q_ref.shape[1] // LANES

    def scores_of(c):
        cols = slice(c * LANES, (c + 1) * LANES)
        qz = two_heads(q_ref[:, cols])
        keys = jnp.concatenate([k_ref[ids[j], :, cols] for j in range(NBR)], axis=0)
        return nt(keys, qz) + bias_scr[...].reshape(keys.shape[0], qz.shape[0])

    ready = scores_of(0)
    for c in range(pairs):
        cols = slice(c * LANES, (c + 1) * LANES)
        scores, ready = ready, scores_of(c + 1) if c + 1 < pairs else None
        peak = jnp.max(scores, axis=0, keepdims=True)
        terms = jnp.exp(scores - peak)
        total = jnp.sum(terms, axis=0, keepdims=True)
        vt = jnp.concatenate([vt_ref[ids[j], cols, :] for j in range(NBR)], axis=1)
        out_ref[0, cols, :] = own_heads(nn(vt, terms.astype(BF16)))
        store_rows(sums_ref, c, (peak, total))


def store_rows(ref, c, rows):
    for s, row in enumerate(rows):
        for e, part in enumerate(split_stat(row)):
            at = s * H + 2 * c + e
            ref[0, at : at + 1, :] = part


def merge_kernel(meta, q_ref, cot_t_ref, fk_ref, fvt_ref, out_ref, sums_ref, att_ref, stats_ref, slot_ref):
    mid = LANES // 2
    pairs = q_ref.shape[1] // LANES
    cols = [slice(c * LANES, (c + 1) * LANES) for c in range(pairs)]
    scores = [nt(fk_ref[0, :, cols[c]], two_heads(q_ref[:, cols[c]])) for c in range(pairs)]
    peaks, kepts, invs, lows = [], [], [], []
    for c in range(pairs):
        near_peak, near_total = load_rows(sums_ref, c, 2)
        peak = jnp.maximum(near_peak, jnp.max(scores[c], axis=0, keepdims=True))
        terms = jnp.exp(scores[c] - peak)
        kept = jnp.exp(near_peak - peak)
        inv = 1.0 / (near_total * kept + jnp.sum(terms, axis=0, keepdims=True))
        lows.append((terms * inv).astype(BF16))
        peaks.append(peak)
        kepts.append(kept)
        invs.append(inv)
    far_outs = [own_heads(nn(fvt_ref[0, cols[c], :], lows[c])) for c in range(pairs)]
    atts = []
    for c in range(pairs):
        first, second = split_stat(kepts[c] * invs[c])
        near_out = out_ref[0, cols[c], :]
        near_out = jnp.concatenate([near_out[:mid] * first, near_out[mid:] * second], axis=0)
        atts.append((far_outs[c] + near_out).astype(BF16).astype(F32))
    for c in range(pairs):
        att_ref[0, cols[c], :] = atts[c].astype(BF16)
        prod = cot_t_ref[0, cols[c], :].astype(F32) * atts[c]
        delta = jnp.concatenate(
            [jnp.sum(prod[:mid], axis=0, keepdims=True), jnp.sum(prod[mid:], axis=0, keepdims=True)], axis=1
        )
        store_rows(stats_ref, c, (peaks[c], invs[c], delta))
        store_rows(slot_ref, c, (peaks[c], invs[c], delta))


def deal(dw_scr, kept_ref, given_ref, core):
    groups, span = kept_ref.shape[0], kept_ref.shape[3] // 2
    for g in range(groups):
        for t in range(2):
            at = (t * groups + g) * span
            kept_ref[g, :, :, t * span : (t + 1) * span] = dw_scr[:, core, :, at : at + span]
            given_ref[g, :, :, t * span : (t + 1) * span] = dw_scr[:, 1 - core, :, at : at + span]


def own_kernel(near_ids, meta, q_ref, cot_ref, tile_ref, stats_ref, k_ref, v_ref, kt_ref, fk_ref, fv_ref, fkt_ref,
               xt_ref, ct_ref, att_ref, dq_ref, acc_ref, kept_ref, given_ref, p_scr, ds_scr, qz_scr, cz_scr, bias_scr,
               dw_scr):
    i = pl.program_id(0)
    bs, width = q_ref.shape
    pairs = width // LANES
    own = acc_ref.shape[0]

    @pl.when(i == 0)
    def _():
        acc_ref[...] = jnp.zeros_like(acc_ref)
        dw_scr[...] = jnp.zeros_like(dw_scr)

    for j in range(NBR):
        bias_scr[j] = bias_of(tile_ref[0, j])
    ids = [near_ids[i, j] for j in range(NBR)]
    for c in range(pairs):
        cols = slice(c * LANES, (c + 1) * LANES)
        qz = two_heads(q_ref[:, cols])
        cz = two_heads(cot_ref[:, cols])
        qz_scr[c] = qz
        cz_scr[c] = cz
        peak, inv, delta = load_rows(stats_ref, c, 3)
        keys = jnp.concatenate([k_ref[ids[j], :, cols] for j in range(NBR)] + [fk_ref[0, :, cols]], axis=0)
        values = jnp.concatenate([v_ref[ids[j], :, cols] for j in range(NBR)] + [fv_ref[0, :, cols]], axis=0)
        all_scores = nt(keys, qz)
        all_grads = nt(values, cz)
        parts = []
        for j in range(NBR + 1):
            rows = slice(j * bs, (j + 1) * bs)
            scores = all_scores[rows] + bias_scr[j] if j < NBR else all_scores[rows]
            probs = jnp.exp(scores - peak) * inv
            parts.append((probs * (all_grads[rows] - delta)).astype(BF16))
            if j < NBR:
                p_scr[c, rows, :] = probs.astype(BF16)
                ds_scr[c, rows, :] = parts[j]
        kt = jnp.concatenate([kt_ref[ids[j], cols, :] for j in range(NBR)] + [fkt_ref[0, cols, :]], axis=1)
        dq_ref[0, cols, :] = (own_heads(nn(kt, jnp.concatenate(parts, axis=0))) * 0.125).astype(BF16)
    half = dw_scr.shape[:3] + (width,)
    dw_scr[:, :, :, :width] += nt(ct_ref[0], att_ref[0]).reshape(half)
    dw_scr[:, :, :, width:] += nt(xt_ref[0], dq_ref[0]).reshape(half)

    for j in range(NBR):

        @pl.when(ids[j] < own)
        def _(j=j):
            n = ids[j]
            for c in range(pairs):
                cols = slice(c * LANES, (c + 1) * LANES)
                vcols = slice(width + c * LANES, width + (c + 1) * LANES)
                rows = slice(j * bs, (j + 1) * bs)
                acc_ref[n, :, cols] += nn(ds_scr[c, rows, :], qz_scr[c])
                acc_ref[n, :, vcols] += nn(p_scr[c, rows, :], cz_scr[c])

    @pl.when(i == own - 1)
    def _():
        deal(dw_scr, kept_ref, given_ref, meta[1 + own])


def load_rows(ref, c, count):
    return [
        jnp.concatenate(
            [ref[0, s * H + 2 * c : s * H + 2 * c + 1, :], ref[0, s * H + 2 * c + 1 : s * H + 2 * c + 2, :]], axis=1
        )
        for s in range(count)
    ]


def key_terms(ks, vs, qzs, czs, bias, stats):
    scores = [nt(k, qz) for k, qz in zip(ks, qzs)]
    grads = [nt(v, cz) for v, cz in zip(vs, czs)]
    probs = [
        jnp.exp((s if bias is None else s + bias) - peak) * inv for s, (peak, inv, _) in zip(scores, stats)
    ]
    ds = [(p * (g - delta)).astype(BF16) for p, g, (_, _, delta) in zip(probs, grads, stats)]
    return [nn(d, qz) for d, qz in zip(ds, qzs)], [nn(p.astype(BF16), cz) for p, cz in zip(probs, czs)]


def peer_kernel(near_ids, meta, q_ref, cot_ref, stats_ref, tile_ref, k_ref, v_ref, acc_in, acc_ref, qz_scr, cz_scr):
    i = pl.program_id(0)
    pairs = q_ref.shape[1] // LANES
    width = q_ref.shape[1]
    own = acc_ref.shape[0]

    @pl.when(i == 0)
    def _():
        acc_ref[...] = acc_in[...]

    for c in range(pairs):
        cols = slice(c * LANES, (c + 1) * LANES)
        qz_scr[c] = two_heads(q_ref[:, cols])
        cz_scr[c] = two_heads(cot_ref[:, cols])
    for j in range(NBR):
        n = near_ids[own + i, j]

        @pl.when(n < own)
        def _(j=j, n=n):
            every = range(pairs)
            cols = [slice(c * LANES, (c + 1) * LANES) for c in every]
            dks, dvs = key_terms(
                [k_ref[n, :, cols[c]] for c in every], [v_ref[n, :, cols[c]] for c in every],
                [qz_scr[c] for c in every], [cz_scr[c] for c in every], bias_of(tile_ref[0, j]),
                [load_rows(stats_ref, c, 3) for c in every],
            )
            for c in every:
                acc_ref[n, :, cols[c]] += dks[c]
                acc_ref[n, :, width + c * LANES : width + (c + 1) * LANES] += dvs[c]


def far_kernel(meta, q_ref, cot_ref, stats_ref, k_ref, v_ref, acc_ref, xt_ref, dkv_ref, kept_ref, given_ref, dw_scr):
    width = q_ref.shape[1]
    i = pl.program_id(0)
    own = pl.num_programs(0)

    @pl.when(i == 0)
    def _():
        dw_scr[...] = jnp.zeros_like(dw_scr)

    every = range(width // LANES)
    cols = [slice(c * LANES, (c + 1) * LANES) for c in every]
    dks, dvs = key_terms(
        [k_ref[0, :, cols[c]] for c in every], [v_ref[0, :, cols[c]] for c in every],
        [two_heads(q_ref[:, cols[c]]) for c in every], [two_heads(cot_ref[:, cols[c]]) for c in every], None,
        [load_rows(stats_ref, c, 3) for c in every],
    )
    for c in every:
        vcols = slice(width + c * LANES, width + (c + 1) * LANES)
        dkv_ref[:, cols[c]] = (acc_ref[0, :, cols[c]] + dks[c].astype(BF16).astype(F32)).astype(BF16)
        dkv_ref[:, vcols] = (acc_ref[0, :, vcols] + dvs[c].astype(BF16).astype(F32)).astype(BF16)
    dw_scr[...] += nn(xt_ref[0], dkv_ref[...]).reshape(dw_scr.shape)

    @pl.when(i == own - 1)
    def _():
        deal(dw_scr, kept_ref, given_ref, meta[1 + own])


def project_kernel(x_ref, w_ref, wt_ref, *rest):
    qkv_ref, t_ref = rest[-2:]
    bs = t_ref.shape[2]
    qkv_ref[...] = nn(x_ref[...], w_ref[...]).astype(BF16)

    @pl.when(pl.program_id(0) < 2)
    def _():
        turned = nt(wt_ref[...], x_ref[...]).astype(BF16)
        for b in range(t_ref.shape[0]):
            t_ref[b] = turned[:, b * bs : (b + 1) * bs]


def call(kernel, scalars, steps, in_specs, out_specs, out_shape, scratch, flops, touched, name, aliases={}):
    return pl.pallas_call(
        kernel,
        grid_spec=pltpu.PrefetchScalarGridSpec(
            num_scalar_prefetch=scalars, grid=(steps,), in_specs=in_specs, out_specs=out_specs, scratch_shapes=scratch
        ),
        out_shape=out_shape,
        input_output_aliases=aliases,
        compiler_params=pltpu.CompilerParams(dimension_semantics=("arbitrary",), vmem_limit_bytes=VMEM_LIMIT),
        cost_estimate=pl.CostEstimate(flops=flops, bytes_accessed=touched, transcendentals=0),
        name=name,
    )


def once(shape, at=0):
    return pl.BlockSpec(shape, lambda i, *s: (at,) + (0,) * (len(shape) - 1), pipeline_mode=pl.Buffered(1))


def body(node_feats, w_qkv, w_out, neighbours, tiles, partner, layer_cot):
    rows, width = node_feats.shape
    doms, groups = lax.axis_size("dom"), lax.axis_size("head")
    devices = doms * groups
    blocks = partner.shape[0]
    own = blocks // groups
    bs = tiles.shape[2]
    span = width // groups
    half = lax.axis_index("head")
    base = half * own

    near_ids = jnp.roll((neighbours - base) % blocks, -base, axis=0)
    mine = lax.dynamic_slice_in_dim(partner, base, own, 0)
    core = lax.axis_index("dom") % 2
    meta = jnp.concatenate([base[None].astype(jnp.int32), mine // own, core[None].astype(jnp.int32)])

    w_by = w_qkv.reshape(width, groups, 3, span).transpose(2, 0, 1, 3).reshape(3, width, width)
    w_all = jnp.concatenate([w_by[0] * jnp.asarray(0.125, BF16), w_by[1], w_by[2]], axis=1)

    def swap(x):
        return lax.ppermute(x, "head", [(0, 1), (1, 0)])

    def exchange(x):
        return lax.all_to_all(x, DEVICES, split_axis=0, concat_axis=0, tiled=True)

    def spread(x):
        return x.reshape(own, bs, width).transpose(1, 0, 2)

    def gathered(x):
        return jnp.dot(one_hot, x.reshape(-1, width), preferred_element_type=F32).astype(BF16).reshape(
            devices, own, width
        )

    digits = jnp.stack([mine // DIGIT, mine % DIGIT], axis=1).astype(BF16)
    digits = jnp.pad(digits, ((0, 0), (0, LANES - 2)))
    digits = jnp.broadcast_to(digits[None], (devices, own, LANES))
    first_hop = jnp.concatenate([spread(node_feats), digits], axis=2)
    rows_in = exchange(first_hop)
    peer_feats = swap(node_feats)
    cot = jnp.dot(layer_cot, w_out.T, preferred_element_type=F32).astype(BF16)
    cot_rows = spread(cot)
    cot_t = jnp.einsum("ck,brk->bcr", w_out, layer_cot.reshape(own, bs, width), preferred_element_type=F32).astype(BF16)

    w_turned = w_all[:, width:].T
    hold = pl.BlockSpec(memory_space=pl.ANY)

    def project(feats, total, at, carried, name):
        return call(
            project_kernel, 0, 3,
            [
                once((rows, width)),
                pl.BlockSpec((width, width), lambda i: (0, (i + 1) % 3)),
                pl.BlockSpec((width, width), lambda i: (jnp.minimum(i, 1), 0)),
            ]
            + [hold] * len(carried),
            [
                pl.BlockSpec((rows, width), lambda i: (at, (i + 1) % 3)),
                pl.BlockSpec((own, width, bs), lambda i: (at, jnp.minimum(i, 1), 0)),
            ],
            [
                jax.ShapeDtypeStruct((total * bs, 3 * width), BF16),
                jax.ShapeDtypeStruct((total, 2 * width, bs), BF16),
            ],
            [], 2 * rows * width * 5 * width, 8 << 20, name, aliases={3: 0, 4: 1} if carried else {},
        )(feats, w_all, w_turned, *carried)

    own_part = project(node_feats, blocks, 0, (), "project_own")
    feats_t = node_feats.reshape(own, bs, width).transpose(0, 2, 1)
    out_t = layer_cot.reshape(own, bs, width).transpose(0, 2, 1)
    rows_in, cot_rows, own_part, peer_feats, cot_t, feats_t, out_t = lax.optimization_barrier(
        (rows_in, cot_rows, own_part, peer_feats, cot_t, feats_t, out_t)
    )

    weigh = jnp.pad(jnp.asarray([DIGIT, 1], F32), (0, LANES - 2))
    ids = jnp.sum(rows_in.reshape(-1, width + LANES)[:, width:].astype(F32) * weigh[None], axis=1, keepdims=True)
    one_hot = (ids == jnp.arange(ids.shape[0], dtype=jnp.int32)[None, :].astype(F32)).astype(BF16)
    second = jnp.concatenate([gathered(rows_in[:, :, :width]), cot_rows], axis=2)
    second = exchange(second)
    part_qkv, part_t = project(peer_feats, blocks, 1, own_part, "project_peer")
    part_blk = part_qkv.reshape(blocks, bs, 3 * width)
    pair_flops = 2 * bs * bs * width * 2
    step = lambda i, *s: (i, 0)
    row_step = lambda i, *s: (i, 0, 0)
    rows_spec = pl.BlockSpec((bs, width), step)
    tile_spec = pl.BlockSpec((1, NBR, bs, bs), lambda i, ids, meta: (meta[0] + i, 0, 0, 0))
    k_spec = pl.BlockSpec((blocks, bs, width), lambda i, *s: (0, 0, 1), pipeline_mode=pl.Buffered(1))
    v_spec = pl.BlockSpec((blocks, bs, width), lambda i, *s: (0, 0, 2), pipeline_mode=pl.Buffered(1))
    kt_spec = pl.BlockSpec((blocks, width, bs), lambda i, *s: (0, 0, 0), pipeline_mode=pl.Buffered(1))
    vt_spec = pl.BlockSpec((blocks, width, bs), lambda i, *s: (0, 1, 0), pipeline_mode=pl.Buffered(1))
    stats_spec = pl.BlockSpec((1, STATS, bs), row_step)
    turned_spec = pl.BlockSpec((1, width, bs), row_step)
    near_out, sums = call(
        near_kernel, 2, own,
        [rows_spec, tile_spec, k_spec, vt_spec],
        [pl.BlockSpec((1, width, bs), row_step), pl.BlockSpec((1, 2 * H, bs), row_step)],
        [jax.ShapeDtypeStruct((own, width, bs), F32), jax.ShapeDtypeStruct((own, 2 * H, bs), F32)],
        [pltpu.VMEM((NBR, bs, 2 * bs), F32)],
        own * 16 * pair_flops, 10 << 20, "near_forward",
    )(near_ids, meta, part_qkv, tiles, part_blk, part_t)
    second, near_out, sums, cot_out = lax.optimization_barrier((second, near_out, sums, cot))

    picked = gathered(second[:, :, width:])
    far_feats = second[:, :, :width].transpose(1, 0, 2).reshape(rows, width)
    picked, far_feats = lax.optimization_barrier((picked, far_feats))
    far_cot = exchange(picked)
    far_qkv, far_t = project(far_feats, own, 0, (), "project_far")
    far_blk = far_qkv.reshape(own, bs, 3 * width)
    peer_cot = swap(cot_out)

    far_k_spec = pl.BlockSpec((1, bs, width), lambda i, *s: (i, 0, 1))
    far_v_spec = pl.BlockSpec((1, bs, width), lambda i, *s: (i, 0, 2))
    far_kt_spec = pl.BlockSpec((1, width, bs), row_step)
    far_vt_spec = pl.BlockSpec((1, width, bs), lambda i, *s: (i, 1, 0))
    att, stats, slots = call(
        merge_kernel, 1, own,
        [rows_spec, turned_spec, far_k_spec, far_vt_spec, turned_spec, pl.BlockSpec((1, 2 * H, bs), row_step)],
        [turned_spec, stats_spec, pl.BlockSpec((1, STATS, bs), lambda i, meta: (meta[1 + i], 0, 0))],
        [
            jax.ShapeDtypeStruct((own, width, bs), BF16),
            jax.ShapeDtypeStruct((own, STATS, bs), F32),
            jax.ShapeDtypeStruct((devices, STATS, bs), F32),
        ],
        [], own * 4 * pair_flops, 6 << 20, "far_forward",
    )(meta, part_qkv, cot_t, far_blk, far_t, near_out, sums)
    peer_stats = swap(stats)
    pairs = width // LANES
    piece = (groups, doms // 2, width // doms, width)
    piece_spec = pl.BlockSpec(piece, lambda i, *s: (0, 0, 0, 0), pipeline_mode=pl.Buffered(1))
    piece_out = jax.ShapeDtypeStruct(piece, F32)
    dw_scratch = pltpu.VMEM((doms // 2, 2, width // doms, 2 * width), F32)
    dq, acc, kept, given = call(
        own_kernel, 2, own,
        [rows_spec, rows_spec, tile_spec, stats_spec, k_spec, v_spec, kt_spec, far_k_spec, far_v_spec, far_kt_spec,
         turned_spec, turned_spec, turned_spec],
        [turned_spec, pl.BlockSpec((own, bs, 2 * width), lambda i, *s: (0, 0, 0)), piece_spec, piece_spec],
        [
            jax.ShapeDtypeStruct((own, width, bs), BF16),
            jax.ShapeDtypeStruct((own, bs, 2 * width), F32),
            piece_out,
            piece_out,
        ],
        [
            pltpu.VMEM((pairs, NBR * bs, 2 * bs), BF16),
            pltpu.VMEM((pairs, NBR * bs, 2 * bs), BF16),
            pltpu.VMEM((pairs, 2 * bs, LANES), BF16),
            pltpu.VMEM((pairs, 2 * bs, LANES), BF16),
            pltpu.VMEM((NBR, bs, 2 * bs), F32),
            dw_scratch,
        ],
        own * 24 * pair_flops, 30 << 20, "own_backward",
    )(near_ids, meta, part_qkv, cot, tiles, stats, part_blk, part_blk, part_t, far_blk, far_blk, far_t,
      feats_t, out_t, att)
    acc, peer_stats, peer_cot, far_cot, slots = lax.optimization_barrier((acc, peer_stats, peer_cot, far_cot, slots))
    far_slots = exchange(slots)
    far_cot = far_cot.transpose(1, 0, 2).reshape(rows, width)

    layer_out = jnp.einsum("bar,ac->brc", att, w_out, preferred_element_type=F32).astype(BF16).reshape(rows, width)

    def paired(kept, given):
        return (kept + lax.ppermute(given, "dom", [(d, d ^ 1) for d in range(doms)])).astype(BF16)

    early = paired(kept, given)

    (acc,) = call(
        peer_kernel, 2, own,
        [
            pl.BlockSpec((bs, width), lambda i, *s: (own + i, 0)),
            pl.BlockSpec((bs, width), step),
            pl.BlockSpec((1, STATS, bs), lambda i, *s: (i, 0, 0)),
            pl.BlockSpec((1, NBR, bs, bs), lambda i, ids, meta: (own - meta[0] + i, 0, 0, 0)),
            pl.BlockSpec((own, bs, width), lambda i, *s: (0, 0, 1), pipeline_mode=pl.Buffered(1)),
            pl.BlockSpec((own, bs, width), lambda i, *s: (0, 0, 2), pipeline_mode=pl.Buffered(1)),
            once((own, bs, 2 * width)),
        ],
        [pl.BlockSpec((own, bs, 2 * width), lambda i, *s: (0, 0, 0))],
        [jax.ShapeDtypeStruct((own, bs, 2 * width), F32)],
        [
            pltpu.VMEM((width // LANES, 2 * bs, LANES), BF16),
            pltpu.VMEM((width // LANES, 2 * bs, LANES), BF16),
        ],
        own * 16 * pair_flops, 20 << 20, "peer_queries",
    )(near_ids, meta, part_qkv, peer_cot, peer_stats, tiles, part_blk, part_blk, acc)

    dkv, kept, given = call(
        far_kernel, 1, own,
        [
            pl.BlockSpec((bs, width), step),
            pl.BlockSpec((bs, width), step),
            pl.BlockSpec((1, STATS, bs), lambda i, meta: (meta[1 + i], 0, 0)),
            pl.BlockSpec((1, bs, width), lambda i, *s: (i, 0, 1)),
            pl.BlockSpec((1, bs, width), lambda i, *s: (i, 0, 2)),
            pl.BlockSpec((1, bs, 2 * width), lambda i, *s: (i, 0, 0)),
            turned_spec,
        ],
        [pl.BlockSpec((bs, 2 * width), step), piece_spec, piece_spec],
        [jax.ShapeDtypeStruct((rows, 2 * width), BF16), piece_out, piece_out],
        [dw_scratch], own * 8 * pair_flops, 10 << 20, "far_queries",
    )(meta, far_qkv, far_cot, far_slots, part_blk, part_blk, acc, feats_t)

    split = jnp.concatenate([early, paired(kept, given)], axis=2).reshape(devices // 2, 2 * width // doms, width)
    same_core = [[d * groups + g for g in range(groups) for d in range(e, doms, 2)] for e in range(2)]
    moved = lax.all_to_all(split, DEVICES, split_axis=0, concat_axis=0, axis_index_groups=same_core, tiled=True)
    summed = jnp.sum(moved.astype(F32), axis=0)
    w_plain = w_by.transpose(1, 0, 2).reshape(width, 3 * width)
    feat_grad = (
        jnp.einsum("bcr,dc->brd", dq, w_plain[:, :width], preferred_element_type=F32).reshape(rows, width)
        + lax.dot_general(dkv, w_plain[:, width:], (((1,), (1,)), ((), ())), preferred_element_type=F32)
    ).astype(BF16)
    deep = width // doms
    dw_out = summed[:deep, :span].T
    dw_qkv = jnp.concatenate([summed[:deep, span:], summed[deep:]], axis=1)
    return (layer_out, feat_grad, dw_qkv, dw_out)


def solution(mesh):
    placed = (
        P(DEVICES, None),
        P(),
        P(),
        P("dom", None),
        P("dom", None, None, None),
        P("dom"),
        P(DEVICES, None),
    )
    return jax.shard_map(
        body,
        mesh=mesh,
        in_specs=placed,
        out_specs=(P(DEVICES, None), P(DEVICES, None), P("dom", "head"), P("head", "dom")),
        check_vma=False,
    )
```

```python
import jax
import jax.numpy as jnp
from jax import lax
from jax.experimental import pallas as pl
from jax.experimental.pallas import tpu as pltpu
from jax.sharding import PartitionSpec as P

H = 8
NBR = 4
DEVICES = ("dom", "head")
F32, BF16 = jnp.float32, jnp.bfloat16
NEG = -1e30
LANES = 128
STATS = 3 * H
DIGIT = 32
VMEM_LIMIT = 58 * 1024 * 1024


def nn(a, b):
    return jnp.dot(a, b, preferred_element_type=F32)


def nt(a, b):
    return lax.dot_general(a, b, (((1,), (1,)), ((), ())), preferred_element_type=F32)


def tn(a, b):
    return lax.dot_general(a, b, (((0,), (0,)), ((), ())), preferred_element_type=F32)


def two_heads(pair):
    lane = lax.broadcasted_iota(jnp.int32, pair.shape, 1)
    zero = jnp.zeros_like(pair)
    return jnp.concatenate(
        [jnp.where(lane < LANES // 2, pair, zero), jnp.where(lane >= LANES // 2, pair, zero)], axis=0
    )


def own_heads(both):
    half, rows = both.shape[0] // 2, both.shape[1] // 2
    return jnp.concatenate([both[:half, :rows], both[half:, rows:]], axis=0)


def bias_of(tile):
    bias = jnp.where(tile != 0, 0.0, NEG).astype(F32).T
    return jnp.concatenate([bias, bias], axis=1)


def split_stat(row):
    return row[:, : row.shape[1] // 2], row[:, row.shape[1] // 2 :]


def near_kernel(near_ids, meta, q_ref, tile_ref, k_ref, v_ref, out_ref, sums_ref, bias_scr):
    i = pl.program_id(0)
    for j in range(NBR):
        bias_scr[j] = bias_of(tile_ref[0, j])
    ids = [near_ids[i, j] for j in range(NBR)]
    pairs = q_ref.shape[1] // LANES

    def scores_of(c):
        cols = slice(c * LANES, (c + 1) * LANES)
        qz = two_heads(q_ref[:, cols])
        return jnp.concatenate([nt(k_ref[ids[j], :, cols], qz) + bias_scr[j] for j in range(NBR)], axis=0)

    ready = scores_of(0)
    for c in range(pairs):
        cols = slice(c * LANES, (c + 1) * LANES)
        scores, ready = ready, scores_of(c + 1) if c + 1 < pairs else None
        peak = jnp.max(scores, axis=0, keepdims=True)
        terms = jnp.exp(scores - peak)
        total = jnp.sum(terms, axis=0, keepdims=True)
        values = jnp.concatenate([v_ref[ids[j], :, cols] for j in range(NBR)], axis=0)
        out_ref[0, cols, :] = own_heads(tn(values, terms.astype(BF16)))
        store_rows(sums_ref, c, (peak, total))


def store_rows(ref, c, rows, b=0):
    for s, row in enumerate(rows):
        for e, part in enumerate(split_stat(row)):
            at = s * H + 2 * c + e
            ref[b, at : at + 1, :] = part


def merge_kernel(q_ref, cot_t_ref, fk_ref, fv_ref, out_ref, sums_ref, att_ref, stats_ref):
    mid = LANES // 2
    bs = fk_ref.shape[1]
    units = [(b, c) for b in range(fk_ref.shape[0]) for c in range(q_ref.shape[1] // LANES)]
    cols = [slice(c * LANES, (c + 1) * LANES) for _, c in units]
    scores = [
        nt(fk_ref[b, :, cols[u]], two_heads(q_ref[b * bs : (b + 1) * bs, cols[u]])) for u, (b, c) in enumerate(units)
    ]
    peaks, kepts, invs, lows = [], [], [], []
    for u, (b, c) in enumerate(units):
        near_peak, near_total = load_rows(sums_ref, c, 2, b)
        peak = jnp.maximum(near_peak, jnp.max(scores[u], axis=0, keepdims=True))
        terms = jnp.exp(scores[u] - peak)
        kept = jnp.exp(near_peak - peak)
        inv = 1.0 / (near_total * kept + jnp.sum(terms, axis=0, keepdims=True))
        lows.append((terms * inv).astype(BF16))
        peaks.append(peak)
        kepts.append(kept)
        invs.append(inv)
    far_outs = [own_heads(tn(fv_ref[b, :, cols[u]], lows[u])) for u, (b, c) in enumerate(units)]
    for u, (b, c) in enumerate(units):
        first, second = split_stat(kepts[u] * invs[u])
        near_out = out_ref[b, cols[u], :]
        near_out = jnp.concatenate([near_out[:mid] * first, near_out[mid:] * second], axis=0)
        att = (far_outs[u] + near_out).astype(BF16)
        att_ref[b, cols[u], :] = att
        prod = cot_t_ref[b, cols[u], :].astype(F32) * att.astype(F32)
        delta = jnp.concatenate(
            [jnp.sum(prod[:mid], axis=0, keepdims=True), jnp.sum(prod[mid:], axis=0, keepdims=True)], axis=1
        )
        store_rows(stats_ref, c, (peaks[u], invs[u], delta), b)


def deal(dw_scr, kept_ref, given_ref, core):
    groups, span = kept_ref.shape[0], kept_ref.shape[3] // 2
    for g in range(groups):
        for t in range(2):
            at = (t * groups + g) * span
            kept_ref[g, :, :, t * span : (t + 1) * span] = dw_scr[:, core, :, at : at + span]
            given_ref[g, :, :, t * span : (t + 1) * span] = dw_scr[:, 1 - core, :, at : at + span]


def own_kernel(near_ids, meta, q_ref, cot_ref, tile_ref, stats_ref, k_ref, v_ref, fk_ref, fv_ref,
               xt_ref, ct_ref, att_ref, dq_ref, acc_ref, kept_ref, given_ref, slot_ref, p_scr, ds_scr, qz_scr, cz_scr, bias_scr,
               dw_scr):
    i = pl.program_id(0)
    bs, width = q_ref.shape
    pairs = width // LANES
    own = acc_ref.shape[0]

    @pl.when(i == 0)
    def _():
        acc_ref[...] = jnp.zeros_like(acc_ref)
        dw_scr[...] = jnp.zeros_like(dw_scr)

    slot_ref[...] = stats_ref[...]
    for j in range(NBR):
        bias_scr[j] = bias_of(tile_ref[0, j])
    ids = [near_ids[i, j] for j in range(NBR)]
    for c in range(pairs):
        cols = slice(c * LANES, (c + 1) * LANES)
        qz = two_heads(q_ref[:, cols])
        cz = two_heads(cot_ref[:, cols])
        qz_scr[c] = qz
        cz_scr[c] = cz
        peak, inv, delta = load_rows(stats_ref, c, 3)
        parts = []
        for j in range(NBR + 1):
            rows = slice(j * bs, (j + 1) * bs)
            if j < NBR:
                scores = nt(k_ref[ids[j], :, cols], qz) + bias_scr[j]
                grad_probs = nt(v_ref[ids[j], :, cols], cz)
            else:
                scores = nt(fk_ref[0, :, cols], qz)
                grad_probs = nt(fv_ref[0, :, cols], cz)
            probs = jnp.exp(scores - peak) * inv
            parts.append((probs * (grad_probs - delta)).astype(BF16))
            if j < NBR:
                p_scr[c, rows, :] = probs.astype(BF16)
                ds_scr[c, rows, :] = parts[j]
        keys = jnp.concatenate([k_ref[ids[j], :, cols] for j in range(NBR)] + [fk_ref[0, :, cols]], axis=0)
        dq_ref[0, cols, :] = (own_heads(tn(keys, jnp.concatenate(parts, axis=0))) * 0.125).astype(BF16)
    half = dw_scr.shape[:3] + (width,)
    dw_scr[:, :, :, :width] += nt(ct_ref[0], att_ref[0]).reshape(half)
    dw_scr[:, :, :, width:] += nt(xt_ref[0], dq_ref[0]).reshape(half)

    for j in range(NBR):

        @pl.when(ids[j] < own)
        def _(j=j):
            n = ids[j]
            for c in range(pairs):
                cols = slice(c * LANES, (c + 1) * LANES)
                vcols = slice(width + c * LANES, width + (c + 1) * LANES)
                rows = slice(j * bs, (j + 1) * bs)
                acc_ref[n, :, cols] += nn(ds_scr[c, rows, :], qz_scr[c])
                acc_ref[n, :, vcols] += nn(p_scr[c, rows, :], cz_scr[c])

    @pl.when(i == own - 1)
    def _():
        deal(dw_scr, kept_ref, given_ref, meta[1 + own])


def load_rows(ref, c, count, b=0):
    return [
        jnp.concatenate(
            [ref[b, s * H + 2 * c : s * H + 2 * c + 1, :], ref[b, s * H + 2 * c + 1 : s * H + 2 * c + 2, :]], axis=1
        )
        for s in range(count)
    ]


def key_terms(ks, vs, qzs, czs, bias, stats):
    scores = [nt(k, qz) for k, qz in zip(ks, qzs)]
    grads = [nt(v, cz) for v, cz in zip(vs, czs)]
    probs = [
        jnp.exp((s if bias is None else s + bias) - peak) * inv for s, (peak, inv, _) in zip(scores, stats)
    ]
    ds = [(p * (g - delta)).astype(BF16) for p, g, (_, _, delta) in zip(probs, grads, stats)]
    return [nn(d, qz) for d, qz in zip(ds, qzs)], [nn(p.astype(BF16), cz) for p, cz in zip(probs, czs)]


def peer_kernel(near_ids, meta, q_ref, cot_ref, stats_ref, tile_ref, k_ref, v_ref, acc_in, acc_ref, qz_scr, cz_scr):
    i = pl.program_id(0)
    pairs = q_ref.shape[1] // LANES
    width = q_ref.shape[1]
    own = acc_ref.shape[0]

    @pl.when(i == 0)
    def _():
        acc_ref[...] = acc_in[...]

    for c in range(pairs):
        cols = slice(c * LANES, (c + 1) * LANES)
        qz_scr[c] = two_heads(q_ref[:, cols])
        cz_scr[c] = two_heads(cot_ref[:, cols])
    for j in range(NBR):
        n = near_ids[own + i, j]

        @pl.when(n < own)
        def _(j=j, n=n):
            every = range(pairs)
            cols = [slice(c * LANES, (c + 1) * LANES) for c in every]
            dks, dvs = key_terms(
                [k_ref[n, :, cols[c]] for c in every], [v_ref[n, :, cols[c]] for c in every],
                [qz_scr[c] for c in every], [cz_scr[c] for c in every], bias_of(tile_ref[0, j]),
                [load_rows(stats_ref, c, 3) for c in every],
            )
            for c in every:
                acc_ref[n, :, cols[c]] += dks[c]
                acc_ref[n, :, width + c * LANES : width + (c + 1) * LANES] += dvs[c]


def far_kernel(meta, q_ref, cot_ref, first_ref, second_ref, k_ref, v_ref, acc_ref, xt_ref, dkv_ref, kept_ref,
               given_ref, dw_scr):
    bs, width = k_ref.shape[1:]
    i = pl.program_id(0)

    @pl.when(i == 0)
    def _():
        dw_scr[...] = jnp.zeros_like(dw_scr)

    units = [(b, c) for b in range(2) for c in range(width // LANES)]
    cols = [slice(c * LANES, (c + 1) * LANES) for _, c in units]
    rows = [slice(b * bs, (b + 1) * bs) for b, _ in units]
    every = range(len(units))
    dks, dvs = key_terms(
        [k_ref[units[u][0], :, cols[u]] for u in every], [v_ref[units[u][0], :, cols[u]] for u in every],
        [two_heads(q_ref[rows[u], cols[u]]) for u in every], [two_heads(cot_ref[rows[u], cols[u]]) for u in every],
        None, [load_rows((first_ref, second_ref)[b], c, 3) for b, c in units],
    )
    for u, (b, c) in enumerate(units):
        vcols = slice(width + c * LANES, width + (c + 1) * LANES)
        dkv_ref[rows[u], cols[u]] = (acc_ref[b, :, cols[u]] + dks[u].astype(BF16).astype(F32)).astype(BF16)
        dkv_ref[rows[u], vcols] = (acc_ref[b, :, vcols] + dvs[u].astype(BF16).astype(F32)).astype(BF16)
    xt = jnp.concatenate([xt_ref[0], xt_ref[1]], axis=1)
    dw_scr[...] += nn(xt, dkv_ref[...]).reshape(dw_scr.shape)

    @pl.when(i == pl.num_programs(0) - 1)
    def _():
        deal(dw_scr, kept_ref, given_ref, meta[1 + 2 * pl.num_programs(0)])


def project_kernel(x_ref, w_ref, *rest):
    rest[-1][...] = nn(x_ref[...], w_ref[...]).astype(BF16)


def call(kernel, scalars, steps, in_specs, out_specs, out_shape, scratch, flops, touched, name, aliases={}):
    return pl.pallas_call(
        kernel,
        grid_spec=pltpu.PrefetchScalarGridSpec(
            num_scalar_prefetch=scalars, grid=(steps,), in_specs=in_specs, out_specs=out_specs, scratch_shapes=scratch
        ),
        out_shape=out_shape,
        input_output_aliases=aliases,
        compiler_params=pltpu.CompilerParams(dimension_semantics=("arbitrary",), vmem_limit_bytes=VMEM_LIMIT),
        cost_estimate=pl.CostEstimate(flops=flops, bytes_accessed=touched, transcendentals=0),
        name=name,
    )


def once(shape, at=0):
    return pl.BlockSpec(shape, lambda i, *s: (at,) + (0,) * (len(shape) - 1), pipeline_mode=pl.Buffered(1))


def body(node_feats, w_qkv, w_out, neighbours, tiles, partner, layer_cot):
    rows, width = node_feats.shape
    doms, groups = lax.axis_size("dom"), lax.axis_size("head")
    devices = doms * groups
    blocks = partner.shape[0]
    own = blocks // groups
    bs = tiles.shape[2]
    span = width // groups
    half = lax.axis_index("head")
    base = half * own

    near_ids = jnp.roll((neighbours - base) % blocks, -base, axis=0)
    mine = lax.dynamic_slice_in_dim(partner, base, own, 0)
    core = lax.axis_index("dom") % 2
    meta = jnp.concatenate([base[None].astype(jnp.int32), mine // own, core[None].astype(jnp.int32)])

    w_by = w_qkv.reshape(width, groups, 3, span).transpose(2, 0, 1, 3).reshape(3, width, width)
    w_all = jnp.concatenate([w_by[0] * jnp.asarray(0.125, BF16), w_by[1], w_by[2]], axis=1)

    def swap(x):
        return lax.ppermute(x, "head", [(0, 1), (1, 0)])

    def exchange(x):
        return lax.all_to_all(x, DEVICES, split_axis=0, concat_axis=0, tiled=True)

    def spread(x):
        return x.reshape(own, bs, width).transpose(1, 0, 2)

    def gathered(x):
        return jnp.dot(one_hot, x.reshape(-1, width), preferred_element_type=F32).astype(BF16).reshape(
            devices, own, width
        )

    digits = jnp.stack([mine // DIGIT, mine % DIGIT], axis=1).astype(BF16)
    digits = jnp.pad(digits, ((0, 0), (0, LANES - 2)))
    digits = jnp.broadcast_to(digits[None], (devices, own, LANES))
    first_hop = jnp.concatenate([spread(node_feats), digits], axis=2)
    rows_in = exchange(first_hop)
    peer_feats = swap(node_feats)
    cot = jnp.dot(layer_cot, w_out.T, preferred_element_type=F32).astype(BF16)
    cot_rows = spread(cot)
    cot_t = jnp.einsum("ck,brk->bcr", w_out, layer_cot.reshape(own, bs, width), preferred_element_type=F32).astype(BF16)

    hold = pl.BlockSpec(memory_space=pl.ANY)

    def project(feats, total, at, carried, name):
        return call(
            project_kernel, 0, 3,
            [
                once((rows, width)),
                pl.BlockSpec((width, width), lambda i: (0, i)),
            ]
            + [hold] * len(carried),
            [
                pl.BlockSpec((rows, width), lambda i: (at, i)),
            ],
            [jax.ShapeDtypeStruct((total * bs, 3 * width), BF16)],
            [], 2 * rows * width * 3 * width, 6 << 20, name, aliases={2: 0} if carried else {},
        )(feats, w_all, *carried)[0]

    own_part = project(node_feats, blocks, 0, (), "project_own")
    feats_t = node_feats.reshape(own, bs, width).transpose(0, 2, 1)
    out_t = layer_cot.reshape(own, bs, width).transpose(0, 2, 1)
    rows_in, cot_rows, own_part, peer_feats, cot_t, feats_t, out_t = lax.optimization_barrier(
        (rows_in, cot_rows, own_part, peer_feats, cot_t, feats_t, out_t)
    )

    weigh = jnp.pad(jnp.asarray([DIGIT, 1], F32), (0, LANES - 2))
    ids = jnp.sum(rows_in.reshape(-1, width + LANES)[:, width:].astype(F32) * weigh[None], axis=1, keepdims=True)
    one_hot = (ids == jnp.arange(ids.shape[0], dtype=jnp.int32)[None, :].astype(F32)).astype(BF16)
    second = jnp.concatenate([gathered(rows_in[:, :, :width]), cot_rows], axis=2)
    second = exchange(second)
    part_qkv = project(peer_feats, blocks, 1, (own_part,), "project_peer")
    part_blk = part_qkv.reshape(blocks, bs, 3 * width)
    pair_flops = 2 * bs * bs * width * 2
    step = lambda i, *s: (i, 0)
    row_step = lambda i, *s: (i, 0, 0)
    rows_spec = pl.BlockSpec((bs, width), step)
    tile_spec = pl.BlockSpec((1, NBR, bs, bs), lambda i, ids, meta: (meta[0] + i, 0, 0, 0))
    k_spec = pl.BlockSpec((blocks, bs, width), lambda i, *s: (0, 0, 1), pipeline_mode=pl.Buffered(1))
    v_spec = pl.BlockSpec((blocks, bs, width), lambda i, *s: (0, 0, 2), pipeline_mode=pl.Buffered(1))
    stats_spec = pl.BlockSpec((1, STATS, bs), row_step)
    turned_spec = pl.BlockSpec((1, width, bs), row_step)
    near_out, sums = call(
        near_kernel, 2, own,
        [rows_spec, tile_spec, k_spec, v_spec],
        [pl.BlockSpec((1, width, bs), row_step), pl.BlockSpec((1, 2 * H, bs), row_step)],
        [jax.ShapeDtypeStruct((own, width, bs), F32), jax.ShapeDtypeStruct((own, 2 * H, bs), F32)],
        [pltpu.VMEM((NBR, bs, 2 * bs), F32)],
        own * 16 * pair_flops, 10 << 20, "near_forward",
    )(near_ids, meta, part_qkv, tiles, part_blk, part_blk)
    second, near_out, sums, cot_out = lax.optimization_barrier((second, near_out, sums, cot))

    picked = gathered(second[:, :, width:])
    far_feats = second[:, :, :width].transpose(1, 0, 2).reshape(rows, width)
    picked, far_feats = lax.optimization_barrier((picked, far_feats))
    far_cot = exchange(picked)
    far_qkv = jnp.dot(far_feats, w_all, preferred_element_type=F32).astype(BF16)
    far_blk = far_qkv.reshape(own, bs, 3 * width)
    peer_cot = swap(cot_out)

    far_k_spec = pl.BlockSpec((1, bs, width), lambda i, *s: (i, 0, 1))
    far_v_spec = pl.BlockSpec((1, bs, width), lambda i, *s: (i, 0, 2))
    pair_rows = pl.BlockSpec((2 * bs, width), step)
    pair_turned = pl.BlockSpec((2, width, bs), row_step)
    pair_k = pl.BlockSpec((2, bs, width), lambda i, *s: (i, 0, 1))
    pair_v = pl.BlockSpec((2, bs, width), lambda i, *s: (i, 0, 2))
    att, stats = call(
        merge_kernel, 0, own // 2,
        [pair_rows, pair_turned, pair_k, pair_v, pair_turned, pl.BlockSpec((2, 2 * H, bs), row_step)],
        [pair_turned, pl.BlockSpec((2, STATS, bs), row_step)],
        [jax.ShapeDtypeStruct((own, width, bs), BF16), jax.ShapeDtypeStruct((own, STATS, bs), F32)],
        [], own * 4 * pair_flops, 6 << 20, "far_forward",
    )(part_qkv, cot_t, far_blk, far_blk, near_out, sums)
    peer_stats = swap(stats)
    pairs = width // LANES
    piece = (groups, doms // 2, width // doms, width)
    piece_spec = pl.BlockSpec(piece, lambda i, *s: (0, 0, 0, 0), pipeline_mode=pl.Buffered(1))
    piece_out = jax.ShapeDtypeStruct(piece, F32)
    dw_scratch = pltpu.VMEM((doms // 2, 2, width // doms, 2 * width), F32)
    dq, acc, kept, given, slots = call(
        own_kernel, 2, own,
        [rows_spec, rows_spec, tile_spec, stats_spec, k_spec, v_spec, far_k_spec, far_v_spec,
         turned_spec, turned_spec, turned_spec],
        [turned_spec, pl.BlockSpec((own, bs, 2 * width), lambda i, *s: (0, 0, 0)), piece_spec, piece_spec,
         pl.BlockSpec((1, STATS, bs), lambda i, ids, meta: (meta[1 + i], 0, 0))],
        [
            jax.ShapeDtypeStruct((own, width, bs), BF16),
            jax.ShapeDtypeStruct((own, bs, 2 * width), F32),
            piece_out,
            piece_out,
            jax.ShapeDtypeStruct((devices, STATS, bs), F32),
        ],
        [
            pltpu.VMEM((pairs, NBR * bs, 2 * bs), BF16),
            pltpu.VMEM((pairs, NBR * bs, 2 * bs), BF16),
            pltpu.VMEM((pairs, 2 * bs, LANES), BF16),
            pltpu.VMEM((pairs, 2 * bs, LANES), BF16),
            pltpu.VMEM((NBR, bs, 2 * bs), F32),
            dw_scratch,
        ],
        own * 24 * pair_flops, 30 << 20, "own_backward",
    )(near_ids, meta, part_qkv, cot, tiles, stats, part_blk, part_blk, far_blk, far_blk,
      feats_t, out_t, att)
    acc, peer_stats, peer_cot, far_cot, slots = lax.optimization_barrier((acc, peer_stats, peer_cot, far_cot, slots))
    far_slots = exchange(slots)
    far_cot = far_cot.transpose(1, 0, 2).reshape(rows, width)

    layer_out = jnp.einsum("bar,ac->brc", att, w_out, preferred_element_type=F32).astype(BF16).reshape(rows, width)

    def paired(kept, given):
        return (kept + lax.ppermute(given, "dom", [(d, d ^ 1) for d in range(doms)])).astype(BF16)

    early = paired(kept, given)

    (acc,) = call(
        peer_kernel, 2, own,
        [
            pl.BlockSpec((bs, width), lambda i, *s: (own + i, 0)),
            pl.BlockSpec((bs, width), step),
            pl.BlockSpec((1, STATS, bs), lambda i, *s: (i, 0, 0)),
            pl.BlockSpec((1, NBR, bs, bs), lambda i, ids, meta: (own - meta[0] + i, 0, 0, 0)),
            pl.BlockSpec((own, bs, width), lambda i, *s: (0, 0, 1), pipeline_mode=pl.Buffered(1)),
            pl.BlockSpec((own, bs, width), lambda i, *s: (0, 0, 2), pipeline_mode=pl.Buffered(1)),
            once((own, bs, 2 * width)),
        ],
        [pl.BlockSpec((own, bs, 2 * width), lambda i, *s: (0, 0, 0))],
        [jax.ShapeDtypeStruct((own, bs, 2 * width), F32)],
        [
            pltpu.VMEM((width // LANES, 2 * bs, LANES), BF16),
            pltpu.VMEM((width // LANES, 2 * bs, LANES), BF16),
        ],
        own * 16 * pair_flops, 20 << 20, "peer_queries",
    )(near_ids, meta, part_qkv, peer_cot, peer_stats, tiles, part_blk, part_blk, acc)

    dkv, kept, given = call(
        far_kernel, 1, own // 2,
        [
            pair_rows,
            pair_rows,
            pl.BlockSpec((1, STATS, bs), lambda i, meta: (meta[1 + 2 * i], 0, 0)),
            pl.BlockSpec((1, STATS, bs), lambda i, meta: (meta[2 + 2 * i], 0, 0)),
            pair_k,
            pair_v,
            pl.BlockSpec((2, bs, 2 * width), row_step),
            pair_turned,
        ],
        [pl.BlockSpec((2 * bs, 2 * width), step), piece_spec, piece_spec],
        [jax.ShapeDtypeStruct((rows, 2 * width), BF16), piece_out, piece_out],
        [dw_scratch], own * 8 * pair_flops, 10 << 20, "far_queries",
    )(meta, far_qkv, far_cot, far_slots, far_slots, part_blk, part_blk, acc, feats_t)

    split = jnp.concatenate([early, paired(kept, given)], axis=2).reshape(devices // 2, 2 * width // doms, width)
    same_core = [[d * groups + g for g in range(groups) for d in range(e, doms, 2)] for e in range(2)]
    moved = lax.all_to_all(split, DEVICES, split_axis=0, concat_axis=0, axis_index_groups=same_core, tiled=True)
    summed = jnp.sum(moved.astype(F32), axis=0)
    w_plain = w_by.transpose(1, 0, 2).reshape(width, 3 * width)
    feat_grad = (
        jnp.einsum("bcr,dc->brd", dq, w_plain[:, :width], preferred_element_type=F32).reshape(rows, width)
        + lax.dot_general(dkv, w_plain[:, width:], (((1,), (1,)), ((), ())), preferred_element_type=F32)
    ).astype(BF16)
    deep = width // doms
    dw_out = summed[:deep, :span].T
    dw_qkv = jnp.concatenate([summed[:deep, span:], summed[deep:]], axis=1)
    return (layer_out, feat_grad, dw_qkv, dw_out)


def solution(mesh):
    placed = (
        P(DEVICES, None),
        P(),
        P(),
        P("dom", None),
        P("dom", None, None, None),
        P("dom"),
        P(DEVICES, None),
    )
    return jax.shard_map(
        body,
        mesh=mesh,
        in_specs=placed,
        out_specs=(P(DEVICES, None), P(DEVICES, None), P("dom", "head"), P("head", "dom")),
        check_vma=False,
    )
```

```python
import jax
import jax.numpy as jnp
from jax import lax
from jax.experimental import pallas as pl
from jax.experimental.pallas import tpu as pltpu
from jax.sharding import PartitionSpec as P

H = 8
NBR = 4
DEVICES = ("dom", "head")
F32, BF16 = jnp.float32, jnp.bfloat16
NEG = -1e30
LANES = 128
STATS = 3 * H
DIGIT = 32
VMEM_LIMIT = 58 * 1024 * 1024


def nn(a, b):
    return jnp.dot(a, b, preferred_element_type=F32)


def nt(a, b):
    return lax.dot_general(a, b, (((1,), (1,)), ((), ())), preferred_element_type=F32)


def tn(a, b):
    return lax.dot_general(a, b, (((0,), (0,)), ((), ())), preferred_element_type=F32)


def two_heads(pair):
    lane = lax.broadcasted_iota(jnp.int32, pair.shape, 1)
    zero = jnp.zeros_like(pair)
    return jnp.concatenate(
        [jnp.where(lane < LANES // 2, pair, zero), jnp.where(lane >= LANES // 2, pair, zero)], axis=0
    )


def own_heads(both):
    half, rows = both.shape[0] // 2, both.shape[1] // 2
    return jnp.concatenate([both[:half, :rows], both[half:, rows:]], axis=0)


def bias_of(tile):
    bias = jnp.where(tile != 0, 0.0, NEG).astype(F32).T
    return jnp.concatenate([bias, bias], axis=1)


def split_stat(row):
    return row[:, : row.shape[1] // 2], row[:, row.shape[1] // 2 :]


def near_kernel(near_ids, meta, q_ref, tile_ref, k_ref, v_ref, out_ref, sums_ref, bias_scr):
    i = pl.program_id(0)
    for j in range(NBR):
        bias_scr[j] = bias_of(tile_ref[0, j])
    ids = [near_ids[i, j] for j in range(NBR)]
    pairs = q_ref.shape[1] // LANES

    def scores_of(c):
        cols = slice(c * LANES, (c + 1) * LANES)
        qz = two_heads(q_ref[:, cols])
        return jnp.concatenate([nt(k_ref[ids[j], :, cols], qz) + bias_scr[j] for j in range(NBR)], axis=0)

    ready = scores_of(0)
    for c in range(pairs):
        cols = slice(c * LANES, (c + 1) * LANES)
        scores, ready = ready, scores_of(c + 1) if c + 1 < pairs else None
        peak = jnp.max(scores, axis=0, keepdims=True)
        terms = jnp.exp(scores - peak)
        total = jnp.sum(terms, axis=0, keepdims=True)
        values = jnp.concatenate([v_ref[ids[j], :, cols] for j in range(NBR)], axis=0)
        out_ref[0, cols, :] = own_heads(tn(values, terms.astype(BF16)))
        store_rows(sums_ref, c, (peak, total))


def store_rows(ref, c, rows, b=0):
    for s, row in enumerate(rows):
        for e, part in enumerate(split_stat(row)):
            at = s * H + 2 * c + e
            ref[b, at : at + 1, :] = part


def merge_kernel(q_ref, cot_t_ref, fk_ref, fv_ref, out_ref, sums_ref, att_ref, stats_ref):
    mid = LANES // 2
    bs = fk_ref.shape[1]
    units = [(b, c) for b in range(fk_ref.shape[0]) for c in range(q_ref.shape[1] // LANES)]
    cols = [slice(c * LANES, (c + 1) * LANES) for _, c in units]
    scores = [
        nt(fk_ref[b, :, cols[u]], two_heads(q_ref[b * bs : (b + 1) * bs, cols[u]])) for u, (b, c) in enumerate(units)
    ]
    peaks, kepts, invs, lows = [], [], [], []
    for u, (b, c) in enumerate(units):
        near_peak, near_total = load_rows(sums_ref, c, 2, b)
        peak = jnp.maximum(near_peak, jnp.max(scores[u], axis=0, keepdims=True))
        terms = jnp.exp(scores[u] - peak)
        kept = jnp.exp(near_peak - peak)
        inv = 1.0 / (near_total * kept + jnp.sum(terms, axis=0, keepdims=True))
        lows.append((terms * inv).astype(BF16))
        peaks.append(peak)
        kepts.append(kept)
        invs.append(inv)
    far_outs = [own_heads(tn(fv_ref[b, :, cols[u]], lows[u])) for u, (b, c) in enumerate(units)]
    for u, (b, c) in enumerate(units):
        first, second = split_stat(kepts[u] * invs[u])
        near_out = out_ref[b, cols[u], :]
        near_out = jnp.concatenate([near_out[:mid] * first, near_out[mid:] * second], axis=0)
        att = (far_outs[u] + near_out).astype(BF16)
        att_ref[b, cols[u], :] = att
        prod = cot_t_ref[b, cols[u], :].astype(F32) * att.astype(F32)
        delta = jnp.concatenate(
            [jnp.sum(prod[:mid], axis=0, keepdims=True), jnp.sum(prod[mid:], axis=0, keepdims=True)], axis=1
        )
        store_rows(stats_ref, c, (peaks[u], invs[u], delta), b)


def deal(dw_scr, kept_ref, given_ref, core):
    groups, span = kept_ref.shape[0], kept_ref.shape[3] // 2
    for g in range(groups):
        for t in range(2):
            at = (t * groups + g) * span
            kept_ref[g, :, :, t * span : (t + 1) * span] = dw_scr[:, core, :, at : at + span]
            given_ref[g, :, :, t * span : (t + 1) * span] = dw_scr[:, 1 - core, :, at : at + span]


def own_kernel(near_ids, meta, q_ref, cot_ref, tile_ref, stats_ref, k_ref, v_ref, fk_ref, fv_ref,
               xt_ref, ct_ref, att_ref, dq_ref, acc_ref, kept_ref, given_ref, slot_ref, p_scr, ds_scr, qz_scr, cz_scr, bias_scr,
               dw_scr):
    i = pl.program_id(0)
    bs, width = q_ref.shape
    pairs = width // LANES
    own = acc_ref.shape[0]

    @pl.when(i == 0)
    def _():
        acc_ref[...] = jnp.zeros_like(acc_ref)
        dw_scr[...] = jnp.zeros_like(dw_scr)

    slot_ref[...] = stats_ref[...]
    for j in range(NBR):
        bias_scr[j] = bias_of(tile_ref[0, j])
    ids = [near_ids[i, j] for j in range(NBR)]

    def products(c):
        cols = slice(c * LANES, (c + 1) * LANES)
        qz = two_heads(q_ref[:, cols])
        cz = two_heads(cot_ref[:, cols])
        qz_scr[c] = qz
        cz_scr[c] = cz
        scores = [nt(k_ref[ids[j], :, cols], qz) + bias_scr[j] for j in range(NBR)] + [nt(fk_ref[0, :, cols], qz)]
        grads = [nt(v_ref[ids[j], :, cols], cz) for j in range(NBR)] + [nt(fv_ref[0, :, cols], cz)]
        return scores, grads

    ready = products(0)
    for c in range(pairs):
        cols = slice(c * LANES, (c + 1) * LANES)
        (scores, grads), ready = ready, products(c + 1) if c + 1 < pairs else None
        peak, inv, delta = load_rows(stats_ref, c, 3)
        parts = []
        for j in range(NBR + 1):
            rows = slice(j * bs, (j + 1) * bs)
            probs = jnp.exp(scores[j] - peak) * inv
            parts.append((probs * (grads[j] - delta)).astype(BF16))
            if j < NBR:
                p_scr[c, rows, :] = probs.astype(BF16)
                ds_scr[c, rows, :] = parts[j]
        keys = jnp.concatenate([k_ref[ids[j], :, cols] for j in range(NBR)] + [fk_ref[0, :, cols]], axis=0)
        dq_ref[0, cols, :] = (own_heads(tn(keys, jnp.concatenate(parts, axis=0))) * 0.125).astype(BF16)
    half = dw_scr.shape[:3] + (width,)
    dw_scr[:, :, :, :width] += nt(ct_ref[0], att_ref[0]).reshape(half)
    dw_scr[:, :, :, width:] += nt(xt_ref[0], dq_ref[0]).reshape(half)

    for j in range(NBR):

        @pl.when(ids[j] < own)
        def _(j=j):
            n = ids[j]
            for c in range(pairs):
                cols = slice(c * LANES, (c + 1) * LANES)
                vcols = slice(width + c * LANES, width + (c + 1) * LANES)
                rows = slice(j * bs, (j + 1) * bs)
                acc_ref[n, :, cols] += nn(ds_scr[c, rows, :], qz_scr[c])
                acc_ref[n, :, vcols] += nn(p_scr[c, rows, :], cz_scr[c])

    @pl.when(i == own - 1)
    def _():
        deal(dw_scr, kept_ref, given_ref, meta[1 + own])


def load_rows(ref, c, count, b=0):
    return [
        jnp.concatenate(
            [ref[b, s * H + 2 * c : s * H + 2 * c + 1, :], ref[b, s * H + 2 * c + 1 : s * H + 2 * c + 2, :]], axis=1
        )
        for s in range(count)
    ]


def key_terms(ks, vs, qzs, czs, bias, stats):
    scores = [nt(k, qz) for k, qz in zip(ks, qzs)]
    grads = [nt(v, cz) for v, cz in zip(vs, czs)]
    probs = [
        jnp.exp((s if bias is None else s + bias) - peak) * inv for s, (peak, inv, _) in zip(scores, stats)
    ]
    ds = [(p * (g - delta)).astype(BF16) for p, g, (_, _, delta) in zip(probs, grads, stats)]
    return [nn(d, qz) for d, qz in zip(ds, qzs)], [nn(p.astype(BF16), cz) for p, cz in zip(probs, czs)]


def peer_kernel(near_ids, meta, q_ref, cot_ref, stats_ref, tile_ref, k_ref, v_ref, acc_in, acc_ref, qz_scr, cz_scr):
    i = pl.program_id(0)
    pairs = q_ref.shape[1] // LANES
    width = q_ref.shape[1]
    own = acc_ref.shape[0]

    @pl.when(i == 0)
    def _():
        acc_ref[...] = acc_in[...]

    for c in range(pairs):
        cols = slice(c * LANES, (c + 1) * LANES)
        qz_scr[c] = two_heads(q_ref[:, cols])
        cz_scr[c] = two_heads(cot_ref[:, cols])
    for j in range(NBR):
        n = near_ids[own + i, j]

        @pl.when(n < own)
        def _(j=j, n=n):
            every = range(pairs)
            cols = [slice(c * LANES, (c + 1) * LANES) for c in every]
            dks, dvs = key_terms(
                [k_ref[n, :, cols[c]] for c in every], [v_ref[n, :, cols[c]] for c in every],
                [qz_scr[c] for c in every], [cz_scr[c] for c in every], bias_of(tile_ref[0, j]),
                [load_rows(stats_ref, c, 3) for c in every],
            )
            for c in every:
                acc_ref[n, :, cols[c]] += dks[c]
                acc_ref[n, :, width + c * LANES : width + (c + 1) * LANES] += dvs[c]


def far_kernel(meta, q_ref, cot_ref, first_ref, second_ref, k_ref, v_ref, acc_ref, xt_ref, dkv_ref, kept_ref,
               given_ref, dw_scr):
    bs, width = k_ref.shape[1:]
    i = pl.program_id(0)

    @pl.when(i == 0)
    def _():
        dw_scr[...] = jnp.zeros_like(dw_scr)

    units = [(b, c) for b in range(2) for c in range(width // LANES)]
    cols = [slice(c * LANES, (c + 1) * LANES) for _, c in units]
    rows = [slice(b * bs, (b + 1) * bs) for b, _ in units]
    every = range(len(units))
    dks, dvs = key_terms(
        [k_ref[units[u][0], :, cols[u]] for u in every], [v_ref[units[u][0], :, cols[u]] for u in every],
        [two_heads(q_ref[rows[u], cols[u]]) for u in every], [two_heads(cot_ref[rows[u], cols[u]]) for u in every],
        None, [load_rows((first_ref, second_ref)[b], c, 3) for b, c in units],
    )
    for u, (b, c) in enumerate(units):
        vcols = slice(width + c * LANES, width + (c + 1) * LANES)
        dkv_ref[rows[u], cols[u]] = (acc_ref[b, :, cols[u]] + dks[u].astype(BF16).astype(F32)).astype(BF16)
        dkv_ref[rows[u], vcols] = (acc_ref[b, :, vcols] + dvs[u].astype(BF16).astype(F32)).astype(BF16)
    xt = jnp.concatenate([xt_ref[0], xt_ref[1]], axis=1)
    dw_scr[...] += nn(xt, dkv_ref[...]).reshape(dw_scr.shape)

    @pl.when(i == pl.num_programs(0) - 1)
    def _():
        deal(dw_scr, kept_ref, given_ref, meta[1 + 2 * pl.num_programs(0)])


def project_kernel(x_ref, w_ref, *rest):
    rest[-1][...] = nn(x_ref[...], w_ref[...]).astype(BF16)


def call(kernel, scalars, steps, in_specs, out_specs, out_shape, scratch, flops, touched, name, aliases={}):
    return pl.pallas_call(
        kernel,
        grid_spec=pltpu.PrefetchScalarGridSpec(
            num_scalar_prefetch=scalars, grid=(steps,), in_specs=in_specs, out_specs=out_specs, scratch_shapes=scratch
        ),
        out_shape=out_shape,
        input_output_aliases=aliases,
        compiler_params=pltpu.CompilerParams(dimension_semantics=("arbitrary",), vmem_limit_bytes=VMEM_LIMIT),
        cost_estimate=pl.CostEstimate(flops=flops, bytes_accessed=touched, transcendentals=0),
        name=name,
    )


def once(shape, at=0):
    return pl.BlockSpec(shape, lambda i, *s: (at,) + (0,) * (len(shape) - 1), pipeline_mode=pl.Buffered(1))


def body(node_feats, w_qkv, w_out, neighbours, tiles, partner, layer_cot):
    rows, width = node_feats.shape
    doms, groups = lax.axis_size("dom"), lax.axis_size("head")
    devices = doms * groups
    blocks = partner.shape[0]
    own = blocks // groups
    bs = tiles.shape[2]
    span = width // groups
    half = lax.axis_index("head")
    base = half * own

    near_ids = jnp.roll((neighbours - base) % blocks, -base, axis=0)
    mine = lax.dynamic_slice_in_dim(partner, base, own, 0)
    core = lax.axis_index("dom") % 2
    meta = jnp.concatenate([base[None].astype(jnp.int32), mine // own, core[None].astype(jnp.int32)])

    w_by = w_qkv.reshape(width, groups, 3, span).transpose(2, 0, 1, 3).reshape(3, width, width)
    w_all = jnp.concatenate([w_by[0] * jnp.asarray(0.125, BF16), w_by[1], w_by[2]], axis=1)

    def swap(x):
        return lax.ppermute(x, "head", [(0, 1), (1, 0)])

    def exchange(x):
        return lax.all_to_all(x, DEVICES, split_axis=0, concat_axis=0, tiled=True)

    def spread(x):
        return x.reshape(own, bs, width).transpose(1, 0, 2)

    def gathered(x):
        return jnp.dot(one_hot, x.reshape(-1, width), preferred_element_type=F32).astype(BF16).reshape(
            devices, own, width
        )

    digits = jnp.stack([mine // DIGIT, mine % DIGIT], axis=1).astype(BF16)
    digits = jnp.pad(digits, ((0, 0), (0, LANES - 2)))
    digits = jnp.broadcast_to(digits[None], (devices, own, LANES))
    first_hop = jnp.concatenate([spread(node_feats), digits], axis=2)
    rows_in = exchange(first_hop)
    peer_feats = swap(node_feats)
    cot = jnp.dot(layer_cot, w_out.T, preferred_element_type=F32).astype(BF16)
    cot_rows = spread(cot)
    cot_t = jnp.einsum("ck,brk->bcr", w_out, layer_cot.reshape(own, bs, width), preferred_element_type=F32).astype(BF16)

    hold = pl.BlockSpec(memory_space=pl.ANY)

    def project(feats, total, at, carried, name):
        return call(
            project_kernel, 0, 3,
            [
                once((rows, width)),
                pl.BlockSpec((width, width), lambda i: (0, i)),
            ]
            + [hold] * len(carried),
            [
                pl.BlockSpec((rows, width), lambda i: (at, i)),
            ],
            [jax.ShapeDtypeStruct((total * bs, 3 * width), BF16)],
            [], 2 * rows * width * 3 * width, 6 << 20, name, aliases={2: 0} if carried else {},
        )(feats, w_all, *carried)[0]

    own_part = project(node_feats, blocks, 0, (), "project_own")
    feats_t = node_feats.reshape(own, bs, width).transpose(0, 2, 1)
    out_t = layer_cot.reshape(own, bs, width).transpose(0, 2, 1)
    rows_in, cot_rows, own_part, peer_feats, cot_t, feats_t, out_t = lax.optimization_barrier(
        (rows_in, cot_rows, own_part, peer_feats, cot_t, feats_t, out_t)
    )

    weigh = jnp.pad(jnp.asarray([DIGIT, 1], F32), (0, LANES - 2))
    ids = jnp.sum(rows_in.reshape(-1, width + LANES)[:, width:].astype(F32) * weigh[None], axis=1, keepdims=True)
    one_hot = (ids == jnp.arange(ids.shape[0], dtype=jnp.int32)[None, :].astype(F32)).astype(BF16)
    second = jnp.concatenate([gathered(rows_in[:, :, :width]), cot_rows], axis=2)
    second = exchange(second)
    part_qkv = project(peer_feats, blocks, 1, (own_part,), "project_peer")
    part_blk = part_qkv.reshape(blocks, bs, 3 * width)
    pair_flops = 2 * bs * bs * width * 2
    step = lambda i, *s: (i, 0)
    row_step = lambda i, *s: (i, 0, 0)
    rows_spec = pl.BlockSpec((bs, width), step)
    tile_spec = pl.BlockSpec((1, NBR, bs, bs), lambda i, ids, meta: (meta[0] + i, 0, 0, 0))
    k_spec = pl.BlockSpec((blocks, bs, width), lambda i, *s: (0, 0, 1), pipeline_mode=pl.Buffered(1))
    v_spec = pl.BlockSpec((blocks, bs, width), lambda i, *s: (0, 0, 2), pipeline_mode=pl.Buffered(1))
    stats_spec = pl.BlockSpec((1, STATS, bs), row_step)
    turned_spec = pl.BlockSpec((1, width, bs), row_step)
    near_out, sums = call(
        near_kernel, 2, own,
        [rows_spec, tile_spec, k_spec, v_spec],
        [pl.BlockSpec((1, width, bs), row_step), pl.BlockSpec((1, 2 * H, bs), row_step)],
        [jax.ShapeDtypeStruct((own, width, bs), F32), jax.ShapeDtypeStruct((own, 2 * H, bs), F32)],
        [pltpu.VMEM((NBR, bs, 2 * bs), F32)],
        own * 16 * pair_flops, 10 << 20, "near_forward",
    )(near_ids, meta, part_qkv, tiles, part_blk, part_blk)
    second, near_out, sums, cot_out = lax.optimization_barrier((second, near_out, sums, cot))

    picked = gathered(second[:, :, width:])
    far_feats = second[:, :, :width].transpose(1, 0, 2).reshape(rows, width)
    picked, far_feats = lax.optimization_barrier((picked, far_feats))
    far_cot = exchange(picked)
    far_qkv = jnp.dot(far_feats, w_all, preferred_element_type=F32).astype(BF16)
    far_blk = far_qkv.reshape(own, bs, 3 * width)
    peer_cot = swap(cot_out)

    far_k_spec = pl.BlockSpec((1, bs, width), lambda i, *s: (i, 0, 1))
    far_v_spec = pl.BlockSpec((1, bs, width), lambda i, *s: (i, 0, 2))
    pair_rows = pl.BlockSpec((2 * bs, width), step)
    pair_turned = pl.BlockSpec((2, width, bs), row_step)
    pair_k = pl.BlockSpec((2, bs, width), lambda i, *s: (i, 0, 1))
    pair_v = pl.BlockSpec((2, bs, width), lambda i, *s: (i, 0, 2))
    att, stats = call(
        merge_kernel, 0, own // 2,
        [pair_rows, pair_turned, pair_k, pair_v, pair_turned, pl.BlockSpec((2, 2 * H, bs), row_step)],
        [pair_turned, pl.BlockSpec((2, STATS, bs), row_step)],
        [jax.ShapeDtypeStruct((own, width, bs), BF16), jax.ShapeDtypeStruct((own, STATS, bs), F32)],
        [], own * 4 * pair_flops, 6 << 20, "far_forward",
    )(part_qkv, cot_t, far_blk, far_blk, near_out, sums)
    peer_stats = swap(stats)
    pairs = width // LANES
    piece = (groups, doms // 2, width // doms, width)
    piece_spec = pl.BlockSpec(piece, lambda i, *s: (0, 0, 0, 0), pipeline_mode=pl.Buffered(1))
    piece_out = jax.ShapeDtypeStruct(piece, F32)
    dw_scratch = pltpu.VMEM((doms // 2, 2, width // doms, 2 * width), F32)
    dq, acc, kept, given, slots = call(
        own_kernel, 2, own,
        [rows_spec, rows_spec, tile_spec, stats_spec, k_spec, v_spec, far_k_spec, far_v_spec,
         turned_spec, turned_spec, turned_spec],
        [turned_spec, pl.BlockSpec((own, bs, 2 * width), lambda i, *s: (0, 0, 0)), piece_spec, piece_spec,
         pl.BlockSpec((1, STATS, bs), lambda i, ids, meta: (meta[1 + i], 0, 0))],
        [
            jax.ShapeDtypeStruct((own, width, bs), BF16),
            jax.ShapeDtypeStruct((own, bs, 2 * width), F32),
            piece_out,
            piece_out,
            jax.ShapeDtypeStruct((devices, STATS, bs), F32),
        ],
        [
            pltpu.VMEM((pairs, NBR * bs, 2 * bs), BF16),
            pltpu.VMEM((pairs, NBR * bs, 2 * bs), BF16),
            pltpu.VMEM((pairs, 2 * bs, LANES), BF16),
            pltpu.VMEM((pairs, 2 * bs, LANES), BF16),
            pltpu.VMEM((NBR, bs, 2 * bs), F32),
            dw_scratch,
        ],
        own * 24 * pair_flops, 30 << 20, "own_backward",
    )(near_ids, meta, part_qkv, cot, tiles, stats, part_blk, part_blk, far_blk, far_blk,
      feats_t, out_t, att)
    acc, peer_stats, peer_cot, far_cot, slots = lax.optimization_barrier((acc, peer_stats, peer_cot, far_cot, slots))
    far_slots = exchange(slots)
    far_cot = far_cot.transpose(1, 0, 2).reshape(rows, width)

    layer_out = jnp.einsum("bar,ac->brc", att, w_out, preferred_element_type=F32).astype(BF16).reshape(rows, width)

    def paired(kept, given):
        return (kept + lax.ppermute(given, "dom", [(d, d ^ 1) for d in range(doms)])).astype(BF16)

    early = paired(kept, given)

    (acc,) = call(
        peer_kernel, 2, own,
        [
            pl.BlockSpec((bs, width), lambda i, *s: (own + i, 0)),
            pl.BlockSpec((bs, width), step),
            pl.BlockSpec((1, STATS, bs), lambda i, *s: (i, 0, 0)),
            pl.BlockSpec((1, NBR, bs, bs), lambda i, ids, meta: (own - meta[0] + i, 0, 0, 0)),
            pl.BlockSpec((own, bs, width), lambda i, *s: (0, 0, 1), pipeline_mode=pl.Buffered(1)),
            pl.BlockSpec((own, bs, width), lambda i, *s: (0, 0, 2), pipeline_mode=pl.Buffered(1)),
            once((own, bs, 2 * width)),
        ],
        [pl.BlockSpec((own, bs, 2 * width), lambda i, *s: (0, 0, 0))],
        [jax.ShapeDtypeStruct((own, bs, 2 * width), F32)],
        [
            pltpu.VMEM((width // LANES, 2 * bs, LANES), BF16),
            pltpu.VMEM((width // LANES, 2 * bs, LANES), BF16),
        ],
        own * 16 * pair_flops, 20 << 20, "peer_queries",
    )(near_ids, meta, part_qkv, peer_cot, peer_stats, tiles, part_blk, part_blk, acc)

    dkv, kept, given = call(
        far_kernel, 1, own // 2,
        [
            pair_rows,
            pair_rows,
            pl.BlockSpec((1, STATS, bs), lambda i, meta: (meta[1 + 2 * i], 0, 0)),
            pl.BlockSpec((1, STATS, bs), lambda i, meta: (meta[2 + 2 * i], 0, 0)),
            pair_k,
            pair_v,
            pl.BlockSpec((2, bs, 2 * width), row_step),
            pair_turned,
        ],
        [pl.BlockSpec((2 * bs, 2 * width), step), piece_spec, piece_spec],
        [jax.ShapeDtypeStruct((rows, 2 * width), BF16), piece_out, piece_out],
        [dw_scratch], own * 8 * pair_flops, 10 << 20, "far_queries",
    )(meta, far_qkv, far_cot, far_slots, far_slots, part_blk, part_blk, acc, feats_t)

    split = jnp.concatenate([early, paired(kept, given)], axis=2).reshape(devices // 2, 2 * width // doms, width)
    same_core = [[d * groups + g for g in range(groups) for d in range(e, doms, 2)] for e in range(2)]
    moved = lax.all_to_all(split, DEVICES, split_axis=0, concat_axis=0, axis_index_groups=same_core, tiled=True)
    summed = jnp.sum(moved.astype(F32), axis=0)
    w_plain = w_by.transpose(1, 0, 2).reshape(width, 3 * width)
    feat_grad = (
        jnp.einsum("bcr,dc->brd", dq, w_plain[:, :width], preferred_element_type=F32).reshape(rows, width)
        + lax.dot_general(dkv, w_plain[:, width:], (((1,), (1,)), ((), ())), preferred_element_type=F32)
    ).astype(BF16)
    deep = width // doms
    dw_out = summed[:deep, :span].T
    dw_qkv = jnp.concatenate([summed[:deep, span:], summed[deep:]], axis=1)
    return (layer_out, feat_grad, dw_qkv, dw_out)


def solution(mesh):
    placed = (
        P(DEVICES, None),
        P(),
        P(),
        P("dom", None),
        P("dom", None, None, None),
        P("dom"),
        P(DEVICES, None),
    )
    return jax.shard_map(
        body,
        mesh=mesh,
        in_specs=placed,
        out_specs=(P(DEVICES, None), P(DEVICES, None), P("dom", "head"), P("head", "dom")),
        check_vma=False,
    )
```

```python
import jax
import jax.numpy as jnp
from jax import lax
from jax.experimental import pallas as pl
from jax.experimental.pallas import tpu as pltpu
from jax.sharding import PartitionSpec as P

H = 8
NBR = 4
DEVICES = ("dom", "head")
F32, BF16 = jnp.float32, jnp.bfloat16
NEG = -1e30
LANES = 128
STATS = 3 * H
DIGIT = 32
VMEM_LIMIT = 58 * 1024 * 1024


def nn(a, b):
    return jnp.dot(a, b, preferred_element_type=F32)


def nt(a, b):
    return lax.dot_general(a, b, (((1,), (1,)), ((), ())), preferred_element_type=F32)


def tn(a, b):
    return lax.dot_general(a, b, (((0,), (0,)), ((), ())), preferred_element_type=F32)


def two_heads(pair):
    lane = lax.broadcasted_iota(jnp.int32, pair.shape, 1)
    zero = jnp.zeros_like(pair)
    return jnp.concatenate(
        [jnp.where(lane < LANES // 2, pair, zero), jnp.where(lane >= LANES // 2, pair, zero)], axis=0
    )


def own_heads(both):
    half, rows = both.shape[0] // 2, both.shape[1] // 2
    return jnp.concatenate([both[:half, :rows], both[half:, rows:]], axis=0)


def bias_of(tile):
    bias = jnp.where(tile != 0, 0.0, NEG).astype(F32).T
    return jnp.concatenate([bias, bias], axis=1)


def split_stat(row):
    return row[:, : row.shape[1] // 2], row[:, row.shape[1] // 2 :]


def near_kernel(near_ids, meta, q_ref, tile_ref, k_ref, v_ref, out_ref, sums_ref, bias_scr):
    i = pl.program_id(0)
    for j in range(NBR):
        bias_scr[j] = bias_of(tile_ref[0, j])
    ids = [near_ids[i, j] for j in range(NBR)]
    pairs = q_ref.shape[1] // LANES

    def scores_of(c):
        cols = slice(c * LANES, (c + 1) * LANES)
        qz = two_heads(q_ref[:, cols])
        return jnp.concatenate([nt(k_ref[ids[j], :, cols], qz) + bias_scr[j] for j in range(NBR)], axis=0)

    ready = scores_of(0)
    for c in range(pairs):
        cols = slice(c * LANES, (c + 1) * LANES)
        scores, ready = ready, scores_of(c + 1) if c + 1 < pairs else None
        peak = jnp.max(scores, axis=0, keepdims=True)
        terms = jnp.exp(scores - peak)
        total = jnp.sum(terms, axis=0, keepdims=True)
        values = jnp.concatenate([v_ref[ids[j], :, cols] for j in range(NBR)], axis=0)
        out_ref[0, cols, :] = own_heads(tn(values, terms.astype(BF16)))
        store_rows(sums_ref, c, (peak, total))


def store_rows(ref, c, rows, b=0):
    for s, row in enumerate(rows):
        for e, part in enumerate(split_stat(row)):
            at = s * H + 2 * c + e
            ref[b, at : at + 1, :] = part


def merge_kernel(q_ref, cot_t_ref, fk_ref, fv_ref, out_ref, sums_ref, att_ref, stats_ref):
    mid = LANES // 2
    bs = fk_ref.shape[1]
    units = [(b, c) for b in range(fk_ref.shape[0]) for c in range(q_ref.shape[1] // LANES)]
    cols = [slice(c * LANES, (c + 1) * LANES) for _, c in units]
    scores = [
        nt(fk_ref[b, :, cols[u]], two_heads(q_ref[b * bs : (b + 1) * bs, cols[u]])) for u, (b, c) in enumerate(units)
    ]
    peaks, kepts, invs, lows = [], [], [], []
    for u, (b, c) in enumerate(units):
        near_peak, near_total = load_rows(sums_ref, c, 2, b)
        peak = jnp.maximum(near_peak, jnp.max(scores[u], axis=0, keepdims=True))
        terms = jnp.exp(scores[u] - peak)
        kept = jnp.exp(near_peak - peak)
        inv = 1.0 / (near_total * kept + jnp.sum(terms, axis=0, keepdims=True))
        lows.append((terms * inv).astype(BF16))
        peaks.append(peak)
        kepts.append(kept)
        invs.append(inv)
    far_outs = [own_heads(tn(fv_ref[b, :, cols[u]], lows[u])) for u, (b, c) in enumerate(units)]
    for u, (b, c) in enumerate(units):
        first, second = split_stat(kepts[u] * invs[u])
        near_out = out_ref[b, cols[u], :]
        near_out = jnp.concatenate([near_out[:mid] * first, near_out[mid:] * second], axis=0)
        att = (far_outs[u] + near_out).astype(BF16)
        att_ref[b, cols[u], :] = att
        prod = cot_t_ref[b, cols[u], :].astype(F32) * att.astype(F32)
        delta = jnp.concatenate(
            [jnp.sum(prod[:mid], axis=0, keepdims=True), jnp.sum(prod[mid:], axis=0, keepdims=True)], axis=1
        )
        store_rows(stats_ref, c, (peaks[u], invs[u], delta), b)


def deal(dw_scr, kept_ref, given_ref, core):
    groups, span = kept_ref.shape[0], kept_ref.shape[3] // 2
    for g in range(groups):
        for t in range(2):
            at = (t * groups + g) * span
            kept_ref[g, :, :, t * span : (t + 1) * span] = dw_scr[:, core, :, at : at + span]
            given_ref[g, :, :, t * span : (t + 1) * span] = dw_scr[:, 1 - core, :, at : at + span]


def own_kernel(near_ids, meta, q_ref, cot_ref, tile_ref, stats_ref, k_ref, v_ref, fk_ref, fv_ref,
               xt_ref, ct_ref, att_ref, dq_ref, acc_ref, kept_ref, given_ref, slot_ref, p_scr, ds_scr, qz_scr, cz_scr, bias_scr,
               dw_scr):
    i = pl.program_id(0)
    bs, width = q_ref.shape
    pairs = width // LANES
    own = acc_ref.shape[0]

    @pl.when(i == 0)
    def _():
        acc_ref[...] = jnp.zeros_like(acc_ref)
        dw_scr[...] = jnp.zeros_like(dw_scr)

    slot_ref[...] = stats_ref[...]
    for j in range(NBR):
        bias_scr[j] = bias_of(tile_ref[0, j])
    ids = [near_ids[i, j] for j in range(NBR)]

    def products(c):
        cols = slice(c * LANES, (c + 1) * LANES)
        qz = two_heads(q_ref[:, cols])
        cz = two_heads(cot_ref[:, cols])
        qz_scr[c] = qz
        cz_scr[c] = cz
        scores = [nt(k_ref[ids[j], :, cols], qz) + bias_scr[j] for j in range(NBR)] + [nt(fk_ref[0, :, cols], qz)]
        grads = [nt(v_ref[ids[j], :, cols], cz) for j in range(NBR)] + [nt(fv_ref[0, :, cols], cz)]
        return scores, grads

    ready = products(0)
    for c in range(pairs):
        cols = slice(c * LANES, (c + 1) * LANES)
        (scores, grads), ready = ready, products(c + 1) if c + 1 < pairs else None
        peak, inv, delta = load_rows(stats_ref, c, 3)
        parts = []
        for j in range(NBR + 1):
            rows = slice(j * bs, (j + 1) * bs)
            probs = jnp.exp(scores[j] - peak) * inv
            parts.append((probs * (grads[j] - delta)).astype(BF16))
            if j < NBR:
                p_scr[c, rows, :] = probs.astype(BF16)
                ds_scr[c, rows, :] = parts[j]
        keys = jnp.concatenate([k_ref[ids[j], :, cols] for j in range(NBR)] + [fk_ref[0, :, cols]], axis=0)
        dq_ref[0, cols, :] = (own_heads(tn(keys, jnp.concatenate(parts, axis=0))) * 0.125).astype(BF16)
    half = dw_scr.shape[:3] + (width,)
    dw_scr[:, :, :, :width] += nt(ct_ref[0], att_ref[0]).reshape(half)
    dw_scr[:, :, :, width:] += nt(xt_ref[0], dq_ref[0]).reshape(half)

    for j in range(NBR):

        @pl.when(ids[j] < own)
        def _(j=j):
            n = ids[j]
            for c in range(pairs):
                cols = slice(c * LANES, (c + 1) * LANES)
                vcols = slice(width + c * LANES, width + (c + 1) * LANES)
                rows = slice(j * bs, (j + 1) * bs)
                acc_ref[n, :, cols] += nn(ds_scr[c, rows, :], qz_scr[c])
                acc_ref[n, :, vcols] += nn(p_scr[c, rows, :], cz_scr[c])

    @pl.when(i == own - 1)
    def _():
        deal(dw_scr, kept_ref, given_ref, meta[1 + own])


def load_rows(ref, c, count, b=0):
    return [
        jnp.concatenate(
            [ref[b, s * H + 2 * c : s * H + 2 * c + 1, :], ref[b, s * H + 2 * c + 1 : s * H + 2 * c + 2, :]], axis=1
        )
        for s in range(count)
    ]


def key_terms(ks, vs, qzs, czs, biases, stats):
    scores = [nt(k, qz) for k, qz in zip(ks, qzs)]
    grads = [nt(v, cz) for v, cz in zip(vs, czs)]
    if biases is not None:
        scores = [s + bias for s, bias in zip(scores, biases)]
    probs = [jnp.exp(s - peak) * inv for s, (peak, inv, _) in zip(scores, stats)]
    ds = [(p * (g - delta)).astype(BF16) for p, g, (_, _, delta) in zip(probs, grads, stats)]
    return [nn(d, qz) for d, qz in zip(ds, qzs)], [nn(p.astype(BF16), cz) for p, cz in zip(probs, czs)]


def peer_kernel(near_ids, meta, q_ref, cot_ref, stats_ref, tile_ref, k_ref, v_ref, acc_in, acc_ref, qz_scr, cz_scr):
    i = pl.program_id(0)
    pairs = q_ref.shape[1] // LANES
    width = q_ref.shape[1]
    own = acc_ref.shape[0]

    @pl.when(i == 0)
    def _():
        acc_ref[...] = acc_in[...]

    for c in range(pairs):
        cols = slice(c * LANES, (c + 1) * LANES)
        qz_scr[c] = two_heads(q_ref[:, cols])
        cz_scr[c] = two_heads(cot_ref[:, cols])
    ids = [near_ids[own + i, j] for j in range(NBR)]
    taken = [jnp.where(n < own, 1, 0) for n in ids]
    before = [sum(taken[:j], 0) for j in range(NBR)]
    count = sum(taken)
    order = [sum(jnp.where((before[j] == k) & (ids[j] < own), j, 0) for j in range(NBR)) for k in range(NBR)]
    every = range(pairs)
    cols = [slice(c * LANES, (c + 1) * LANES) for c in every]
    for k in range(0, NBR, 2):

        @pl.when(count > k)
        def _(k=k):
            both = count > k + 1
            slots = (order[k], jnp.where(both, order[k + 1], order[k]))
            weights = (None, jnp.where(both, 1.0, 0.0).astype(F32))
            blocks = [near_ids[own + i, j] for j in slots]
            ks, vs, biases, stats = [], [], [], []
            for n, j, weight in zip(blocks, slots, weights):
                ks += [k_ref[n, :, cols[c]] for c in every]
                vs += [v_ref[n, :, cols[c]] for c in every]
                biases += [bias_of(tile_ref[0, j])] * pairs
                for c in every:
                    peak, inv, delta = load_rows(stats_ref, c, 3)
                    stats.append((peak, inv if weight is None else inv * weight, delta))
            dks, dvs = key_terms(
                ks, vs, [qz_scr[c] for c in every] * 2, [cz_scr[c] for c in every] * 2, biases, stats
            )
            for b, n in enumerate(blocks):
                for c in every:
                    acc_ref[n, :, cols[c]] += dks[b * pairs + c]
                    acc_ref[n, :, width + c * LANES : width + (c + 1) * LANES] += dvs[b * pairs + c]


def far_kernel(meta, q_ref, cot_ref, first_ref, second_ref, k_ref, v_ref, acc_ref, xt_ref, dkv_ref, kept_ref,
               given_ref, dw_scr):
    bs, width = k_ref.shape[1:]
    i = pl.program_id(0)

    @pl.when(i == 0)
    def _():
        dw_scr[...] = jnp.zeros_like(dw_scr)

    units = [(b, c) for b in range(2) for c in range(width // LANES)]
    cols = [slice(c * LANES, (c + 1) * LANES) for _, c in units]
    rows = [slice(b * bs, (b + 1) * bs) for b, _ in units]
    every = range(len(units))
    dks, dvs = key_terms(
        [k_ref[units[u][0], :, cols[u]] for u in every], [v_ref[units[u][0], :, cols[u]] for u in every],
        [two_heads(q_ref[rows[u], cols[u]]) for u in every], [two_heads(cot_ref[rows[u], cols[u]]) for u in every],
        None, [load_rows((first_ref, second_ref)[b], c, 3) for b, c in units],
    )
    for u, (b, c) in enumerate(units):
        vcols = slice(width + c * LANES, width + (c + 1) * LANES)
        dkv_ref[rows[u], cols[u]] = (acc_ref[b, :, cols[u]] + dks[u].astype(BF16).astype(F32)).astype(BF16)
        dkv_ref[rows[u], vcols] = (acc_ref[b, :, vcols] + dvs[u].astype(BF16).astype(F32)).astype(BF16)
    xt = jnp.concatenate([xt_ref[0], xt_ref[1]], axis=1)
    dw_scr[...] += nn(xt, dkv_ref[...]).reshape(dw_scr.shape)

    @pl.when(i == pl.num_programs(0) - 1)
    def _():
        deal(dw_scr, kept_ref, given_ref, meta[1 + 2 * pl.num_programs(0)])


def project_kernel(x_ref, w_ref, *rest):
    rest[-1][...] = nn(x_ref[...], w_ref[...]).astype(BF16)


def call(kernel, scalars, steps, in_specs, out_specs, out_shape, scratch, flops, touched, name, aliases={}):
    return pl.pallas_call(
        kernel,
        grid_spec=pltpu.PrefetchScalarGridSpec(
            num_scalar_prefetch=scalars, grid=(steps,), in_specs=in_specs, out_specs=out_specs, scratch_shapes=scratch
        ),
        out_shape=out_shape,
        input_output_aliases=aliases,
        compiler_params=pltpu.CompilerParams(dimension_semantics=("arbitrary",), vmem_limit_bytes=VMEM_LIMIT),
        cost_estimate=pl.CostEstimate(flops=flops, bytes_accessed=touched, transcendentals=0),
        name=name,
    )


def once(shape, at=0):
    return pl.BlockSpec(shape, lambda i, *s: (at,) + (0,) * (len(shape) - 1), pipeline_mode=pl.Buffered(1))


def body(node_feats, w_qkv, w_out, neighbours, tiles, partner, layer_cot):
    rows, width = node_feats.shape
    doms, groups = lax.axis_size("dom"), lax.axis_size("head")
    devices = doms * groups
    blocks = partner.shape[0]
    own = blocks // groups
    bs = tiles.shape[2]
    span = width // groups
    half = lax.axis_index("head")
    base = half * own

    near_ids = jnp.roll((neighbours - base) % blocks, -base, axis=0)
    mine = lax.dynamic_slice_in_dim(partner, base, own, 0)
    core = lax.axis_index("dom") % 2
    meta = jnp.concatenate([base[None].astype(jnp.int32), mine // own, core[None].astype(jnp.int32)])

    w_by = w_qkv.reshape(width, groups, 3, span).transpose(2, 0, 1, 3).reshape(3, width, width)
    w_all = jnp.concatenate([w_by[0] * jnp.asarray(0.125, BF16), w_by[1], w_by[2]], axis=1)

    def swap(x):
        return lax.ppermute(x, "head", [(0, 1), (1, 0)])

    def exchange(x):
        return lax.all_to_all(x, DEVICES, split_axis=0, concat_axis=0, tiled=True)

    def spread(x):
        return x.reshape(own, bs, width).transpose(1, 0, 2)

    def gathered(x):
        return jnp.dot(one_hot, x.reshape(-1, width), preferred_element_type=F32).astype(BF16).reshape(
            devices, own, width
        )

    digits = jnp.stack([mine // DIGIT, mine % DIGIT], axis=1).astype(BF16)
    digits = jnp.pad(digits, ((0, 0), (0, LANES - 2)))
    digits = jnp.broadcast_to(digits[None], (devices, own, LANES))
    first_hop = jnp.concatenate([spread(node_feats), digits], axis=2)
    rows_in = exchange(first_hop)
    peer_feats = swap(node_feats)
    cot = jnp.dot(layer_cot, w_out.T, preferred_element_type=F32).astype(BF16)
    cot_rows = spread(cot)
    cot_t = jnp.einsum("ck,brk->bcr", w_out, layer_cot.reshape(own, bs, width), preferred_element_type=F32).astype(BF16)

    hold = pl.BlockSpec(memory_space=pl.ANY)

    def project(feats, total, at, carried, name):
        return call(
            project_kernel, 0, 3,
            [
                once((rows, width)),
                pl.BlockSpec((width, width), lambda i: (0, i)),
            ]
            + [hold] * len(carried),
            [
                pl.BlockSpec((rows, width), lambda i: (at, i)),
            ],
            [jax.ShapeDtypeStruct((total * bs, 3 * width), BF16)],
            [], 2 * rows * width * 3 * width, 6 << 20, name, aliases={2: 0} if carried else {},
        )(feats, w_all, *carried)[0]

    own_part = project(node_feats, blocks, 0, (), "project_own")
    feats_t = node_feats.reshape(own, bs, width).transpose(0, 2, 1)
    out_t = layer_cot.reshape(own, bs, width).transpose(0, 2, 1)
    rows_in, cot_rows, own_part, peer_feats, cot_t, feats_t, out_t = lax.optimization_barrier(
        (rows_in, cot_rows, own_part, peer_feats, cot_t, feats_t, out_t)
    )

    weigh = jnp.pad(jnp.asarray([DIGIT, 1], F32), (0, LANES - 2))
    ids = jnp.sum(rows_in.reshape(-1, width + LANES)[:, width:].astype(F32) * weigh[None], axis=1, keepdims=True)
    one_hot = (ids == jnp.arange(ids.shape[0], dtype=jnp.int32)[None, :].astype(F32)).astype(BF16)
    second = jnp.concatenate([gathered(rows_in[:, :, :width]), cot_rows], axis=2)
    second = exchange(second)
    part_qkv = project(peer_feats, blocks, 1, (own_part,), "project_peer")
    part_blk = part_qkv.reshape(blocks, bs, 3 * width)
    pair_flops = 2 * bs * bs * width * 2
    step = lambda i, *s: (i, 0)
    row_step = lambda i, *s: (i, 0, 0)
    rows_spec = pl.BlockSpec((bs, width), step)
    tile_spec = pl.BlockSpec((1, NBR, bs, bs), lambda i, ids, meta: (meta[0] + i, 0, 0, 0))
    k_spec = pl.BlockSpec((blocks, bs, width), lambda i, *s: (0, 0, 1), pipeline_mode=pl.Buffered(1))
    v_spec = pl.BlockSpec((blocks, bs, width), lambda i, *s: (0, 0, 2), pipeline_mode=pl.Buffered(1))
    stats_spec = pl.BlockSpec((1, STATS, bs), row_step)
    turned_spec = pl.BlockSpec((1, width, bs), row_step)
    near_out, sums = call(
        near_kernel, 2, own,
        [rows_spec, tile_spec, k_spec, v_spec],
        [pl.BlockSpec((1, width, bs), row_step), pl.BlockSpec((1, 2 * H, bs), row_step)],
        [jax.ShapeDtypeStruct((own, width, bs), F32), jax.ShapeDtypeStruct((own, 2 * H, bs), F32)],
        [pltpu.VMEM((NBR, bs, 2 * bs), F32)],
        own * 16 * pair_flops, 10 << 20, "near_forward",
    )(near_ids, meta, part_qkv, tiles, part_blk, part_blk)
    second, near_out, sums, cot_out = lax.optimization_barrier((second, near_out, sums, cot))

    picked = gathered(second[:, :, width:])
    far_feats = second[:, :, :width].transpose(1, 0, 2).reshape(rows, width)
    picked, far_feats = lax.optimization_barrier((picked, far_feats))
    far_cot = exchange(picked)
    far_qkv = jnp.dot(far_feats, w_all, preferred_element_type=F32).astype(BF16)
    far_blk = far_qkv.reshape(own, bs, 3 * width)
    peer_cot = swap(cot_out)

    far_k_spec = pl.BlockSpec((1, bs, width), lambda i, *s: (i, 0, 1))
    far_v_spec = pl.BlockSpec((1, bs, width), lambda i, *s: (i, 0, 2))
    pair_rows = pl.BlockSpec((2 * bs, width), step)
    pair_turned = pl.BlockSpec((2, width, bs), row_step)
    pair_k = pl.BlockSpec((2, bs, width), lambda i, *s: (i, 0, 1))
    pair_v = pl.BlockSpec((2, bs, width), lambda i, *s: (i, 0, 2))
    att, stats = call(
        merge_kernel, 0, own // 2,
        [pair_rows, pair_turned, pair_k, pair_v, pair_turned, pl.BlockSpec((2, 2 * H, bs), row_step)],
        [pair_turned, pl.BlockSpec((2, STATS, bs), row_step)],
        [jax.ShapeDtypeStruct((own, width, bs), BF16), jax.ShapeDtypeStruct((own, STATS, bs), F32)],
        [], own * 4 * pair_flops, 6 << 20, "far_forward",
    )(part_qkv, cot_t, far_blk, far_blk, near_out, sums)
    peer_stats = swap(stats)
    pairs = width // LANES
    piece = (groups, doms // 2, width // doms, width)
    piece_spec = pl.BlockSpec(piece, lambda i, *s: (0, 0, 0, 0), pipeline_mode=pl.Buffered(1))
    piece_out = jax.ShapeDtypeStruct(piece, F32)
    dw_scratch = pltpu.VMEM((doms // 2, 2, width // doms, 2 * width), F32)
    dq, acc, kept, given, slots = call(
        own_kernel, 2, own,
        [rows_spec, rows_spec, tile_spec, stats_spec, k_spec, v_spec, far_k_spec, far_v_spec,
         turned_spec, turned_spec, turned_spec],
        [turned_spec, pl.BlockSpec((own, bs, 2 * width), lambda i, *s: (0, 0, 0)), piece_spec, piece_spec,
         pl.BlockSpec((1, STATS, bs), lambda i, ids, meta: (meta[1 + i], 0, 0))],
        [
            jax.ShapeDtypeStruct((own, width, bs), BF16),
            jax.ShapeDtypeStruct((own, bs, 2 * width), F32),
            piece_out,
            piece_out,
            jax.ShapeDtypeStruct((devices, STATS, bs), F32),
        ],
        [
            pltpu.VMEM((pairs, NBR * bs, 2 * bs), BF16),
            pltpu.VMEM((pairs, NBR * bs, 2 * bs), BF16),
            pltpu.VMEM((pairs, 2 * bs, LANES), BF16),
            pltpu.VMEM((pairs, 2 * bs, LANES), BF16),
            pltpu.VMEM((NBR, bs, 2 * bs), F32),
            dw_scratch,
        ],
        own * 24 * pair_flops, 30 << 20, "own_backward",
    )(near_ids, meta, part_qkv, cot, tiles, stats, part_blk, part_blk, far_blk, far_blk,
      feats_t, out_t, att)
    acc, peer_stats, peer_cot, far_cot, slots = lax.optimization_barrier((acc, peer_stats, peer_cot, far_cot, slots))
    far_slots = exchange(slots)
    far_cot = far_cot.transpose(1, 0, 2).reshape(rows, width)

    layer_out = jnp.einsum("bar,ac->brc", att, w_out, preferred_element_type=F32).astype(BF16).reshape(rows, width)

    def paired(kept, given):
        return (kept + lax.ppermute(given, "dom", [(d, d ^ 1) for d in range(doms)])).astype(BF16)

    early = paired(kept, given)

    (acc,) = call(
        peer_kernel, 2, own,
        [
            pl.BlockSpec((bs, width), lambda i, *s: (own + i, 0)),
            pl.BlockSpec((bs, width), step),
            pl.BlockSpec((1, STATS, bs), lambda i, *s: (i, 0, 0)),
            pl.BlockSpec((1, NBR, bs, bs), lambda i, ids, meta: (own - meta[0] + i, 0, 0, 0)),
            pl.BlockSpec((own, bs, width), lambda i, *s: (0, 0, 1), pipeline_mode=pl.Buffered(1)),
            pl.BlockSpec((own, bs, width), lambda i, *s: (0, 0, 2), pipeline_mode=pl.Buffered(1)),
            once((own, bs, 2 * width)),
        ],
        [pl.BlockSpec((own, bs, 2 * width), lambda i, *s: (0, 0, 0))],
        [jax.ShapeDtypeStruct((own, bs, 2 * width), F32)],
        [
            pltpu.VMEM((width // LANES, 2 * bs, LANES), BF16),
            pltpu.VMEM((width // LANES, 2 * bs, LANES), BF16),
        ],
        own * 16 * pair_flops, 20 << 20, "peer_queries",
    )(near_ids, meta, part_qkv, peer_cot, peer_stats, tiles, part_blk, part_blk, acc)

    dkv, kept, given = call(
        far_kernel, 1, own // 2,
        [
            pair_rows,
            pair_rows,
            pl.BlockSpec((1, STATS, bs), lambda i, meta: (meta[1 + 2 * i], 0, 0)),
            pl.BlockSpec((1, STATS, bs), lambda i, meta: (meta[2 + 2 * i], 0, 0)),
            pair_k,
            pair_v,
            pl.BlockSpec((2, bs, 2 * width), row_step),
            pair_turned,
        ],
        [pl.BlockSpec((2 * bs, 2 * width), step), piece_spec, piece_spec],
        [jax.ShapeDtypeStruct((rows, 2 * width), BF16), piece_out, piece_out],
        [dw_scratch], own * 8 * pair_flops, 10 << 20, "far_queries",
    )(meta, far_qkv, far_cot, far_slots, far_slots, part_blk, part_blk, acc, feats_t)

    split = jnp.concatenate([early, paired(kept, given)], axis=2).reshape(devices // 2, 2 * width // doms, width)
    same_core = [[d * groups + g for g in range(groups) for d in range(e, doms, 2)] for e in range(2)]
    moved = lax.all_to_all(split, DEVICES, split_axis=0, concat_axis=0, axis_index_groups=same_core, tiled=True)
    summed = jnp.sum(moved.astype(F32), axis=0)
    w_plain = w_by.transpose(1, 0, 2).reshape(width, 3 * width)
    feat_grad = (
        jnp.einsum("bcr,dc->brd", dq, w_plain[:, :width], preferred_element_type=F32).reshape(rows, width)
        + lax.dot_general(dkv, w_plain[:, width:], (((1,), (1,)), ((), ())), preferred_element_type=F32)
    ).astype(BF16)
    deep = width // doms
    dw_out = summed[:deep, :span].T
    dw_qkv = jnp.concatenate([summed[:deep, span:], summed[deep:]], axis=1)
    return (layer_out, feat_grad, dw_qkv, dw_out)


def solution(mesh):
    placed = (
        P(DEVICES, None),
        P(),
        P(),
        P("dom", None),
        P("dom", None, None, None),
        P("dom"),
        P(DEVICES, None),
    )
    return jax.shard_map(
        body,
        mesh=mesh,
        in_specs=placed,
        out_specs=(P(DEVICES, None), P(DEVICES, None), P("dom", "head"), P("head", "dom")),
        check_vma=False,
    )
```

```python
import jax
import jax.numpy as jnp
from jax import lax
from jax.experimental import pallas as pl
from jax.experimental.pallas import tpu as pltpu
from jax.sharding import PartitionSpec as P

H = 8
NBR = 4
DEVICES = ("dom", "head")
F32, BF16 = jnp.float32, jnp.bfloat16
NEG = -1e30
LANES = 128
STATS = 3 * H
DIGIT = 32
VMEM_LIMIT = 58 * 1024 * 1024


def nn(a, b):
    return jnp.dot(a, b, preferred_element_type=F32)


def nt(a, b):
    return lax.dot_general(a, b, (((1,), (1,)), ((), ())), preferred_element_type=F32)


def tn(a, b):
    return lax.dot_general(a, b, (((0,), (0,)), ((), ())), preferred_element_type=F32)


def two_heads(pair):
    lane = lax.broadcasted_iota(jnp.int32, pair.shape, 1)
    zero = jnp.zeros_like(pair)
    return jnp.concatenate(
        [jnp.where(lane < LANES // 2, pair, zero), jnp.where(lane >= LANES // 2, pair, zero)], axis=0
    )


def own_heads(both):
    half, rows = both.shape[0] // 2, both.shape[1] // 2
    return jnp.concatenate([both[:half, :rows], both[half:, rows:]], axis=0)


def bias_of(tile):
    bias = jnp.where(tile != 0, 0.0, NEG).astype(F32).T
    return jnp.concatenate([bias, bias], axis=1)


def split_stat(row):
    return row[:, : row.shape[1] // 2], row[:, row.shape[1] // 2 :]


def near_kernel(near_ids, meta, q_ref, tile_ref, k_ref, v_ref, out_ref, sums_ref, bias_scr):
    i = pl.program_id(0)
    for j in range(NBR):
        bias_scr[j] = bias_of(tile_ref[0, j])
    ids = [near_ids[i, j] for j in range(NBR)]
    pairs = q_ref.shape[1] // LANES

    def scores_of(c):
        cols = slice(c * LANES, (c + 1) * LANES)
        qz = two_heads(q_ref[:, cols])
        return jnp.concatenate([nt(k_ref[ids[j], :, cols], qz) + bias_scr[j] for j in range(NBR)], axis=0)

    ready = scores_of(0)
    for c in range(pairs):
        cols = slice(c * LANES, (c + 1) * LANES)
        scores, ready = ready, scores_of(c + 1) if c + 1 < pairs else None
        peak = jnp.max(scores, axis=0, keepdims=True)
        terms = jnp.exp(scores - peak)
        total = jnp.sum(terms, axis=0, keepdims=True)
        values = jnp.concatenate([v_ref[ids[j], :, cols] for j in range(NBR)], axis=0)
        out_ref[0, cols, :] = own_heads(tn(values, terms.astype(BF16)))
        store_rows(sums_ref, c, (peak, total))


def store_rows(ref, c, rows, b=0):
    for s, row in enumerate(rows):
        for e, part in enumerate(split_stat(row)):
            at = s * H + 2 * c + e
            ref[b, at : at + 1, :] = part


def merge_kernel(q_ref, cot_t_ref, fk_ref, fv_ref, out_ref, sums_ref, att_ref, stats_ref):
    mid = LANES // 2
    bs = fk_ref.shape[1]
    units = [(b, c) for b in range(fk_ref.shape[0]) for c in range(q_ref.shape[1] // LANES)]
    cols = [slice(c * LANES, (c + 1) * LANES) for _, c in units]
    scores = [
        nt(fk_ref[b, :, cols[u]], two_heads(q_ref[b * bs : (b + 1) * bs, cols[u]])) for u, (b, c) in enumerate(units)
    ]
    peaks, kepts, invs, lows = [], [], [], []
    for u, (b, c) in enumerate(units):
        near_peak, near_total = load_rows(sums_ref, c, 2, b)
        peak = jnp.maximum(near_peak, jnp.max(scores[u], axis=0, keepdims=True))
        terms = jnp.exp(scores[u] - peak)
        kept = jnp.exp(near_peak - peak)
        inv = 1.0 / (near_total * kept + jnp.sum(terms, axis=0, keepdims=True))
        lows.append((terms * inv).astype(BF16))
        peaks.append(peak)
        kepts.append(kept)
        invs.append(inv)
    far_outs = [own_heads(tn(fv_ref[b, :, cols[u]], lows[u])) for u, (b, c) in enumerate(units)]
    for u, (b, c) in enumerate(units):
        first, second = split_stat(kepts[u] * invs[u])
        near_out = out_ref[b, cols[u], :]
        near_out = jnp.concatenate([near_out[:mid] * first, near_out[mid:] * second], axis=0)
        att = (far_outs[u] + near_out).astype(BF16)
        att_ref[b, cols[u], :] = att
        prod = cot_t_ref[b, cols[u], :].astype(F32) * att.astype(F32)
        delta = jnp.concatenate(
            [jnp.sum(prod[:mid], axis=0, keepdims=True), jnp.sum(prod[mid:], axis=0, keepdims=True)], axis=1
        )
        store_rows(stats_ref, c, (peaks[u], invs[u], delta), b)


def deal(dw_scr, kept_ref, given_ref, core):
    groups, span = kept_ref.shape[0], kept_ref.shape[3] // 2
    for g in range(groups):
        for t in range(2):
            at = (t * groups + g) * span
            kept_ref[g, :, :, t * span : (t + 1) * span] = dw_scr[:, core, :, at : at + span]
            given_ref[g, :, :, t * span : (t + 1) * span] = dw_scr[:, 1 - core, :, at : at + span]


def own_kernel(near_ids, meta, q_ref, cot_ref, tile_ref, stats_ref, k_ref, v_ref, fk_ref, fv_ref,
               xt_ref, ct_ref, att_ref, dq_ref, acc_ref, kept_ref, given_ref, slot_ref, p_scr, ds_scr, qz_scr, cz_scr, bias_scr,
               dw_scr):
    i = pl.program_id(0)
    bs, width = q_ref.shape
    pairs = width // LANES
    own = acc_ref.shape[0]

    @pl.when(i == 0)
    def _():
        acc_ref[...] = jnp.zeros_like(acc_ref)
        dw_scr[...] = jnp.zeros_like(dw_scr)

    slot_ref[...] = stats_ref[...]
    for j in range(NBR):
        bias_scr[j] = bias_of(tile_ref[0, j])
    ids = [near_ids[i, j] for j in range(NBR)]

    def products(c):
        cols = slice(c * LANES, (c + 1) * LANES)
        qz = two_heads(q_ref[:, cols])
        cz = two_heads(cot_ref[:, cols])
        qz_scr[c] = qz
        cz_scr[c] = cz
        scores = [nt(k_ref[ids[j], :, cols], qz) + bias_scr[j] for j in range(NBR)] + [nt(fk_ref[0, :, cols], qz)]
        grads = [nt(v_ref[ids[j], :, cols], cz) for j in range(NBR)] + [nt(fv_ref[0, :, cols], cz)]
        return scores, grads

    ready = products(0)
    for c in range(pairs):
        cols = slice(c * LANES, (c + 1) * LANES)
        (scores, grads), ready = ready, products(c + 1) if c + 1 < pairs else None
        peak, inv, delta = load_rows(stats_ref, c, 3)
        parts = []
        for j in range(NBR + 1):
            rows = slice(j * bs, (j + 1) * bs)
            probs = jnp.exp(scores[j] - peak) * inv
            parts.append((probs * (grads[j] - delta)).astype(BF16))
            if j < NBR:
                p_scr[c, rows, :] = probs.astype(BF16)
                ds_scr[c, rows, :] = parts[j]
        keys = jnp.concatenate([k_ref[ids[j], :, cols] for j in range(NBR)] + [fk_ref[0, :, cols]], axis=0)
        dq_ref[0, cols, :] = (own_heads(tn(keys, jnp.concatenate(parts, axis=0))) * 0.125).astype(BF16)
    half = dw_scr.shape[:3] + (width,)
    dw_scr[:, :, :, :width] += nt(ct_ref[0], att_ref[0]).reshape(half)
    dw_scr[:, :, :, width:] += nt(xt_ref[0], dq_ref[0]).reshape(half)

    for j in range(NBR):

        @pl.when(ids[j] < own)
        def _(j=j):
            n = ids[j]
            for c in range(pairs):
                cols = slice(c * LANES, (c + 1) * LANES)
                vcols = slice(width + c * LANES, width + (c + 1) * LANES)
                rows = slice(j * bs, (j + 1) * bs)
                acc_ref[n, :, cols] += nn(ds_scr[c, rows, :], qz_scr[c])
                acc_ref[n, :, vcols] += nn(p_scr[c, rows, :], cz_scr[c])

    @pl.when(i == own - 1)
    def _():
        deal(dw_scr, kept_ref, given_ref, meta[1 + own])


def load_rows(ref, c, count, b=0):
    return [
        jnp.concatenate(
            [ref[b, s * H + 2 * c : s * H + 2 * c + 1, :], ref[b, s * H + 2 * c + 1 : s * H + 2 * c + 2, :]], axis=1
        )
        for s in range(count)
    ]


def key_terms(ks, vs, qzs, czs, biases, stats):
    scores = [nt(k, qz) for k, qz in zip(ks, qzs)]
    grads = [nt(v, cz) for v, cz in zip(vs, czs)]
    if biases is not None:
        scores = [s + bias for s, bias in zip(scores, biases)]
    probs = [jnp.exp(s - peak) * inv for s, (peak, inv, _) in zip(scores, stats)]
    ds = [(p * (g - delta)).astype(BF16) for p, g, (_, _, delta) in zip(probs, grads, stats)]
    return [nn(d, qz) for d, qz in zip(ds, qzs)], [nn(p.astype(BF16), cz) for p, cz in zip(probs, czs)]


def peer_kernel(near_ids, meta, q_ref, cot_ref, stats_ref, tile_ref, k_ref, v_ref, acc_in, acc_ref, qz_scr, cz_scr):
    i = pl.program_id(0)
    pairs = q_ref.shape[1] // LANES
    width = q_ref.shape[1]
    own = acc_ref.shape[0]

    @pl.when(i == 0)
    def _():
        acc_ref[...] = acc_in[...]

    for c in range(pairs):
        cols = slice(c * LANES, (c + 1) * LANES)
        qz_scr[c] = two_heads(q_ref[:, cols])
        cz_scr[c] = two_heads(cot_ref[:, cols])
    ids = [near_ids[own + i, j] for j in range(NBR)]
    taken = [jnp.where(n < own, 1, 0) for n in ids]
    before = [sum(taken[:j], 0) for j in range(NBR)]
    count = sum(taken)
    order = [sum(jnp.where((before[j] == k) & (ids[j] < own), j, 0) for j in range(NBR)) for k in range(NBR)]
    every = range(pairs)
    cols = [slice(c * LANES, (c + 1) * LANES) for c in every]
    for k in range(0, NBR, 2):

        @pl.when(count > k)
        def _(k=k):
            both = count > k + 1
            slots = (order[k], jnp.where(both, order[k + 1], order[k]))
            weights = (None, jnp.where(both, 1.0, 0.0).astype(F32))
            blocks = [near_ids[own + i, j] for j in slots]
            ks, vs, biases, stats = [], [], [], []
            for n, j, weight in zip(blocks, slots, weights):
                ks += [k_ref[n, :, cols[c]] for c in every]
                vs += [v_ref[n, :, cols[c]] for c in every]
                biases += [bias_of(tile_ref[0, j])] * pairs
                for c in every:
                    peak, inv, delta = load_rows(stats_ref, c, 3)
                    stats.append((peak, inv if weight is None else inv * weight, delta))
            dks, dvs = key_terms(
                ks, vs, [qz_scr[c] for c in every] * 2, [cz_scr[c] for c in every] * 2, biases, stats
            )
            for b, n in enumerate(blocks):
                for c in every:
                    acc_ref[n, :, cols[c]] += dks[b * pairs + c]
                    acc_ref[n, :, width + c * LANES : width + (c + 1) * LANES] += dvs[b * pairs + c]


def far_kernel(meta, q_ref, cot_ref, first_ref, second_ref, k_ref, v_ref, acc_ref, xt_ref, dkv_ref, kept_ref,
               given_ref, dw_scr):
    bs, width = k_ref.shape[1:]
    i = pl.program_id(0)

    @pl.when(i == 0)
    def _():
        dw_scr[...] = jnp.zeros_like(dw_scr)

    units = [(b, c) for b in range(2) for c in range(width // LANES)]
    cols = [slice(c * LANES, (c + 1) * LANES) for _, c in units]
    rows = [slice(b * bs, (b + 1) * bs) for b, _ in units]
    every = range(len(units))
    dks, dvs = key_terms(
        [k_ref[units[u][0], :, cols[u]] for u in every], [v_ref[units[u][0], :, cols[u]] for u in every],
        [two_heads(q_ref[rows[u], cols[u]]) for u in every], [two_heads(cot_ref[rows[u], cols[u]]) for u in every],
        None, [load_rows((first_ref, second_ref)[b], c, 3) for b, c in units],
    )
    for u, (b, c) in enumerate(units):
        vcols = slice(width + c * LANES, width + (c + 1) * LANES)
        dkv_ref[rows[u], cols[u]] = (acc_ref[b, :, cols[u]] + dks[u].astype(BF16).astype(F32)).astype(BF16)
        dkv_ref[rows[u], vcols] = (acc_ref[b, :, vcols] + dvs[u].astype(BF16).astype(F32)).astype(BF16)
    xt = jnp.concatenate([xt_ref[0], xt_ref[1]], axis=1)
    dw_scr[...] += nn(xt, dkv_ref[...]).reshape(dw_scr.shape)

    @pl.when(i == pl.num_programs(0) - 1)
    def _():
        deal(dw_scr, kept_ref, given_ref, meta[1 + 2 * pl.num_programs(0)])


def project_kernel(x_ref, w_ref, *rest):
    rest[-1][...] = nn(x_ref[...], w_ref[...]).astype(BF16)


def call(kernel, scalars, steps, in_specs, out_specs, out_shape, scratch, flops, touched, name, aliases={}):
    return pl.pallas_call(
        kernel,
        grid_spec=pltpu.PrefetchScalarGridSpec(
            num_scalar_prefetch=scalars, grid=(steps,), in_specs=in_specs, out_specs=out_specs, scratch_shapes=scratch
        ),
        out_shape=out_shape,
        input_output_aliases=aliases,
        compiler_params=pltpu.CompilerParams(dimension_semantics=("arbitrary",), vmem_limit_bytes=VMEM_LIMIT),
        cost_estimate=pl.CostEstimate(flops=flops, bytes_accessed=touched, transcendentals=0),
        name=name,
    )


def once(shape, at=0):
    return pl.BlockSpec(shape, lambda i, *s: (at,) + (0,) * (len(shape) - 1), pipeline_mode=pl.Buffered(1))


def body(node_feats, w_qkv, w_out, neighbours, tiles, partner, layer_cot):
    rows, width = node_feats.shape
    doms, groups = lax.axis_size("dom"), lax.axis_size("head")
    devices = doms * groups
    blocks = partner.shape[0]
    own = blocks // groups
    bs = tiles.shape[2]
    span = width // groups
    half = lax.axis_index("head")
    base = half * own

    near_ids = jnp.roll((neighbours - base) % blocks, -base, axis=0)
    mine = lax.dynamic_slice_in_dim(partner, base, own, 0)
    core = lax.axis_index("dom") % 2
    meta = jnp.concatenate([base[None].astype(jnp.int32), mine // own, core[None].astype(jnp.int32)])

    w_by = w_qkv.reshape(width, groups, 3, span).transpose(2, 0, 1, 3).reshape(3, width, width)
    w_all = jnp.concatenate([w_by[0] * jnp.asarray(0.125, BF16), w_by[1], w_by[2]], axis=1)

    def swap(x):
        return lax.ppermute(x, "head", [(0, 1), (1, 0)])

    def exchange(x):
        return lax.all_to_all(x, DEVICES, split_axis=0, concat_axis=0, tiled=True)

    def spread(x):
        return x.reshape(own, bs, width).transpose(1, 0, 2)

    def gathered(x):
        return jnp.dot(one_hot, x.reshape(-1, width), preferred_element_type=F32).astype(BF16).reshape(
            devices, own, width
        )

    digits = jnp.stack([mine // DIGIT, mine % DIGIT], axis=1).astype(BF16)
    digits = jnp.pad(digits, ((0, 0), (0, LANES - 2)))
    digits = jnp.broadcast_to(digits[None], (devices, own, LANES))
    first_hop = jnp.concatenate([spread(node_feats), digits], axis=2)
    rows_in = exchange(first_hop)
    peer_feats = swap(node_feats)
    cot = jnp.dot(layer_cot, w_out.T, preferred_element_type=F32).astype(BF16)
    cot_rows = spread(cot)
    cot_t = jnp.einsum("ck,brk->bcr", w_out, layer_cot.reshape(own, bs, width), preferred_element_type=F32).astype(BF16)

    hold = pl.BlockSpec(memory_space=pl.ANY)

    def project(feats, total, at, carried, name):
        return call(
            project_kernel, 0, 3,
            [
                once((rows, width)),
                pl.BlockSpec((width, width), lambda i: (0, i)),
            ]
            + [hold] * len(carried),
            [
                pl.BlockSpec((rows, width), lambda i: (at, i)),
            ],
            [jax.ShapeDtypeStruct((total * bs, 3 * width), BF16)],
            [], 2 * rows * width * 3 * width, 6 << 20, name, aliases={2: 0} if carried else {},
        )(feats, w_all, *carried)[0]

    own_part = project(node_feats, blocks, 0, (), "project_own")
    feats_t = node_feats.reshape(own, bs, width).transpose(0, 2, 1)
    out_t = layer_cot.reshape(own, bs, width).transpose(0, 2, 1)
    rows_in, cot_rows, own_part, peer_feats, cot_t, feats_t, out_t = lax.optimization_barrier(
        (rows_in, cot_rows, own_part, peer_feats, cot_t, feats_t, out_t)
    )

    weigh = jnp.pad(jnp.asarray([DIGIT, 1], F32), (0, LANES - 2))
    ids = jnp.sum(rows_in.reshape(-1, width + LANES)[:, width:].astype(F32) * weigh[None], axis=1, keepdims=True)
    one_hot = (ids == jnp.arange(ids.shape[0], dtype=jnp.int32)[None, :].astype(F32)).astype(BF16)
    second = jnp.concatenate([gathered(rows_in[:, :, :width]), cot_rows], axis=2)
    second = exchange(second)
    part_qkv = project(peer_feats, blocks, 1, (own_part,), "project_peer")
    part_blk = part_qkv.reshape(blocks, bs, 3 * width)
    pair_flops = 2 * bs * bs * width * 2
    step = lambda i, *s: (i, 0)
    row_step = lambda i, *s: (i, 0, 0)
    rows_spec = pl.BlockSpec((bs, width), step)
    tile_spec = pl.BlockSpec((1, NBR, bs, bs), lambda i, ids, meta: (meta[0] + i, 0, 0, 0))
    k_spec = pl.BlockSpec((blocks, bs, width), lambda i, *s: (0, 0, 1), pipeline_mode=pl.Buffered(1))
    v_spec = pl.BlockSpec((blocks, bs, width), lambda i, *s: (0, 0, 2), pipeline_mode=pl.Buffered(1))
    stats_spec = pl.BlockSpec((1, STATS, bs), row_step)
    turned_spec = pl.BlockSpec((1, width, bs), row_step)
    near_out, sums = call(
        near_kernel, 2, own,
        [rows_spec, tile_spec, k_spec, v_spec],
        [pl.BlockSpec((1, width, bs), row_step), pl.BlockSpec((1, 2 * H, bs), row_step)],
        [jax.ShapeDtypeStruct((own, width, bs), F32), jax.ShapeDtypeStruct((own, 2 * H, bs), F32)],
        [pltpu.VMEM((NBR, bs, 2 * bs), F32)],
        own * 16 * pair_flops, 10 << 20, "near_forward",
    )(near_ids, meta, part_qkv, tiles, part_blk, part_blk)
    second, near_out, sums, cot_out = lax.optimization_barrier((second, near_out, sums, cot))

    picked = gathered(second[:, :, width:])
    far_feats = second[:, :, :width].transpose(1, 0, 2).reshape(rows, width)
    far_cot = exchange(picked)
    far_qkv = jnp.dot(far_feats, w_all, preferred_element_type=F32).astype(BF16)
    far_blk = far_qkv.reshape(own, bs, 3 * width)
    peer_cot = swap(cot_out)

    far_k_spec = pl.BlockSpec((1, bs, width), lambda i, *s: (i, 0, 1))
    far_v_spec = pl.BlockSpec((1, bs, width), lambda i, *s: (i, 0, 2))
    pair_rows = pl.BlockSpec((2 * bs, width), step)
    pair_turned = pl.BlockSpec((2, width, bs), row_step)
    pair_k = pl.BlockSpec((2, bs, width), lambda i, *s: (i, 0, 1))
    pair_v = pl.BlockSpec((2, bs, width), lambda i, *s: (i, 0, 2))
    att, stats = call(
        merge_kernel, 0, own // 2,
        [pair_rows, pair_turned, pair_k, pair_v, pair_turned, pl.BlockSpec((2, 2 * H, bs), row_step)],
        [pair_turned, pl.BlockSpec((2, STATS, bs), row_step)],
        [jax.ShapeDtypeStruct((own, width, bs), BF16), jax.ShapeDtypeStruct((own, STATS, bs), F32)],
        [], own * 4 * pair_flops, 6 << 20, "far_forward",
    )(part_qkv, cot_t, far_blk, far_blk, near_out, sums)
    peer_stats = swap(stats)
    pairs = width // LANES
    piece = (groups, doms // 2, width // doms, width)
    piece_spec = pl.BlockSpec(piece, lambda i, *s: (0, 0, 0, 0), pipeline_mode=pl.Buffered(1))
    piece_out = jax.ShapeDtypeStruct(piece, F32)
    dw_scratch = pltpu.VMEM((doms // 2, 2, width // doms, 2 * width), F32)
    dq, acc, kept, given, slots = call(
        own_kernel, 2, own,
        [rows_spec, rows_spec, tile_spec, stats_spec, k_spec, v_spec, far_k_spec, far_v_spec,
         turned_spec, turned_spec, turned_spec],
        [turned_spec, pl.BlockSpec((own, bs, 2 * width), lambda i, *s: (0, 0, 0)), piece_spec, piece_spec,
         pl.BlockSpec((1, STATS, bs), lambda i, ids, meta: (meta[1 + i], 0, 0))],
        [
            jax.ShapeDtypeStruct((own, width, bs), BF16),
            jax.ShapeDtypeStruct((own, bs, 2 * width), F32),
            piece_out,
            piece_out,
            jax.ShapeDtypeStruct((devices, STATS, bs), F32),
        ],
        [
            pltpu.VMEM((pairs, NBR * bs, 2 * bs), BF16),
            pltpu.VMEM((pairs, NBR * bs, 2 * bs), BF16),
            pltpu.VMEM((pairs, 2 * bs, LANES), BF16),
            pltpu.VMEM((pairs, 2 * bs, LANES), BF16),
            pltpu.VMEM((NBR, bs, 2 * bs), F32),
            dw_scratch,
        ],
        own * 24 * pair_flops, 30 << 20, "own_backward",
    )(near_ids, meta, part_qkv, cot, tiles, stats, part_blk, part_blk, far_blk, far_blk,
      feats_t, out_t, att)
    acc, peer_stats, peer_cot, far_cot, slots = lax.optimization_barrier((acc, peer_stats, peer_cot, far_cot, slots))
    far_slots = exchange(slots)
    far_cot = far_cot.transpose(1, 0, 2).reshape(rows, width)

    layer_out = jnp.einsum("bar,ac->brc", att, w_out, preferred_element_type=F32).astype(BF16).reshape(rows, width)

    def paired(kept, given):
        return (kept + lax.ppermute(given, "dom", [(d, d ^ 1) for d in range(doms)])).astype(BF16)

    early = paired(kept, given)

    (acc,) = call(
        peer_kernel, 2, own,
        [
            pl.BlockSpec((bs, width), lambda i, *s: (own + i, 0)),
            pl.BlockSpec((bs, width), step),
            pl.BlockSpec((1, STATS, bs), lambda i, *s: (i, 0, 0)),
            pl.BlockSpec((1, NBR, bs, bs), lambda i, ids, meta: (own - meta[0] + i, 0, 0, 0)),
            pl.BlockSpec((own, bs, width), lambda i, *s: (0, 0, 1), pipeline_mode=pl.Buffered(1)),
            pl.BlockSpec((own, bs, width), lambda i, *s: (0, 0, 2), pipeline_mode=pl.Buffered(1)),
            once((own, bs, 2 * width)),
        ],
        [pl.BlockSpec((own, bs, 2 * width), lambda i, *s: (0, 0, 0))],
        [jax.ShapeDtypeStruct((own, bs, 2 * width), F32)],
        [
            pltpu.VMEM((width // LANES, 2 * bs, LANES), BF16),
            pltpu.VMEM((width // LANES, 2 * bs, LANES), BF16),
        ],
        own * 16 * pair_flops, 20 << 20, "peer_queries",
    )(near_ids, meta, part_qkv, peer_cot, peer_stats, tiles, part_blk, part_blk, acc)

    dkv, kept, given = call(
        far_kernel, 1, own // 2,
        [
            pair_rows,
            pair_rows,
            pl.BlockSpec((1, STATS, bs), lambda i, meta: (meta[1 + 2 * i], 0, 0)),
            pl.BlockSpec((1, STATS, bs), lambda i, meta: (meta[2 + 2 * i], 0, 0)),
            pair_k,
            pair_v,
            pl.BlockSpec((2, bs, 2 * width), row_step),
            pair_turned,
        ],
        [pl.BlockSpec((2 * bs, 2 * width), step), piece_spec, piece_spec],
        [jax.ShapeDtypeStruct((rows, 2 * width), BF16), piece_out, piece_out],
        [dw_scratch], own * 8 * pair_flops, 10 << 20, "far_queries",
    )(meta, far_qkv, far_cot, far_slots, far_slots, part_blk, part_blk, acc, feats_t)

    split = jnp.concatenate([early, paired(kept, given)], axis=2).reshape(devices // 2, 2 * width // doms, width)
    same_core = [[d * groups + g for g in range(groups) for d in range(e, doms, 2)] for e in range(2)]
    moved = lax.all_to_all(split, DEVICES, split_axis=0, concat_axis=0, axis_index_groups=same_core, tiled=True)
    summed = jnp.sum(moved.astype(F32), axis=0)
    w_plain = w_by.transpose(1, 0, 2).reshape(width, 3 * width)
    feat_grad = (
        jnp.einsum("bcr,dc->brd", dq, w_plain[:, :width], preferred_element_type=F32).reshape(rows, width)
        + lax.dot_general(dkv, w_plain[:, width:], (((1,), (1,)), ((), ())), preferred_element_type=F32)
    ).astype(BF16)
    deep = width // doms
    dw_out = summed[:deep, :span].T
    dw_qkv = jnp.concatenate([summed[:deep, span:], summed[deep:]], axis=1)
    return (layer_out, feat_grad, dw_qkv, dw_out)


def solution(mesh):
    placed = (
        P(DEVICES, None),
        P(),
        P(),
        P("dom", None),
        P("dom", None, None, None),
        P("dom"),
        P(DEVICES, None),
    )
    return jax.shard_map(
        body,
        mesh=mesh,
        in_specs=placed,
        out_specs=(P(DEVICES, None), P(DEVICES, None), P("dom", "head"), P("head", "dom")),
        check_vma=False,
    )
```
